32 devices in a mesh: ens: 2 (over y), tile: 4 (over z), lev: 2 (over x), sub: 2 (over core).
Axes of the slice: x: 2, y: 2, z: 4, core: 2. Of those that a mesh axis runs over, the one named last changes fastest.
Arguments:
- marine_layered_warmth: float32 [8, 128, 512], P(('ens', 'lev'), 'sub', 'tile'), parts along dimension 0, may hold values from -6 to 6
- bottom_sky_warmth: float32 [8192], P(('ens', 'tile', 'lev', 'sub')), parts along dimension 0, may hold values from -6 to 6
- bottom_breeze_magnitude: float32 [8192], P(('ens', 'tile', 'lev', 'sub')), parts along dimension 0, may hold values from 0.3 to 3
- depth_shares: float32 [4], P('lev'), may hold values from 0.05 to 0.25
- piece_sky_box: int32 [16, 8, 256], P(('tile', 'lev', 'sub')), may hold values from 0 to 255, as said below
- sky_share_fraction: float32 [16, 8, 256], P(('tile', 'lev', 'sub')), as said below
- piece_marine_box: int32 [16, 8, 256], P(('tile', 'lev', 'sub')), may hold values from 0 to 8191, as said below
- marine_share_fraction: float32 [16, 8, 256], P(('tile', 'lev', 'sub')), as said below
- marine_indicator: int32 [128, 512], P('sub', 'tile'), may hold values from 0 to 1
- marine_result_adjoint: float32 [8, 128, 512], P(('ens', 'lev'), 'sub', 'tile'), parts along dimension 0, may hold values from -6 to 6
- energy_transport_adjoint: float32 [8192], P(('ens', 'tile', 'lev', 'sub')), parts along dimension 0, may hold values from -6 to 6
Outputs:
- state_gradient: float32 [8, 128, 512], P(('ens', 'lev'), 'sub', 'tile'), parts along dimension 0
- air_gradient: float32 [8192], P(('ens', 'tile', 'lev', 'sub')), parts along dimension 0
- wind_gradient: float32 [8192], P(('ens', 'tile', 'lev', 'sub')), parts along dimension 0
The draws below stay inside these ranges and needn't reach their ends.
There are 2 independent parts, one for each index of `ens`. The reference program is written for one: setup_inputs(seed, part) draws one part's arguments, and reference() takes and returns one part's arrays. A program takes and returns all parts, laid end to end along the dimension named above; an argument that names none is the same for every part. Nothing has to cross between parts.
Inputs may be any that keep to these rules, and one draw needn't show every extreme that they name: `piece_sky_box`: indices into the device's own 256 atmosphere cells. `piece_marine_box`: slot j of block r = a * 2 + s on ocean device e = (o * 2 + l) * 2 + u is the same exchange-grid cell as slot j of block o * 2 + u on atmosphere device (a * 2 + l) * 2 + s; entries index the device's own 64 x 128 ocean cells row by row. `sky_share_fraction`: in each block the live slots come first, the rest carry weight zero; a live slot also has weight zero where its ocean cell is land; the blocks to 2 ocean owners of every lev index are full from every source. `marine_share_fraction`: zero at the same slots as sky_share_fraction.
All inputs are finite; a program needn't handle non-finite values.
Results may differ from the reference program's by a relative error of at most 0.0003.
Values sent between devices are 32-bit elements; how exact they have to be, the bound alone decides.
No kernel may reach another device: no remote copies, remote signals or barrier semaphores. Data moves between devices by JAX's collectives and lax.ppermute only.
A program may use at most 64 MiB of HBM per device.

```python
import math
import jax
import jax.numpy as jnp
from jax import lax

DEPTH_LAYERS = 4
OY = 64
OX = 128
GRID_HEIGHT = 128
GRID_WIDTH = 512
ACELL = 256
GROUP = 16
SKY_BOXES = 4096
OWNERS = 8
SLOTS = 256
BULK_ITERS = 3
STEPS = 3
STORMS = 2
N_TILE = 4
N_LEV = 2
N_SUB = 2


def xgrid_lists(key):
    key_land, key_storm, key_count, key_air, key_ocean = jax.random.split(key, 5)
    land_grid = (jax.random.randint(key_land, (OY * N_SUB, OX * N_TILE), 0, 5) != 0).astype(jnp.int32)
    shuffled = jax.random.permutation(key_storm, OWNERS)
    storm_flag = jnp.zeros((OWNERS,), jnp.int32).at[shuffled[:STORMS]].set(1)
    counts = jax.random.randint(key_count, (GROUP, OWNERS), SLOTS // 4, 3 * SLOTS // 4 + 1)
    counts = jnp.where(storm_flag[None, :] == 1, SLOTS, counts)
    live_slot = (jnp.arange(SLOTS, dtype=jnp.int32)[None, None, :] < counts[:, :, None]).astype(jnp.int32)
    air_index = jax.random.randint(key_air, (GROUP, OWNERS, SLOTS), 0, ACELL)
    ocean_local = jax.random.randint(key_ocean, (GROUP, OWNERS, SLOTS), 0, OY * OX)
    owner_ids = jnp.arange(OWNERS, dtype=jnp.int32)
    cell_row = (owner_ids % N_SUB)[None, :, None] * OY + ocean_local // OX
    cell_column = (owner_ids // N_SUB)[None, :, None] * OX + ocean_local % OX
    wet_slot = land_grid[cell_row, cell_column]
    return (land_grid, live_slot * wet_slot, air_index, ocean_local)


def ocean_layout(blocks):
    spread = blocks.reshape(N_TILE, N_LEV, N_SUB, N_TILE, N_SUB, SLOTS)
    return spread.transpose(3, 1, 4, 0, 2, 5).reshape(GROUP, OWNERS, SLOTS)


def spread_factor(key, low, high):
    return jnp.exp(jax.random.uniform(key, (GROUP, OWNERS, SLOTS), jnp.float32, low, high))


def draw_piece_sky_box(key, part):
    shared = xgrid_lists(key)
    return shared[2]


def draw_piece_marine_box(key, part):
    shared = xgrid_lists(key)
    return ocean_layout(shared[3])


def draw_marine_indicator(key, part):
    shared = xgrid_lists(key)
    return shared[0]


def draw_sky_share_fraction(key, part):
    shared = xgrid_lists(key)
    key = jax.random.fold_in(key, 4)
    factor = spread_factor(key, -1.0, 1.0)
    usable = shared[1].astype(jnp.float32)
    return factor * usable * (ACELL / (OWNERS * SLOTS))


def draw_marine_share_fraction(key, part):
    shared = xgrid_lists(key)
    key = jax.random.fold_in(key, 5)
    factor = spread_factor(key, -1.0, 1.0)
    usable = shared[1].astype(jnp.float32)
    return ocean_layout(factor * usable * (OY * OX / (N_LEV * OWNERS * SLOTS)))


def level_of(rng, dims, shards, least, high):
    loudness, own = 1.0, jax.random.fold_in(rng, 6)
    for axis_at, shards_of in shards:
        draws = jnp.exp(jax.random.uniform(jax.random.fold_in(own, axis_at), (shards_of,), jnp.float32, least / len(shards), high / len(shards)))
        loudness = loudness * jnp.repeat(draws, dims[axis_at] // shards_of).reshape([-1 if axis == axis_at else 1 for axis in range(len(dims))])
    return loudness


def normal_values(own_key, shape, width, bound, pieces=(), held_as=jnp.bfloat16):
    entries = width * jax.random.normal(own_key, shape, jnp.float32)
    if pieces:
        entries = entries * level_of(own_key, shape, pieces, -0.22, 0.18)
    return jnp.clip(entries, -bound, bound).astype(held_as)


def setup_inputs(seed: int = 0, part: int = 0) -> dict:
    key_list = jax.random.split(jax.random.key(seed), 12)
    part_keys = jax.random.split(jax.random.fold_in(key_list[11], part), 12)
    marine_layered_warmth = normal_values(part_keys[0], (DEPTH_LAYERS, GRID_HEIGHT, GRID_WIDTH), 1.0, 6.0, ((0, 2), (1, 2), (2, 4)), jnp.float32)
    bottom_sky_warmth = normal_values(part_keys[1], (SKY_BOXES,), 1.0, 6.0, ((0, 16),), jnp.float32)
    bottom_breeze_magnitude = jnp.clip(jnp.exp(math.log(3.0) - 2.3025851 * jax.random.uniform(part_keys[2], (SKY_BOXES,), jnp.float32) ** level_of(part_keys[2], (SKY_BOXES,), ((0, 16),), -0.2, 0.2)), 0.3, 3.0)
    depth_shares = jnp.clip(jnp.exp(math.log(0.25) - 1.609438 * jax.random.uniform(key_list[3], (DEPTH_LAYERS,), jnp.float32) ** level_of(key_list[3], (DEPTH_LAYERS,), ((0, 2),), -0.2, 0.2)), 0.05, 0.25)
    piece_sky_box = draw_piece_sky_box(jax.random.fold_in(key_list[11], 71), part)
    sky_share_fraction = draw_sky_share_fraction(jax.random.fold_in(key_list[11], 71), part)
    piece_marine_box = draw_piece_marine_box(jax.random.fold_in(key_list[11], 71), part)
    marine_share_fraction = draw_marine_share_fraction(jax.random.fold_in(key_list[11], 71), part)
    marine_indicator = draw_marine_indicator(jax.random.fold_in(key_list[11], 71), part)
    marine_result_adjoint = normal_values(part_keys[9], (DEPTH_LAYERS, GRID_HEIGHT, GRID_WIDTH), 1.0, 6.0, ((0, 2), (1, 2), (2, 4)), jnp.float32)
    energy_transport_adjoint = normal_values(part_keys[10], (SKY_BOXES,), 1.0, 6.0, ((0, 16),), jnp.float32)
    return {"marine_layered_warmth": marine_layered_warmth, "bottom_sky_warmth": bottom_sky_warmth, "bottom_breeze_magnitude": bottom_breeze_magnitude, "depth_shares": depth_shares, "piece_sky_box": piece_sky_box, "sky_share_fraction": sky_share_fraction, "piece_marine_box": piece_marine_box, "marine_share_fraction": marine_share_fraction, "marine_indicator": marine_indicator, "marine_result_adjoint": marine_result_adjoint, "energy_transport_adjoint": energy_transport_adjoint}


MIXING = 0.2
TRANSFER = 1.0
STABILITY = 0.5

def diffuse(tracer_pad, wet_pad):
    center = tracer_pad[:, 1:-1, 1:-1]
    wet_center = wet_pad[1:-1, 1:-1]
    wet_above = wet_pad[:-2, 1:-1]
    wet_below = wet_pad[2:, 1:-1]
    wet_left = wet_pad[1:-1, :-2]
    wet_right = wet_pad[1:-1, 2:]
    beside = wet_above * tracer_pad[:, :-2, 1:-1] + wet_below * tracer_pad[:, 2:, 1:-1] + wet_left * tracer_pad[:, 1:-1, :-2] + wet_right * tracer_pad[:, 1:-1, 2:]
    wet_count = wet_above + wet_below + wet_left + wet_right
    return wet_center * (center + MIXING * (beside - wet_count * center))

def bulk_flux(warmth_gap):
    transfer_rate = jnp.full_like(warmth_gap, TRANSFER)
    for sweep_index in range(BULK_ITERS):
        transfer_rate = TRANSFER * (1.0 + STABILITY * jnp.tanh(transfer_rate * warmth_gap))
    return transfer_rate * warmth_gap

def atmos_layout(blocks):
    spread = blocks.reshape(N_TILE, N_LEV, N_SUB, N_TILE, N_SUB, SLOTS)
    return spread.transpose(3, 1, 4, 0, 2, 5).reshape(GROUP, OWNERS, SLOTS)

def reference(marine_layered_warmth, bottom_sky_warmth, bottom_breeze_magnitude, depth_shares, piece_sky_box, sky_share_fraction, piece_marine_box, marine_share_fraction, marine_indicator, marine_result_adjoint, energy_transport_adjoint):
    wet = marine_indicator.astype(jnp.float32)
    device_base = (jnp.arange(GROUP, dtype=jnp.int32) * ACELL)[:, None, None]
    sky_vector_linear = device_base + piece_sky_box
    ocean_local = atmos_layout(piece_marine_box)
    weight_ocean = atmos_layout(marine_share_fraction)
    owner_ids = jnp.arange(OWNERS, dtype=jnp.int32)
    grid_row = (owner_ids % N_SUB)[None, :, None] * OY + ocean_local // OX
    grid_column = (owner_ids // N_SUB)[None, :, None] * OX + ocean_local % OX
    ocean_flat = grid_row * (OX * N_TILE) + grid_column

    def primal_interface_pass(marine_profile_values, boundary_warmth, interface_breeze):
        surface = jnp.einsum('j,jck->ck', depth_shares, marine_profile_values, precision=lax.Precision.HIGHEST)
        shared_interface_pieces = surface.reshape(-1)[ocean_flat]
        warmth_gap = interface_breeze[sky_vector_linear] * (shared_interface_pieces - boundary_warmth[sky_vector_linear])
        interface_energy_transport = bulk_flux(warmth_gap)
        heat = jax.ops.segment_sum((weight_ocean * interface_energy_transport).reshape(-1), ocean_flat.reshape(-1), num_segments=surface.size).reshape(surface.shape)
        sky_energy_transport = jax.ops.segment_sum((sky_share_fraction * interface_energy_transport).reshape(-1), sky_vector_linear.reshape(-1), num_segments=boundary_warmth.shape[0])
        heated = wet * (marine_profile_values + depth_shares[:, None, None] * heat[None])
        for sweep_index in range(STEPS):
            heated = diffuse(jnp.pad(heated, ((0, 0), (1, 1), (1, 1))), jnp.pad(wet, 1))
        return (heated, sky_energy_transport)
    interface_results, reverse_routing_map = jax.vjp(primal_interface_pass, marine_layered_warmth, bottom_sky_warmth, bottom_breeze_magnitude)
    state_gradient, air_gradient, wind_gradient = reverse_routing_map((marine_result_adjoint, energy_transport_adjoint))
    return (state_gradient, air_gradient, wind_gradient)
```

```python
import functools

import jax
import jax.numpy as jnp
from jax import lax
from jax.experimental import pallas as pl
from jax.experimental.pallas import tpu as pltpu
from jax.sharding import PartitionSpec as P

BULK_ITERS = 3
STEPS = 3
HALO = STEPS
MIXING = 0.2
TRANSFER = 1.0
STABILITY = 0.5
F32 = jnp.float32
BF16 = jnp.bfloat16
VMEM = pl.BlockSpec(memory_space=pltpu.VMEM)
SMEM = pl.BlockSpec(memory_space=pltpu.SMEM)


def halves(x):
    high = x.astype(BF16)
    low = (x - high.astype(F32)).astype(BF16)
    return high, low


def call(kernel, out_shapes, operands, specs=None, scratch=()):
    return pl.pallas_call(
        kernel,
        out_shape=[jax.ShapeDtypeStruct(s, F32) for s in out_shapes],
        in_specs=specs or [VMEM] * len(operands),
        out_specs=[VMEM] * len(out_shapes),
        scratch_shapes=list(scratch),
        compiler_params=pltpu.CompilerParams(vmem_limit_bytes=24 * 1024 * 1024),
    )(*operands)


def pack_kernel(n, warm, cot, sea, sky, breeze, energy, shares, sky_index, sky_weight, msg, part):
    sub = lax.axis_index("sub")
    rows, cols = sea.shape
    levels = warm.shape[0]
    wet = sea[...].astype(F32)
    surface = shares[0] * warm[0]
    heat = shares[0] * cot[0]
    for z in range(1, levels):
        surface += shares[z] * warm[z]
        heat += shares[z] * cot[z]
    part[0:rows, :] = surface
    part[rows : 2 * rows, :] = heat
    msg[...] = jnp.zeros_like(msg)
    msg[0 : 2 * n, :] = sky_index[...].astype(F32)
    msg[2 * n : 4 * n, :] = sky_weight[...]
    for i, ref in enumerate((sky, breeze, energy)):
        msg[4 * n + i : 4 * n + i + 1, :] = ref[...]

    def outer(x):
        return jnp.where(sub == 0, x[rows - HALO : rows], x[0:HALO])

    fields = [cot[z] for z in range(levels)] + [wet, heat]
    base = 4 * n + 8
    for i, x in enumerate(fields):
        top, left = base + HALO * (i // 2), cols * (i % 2)
        msg[top : top + HALO, left : left + cols] = outer(x)


def halo_rows(n, msg, i, cols):
    top, left = 4 * n + 8 + HALO * (i // 2), cols * (i % 2)
    return msg[top : top + HALO, left : left + cols]


def air_rows(n, msg, other, step, sub, tile):
    row = 2 * lax.rem(tile + step, n) + sub
    first = sub == 0

    def both(index):
        own, far = msg[pl.ds(index, 1), :], other[pl.ds(index, 1), :]
        return [jnp.where(first, own, far), jnp.where(first, far, own)]

    out = both(row) + both(2 * n + row)
    for i in range(3):
        out += both(4 * n + i)
    return out


def send_kernel(n, far_steps, msg, other, part, lev_out, *far_out):
    sub, tile = lax.axis_index("sub"), lax.axis_index("tile")
    full, cols = part.shape
    lev_out[0:full, :] = part[...]
    lev_out[full : full + 8, :] = jnp.zeros((8, cols), F32)
    lev_out[full : full + HALO, :] = halo_rows(n, other, 3, cols)
    for step, out in zip(far_steps, far_out):
        out[...] = jnp.zeros_like(out)
        for i, row in enumerate(air_rows(n, msg, other, step, sub, tile)):
            out[i : i + 1, :] = row


def edge_place(shape):
    lane = lax.broadcasted_iota(jnp.int32, shape, 1)
    return lax.rem(lane + HALO, shape[1])


def edge_kernel(n, count, *refs):
    lev_parts = refs[:count]
    cot, sea, msg, other, surface_out, ext, right_out, left_out = refs[count:]
    sub, tile = lax.axis_index("sub"), lax.axis_index("tile")
    rows, cols = sea.shape
    levels = cot.shape[0]
    high = rows + 8
    surface_out[...] = sum(ref[0:rows, :] for ref in lev_parts)
    ext[...] = jnp.zeros_like(ext)
    centers = [cot[z] for z in range(levels)] + [sea[...].astype(F32)]
    centers.append(sum(ref[rows : 2 * rows, :] for ref in lev_parts))
    strips = [halo_rows(n, other, i, cols) for i in range(levels + 1)]
    strips.append(sum(ref[2 * rows : 2 * rows + HALO, :] for ref in lev_parts))
    place = edge_place((high, cols))
    edges = jnp.zeros((high, cols), F32)
    for i, (center, strip) in enumerate(zip(centers, strips)):
        base = high * i
        ext[base : base + rows, :] = center
        ext[base + rows : base + rows + HALO, :] = jnp.where(sub == 0, strip, 0.0)
        ext[base + high - HALO : base + high, :] = jnp.where(sub == 0, 0.0, strip)
        field = ext[base : base + high, :]
        moved = pltpu.roll(field, 2 * HALO * i, 1) if i else field
        edges = jnp.where(place // (2 * HALO) == i, moved, edges)
    for step, out in ((1, right_out), (n - 1, left_out)):
        out[0:high, :] = edges
        out[high : out.shape[0], :] = jnp.zeros((out.shape[0] - high, cols), F32)
        for i, row in enumerate(air_rows(n, msg, other, step, sub, tile)):
            out[high + i : high + i + 1, :] = row[:, :cols]
            out[high + 10 + i : high + 11 + i, :] = row[:, cols:]


def diffused(n, ext, from_right, from_left, fields, wet_field, high, tile):
    cols = ext.shape[1]
    place = edge_place((high, cols))
    right = jnp.where(tile < n - 1, from_right[0:high, :], 0.0)
    left = jnp.where(tile > 0, from_left[0:high, :], 0.0)
    edges = jnp.where(lax.rem(place, 2 * HALO) >= HALO, right, left)

    def wide(i):
        moved = pltpu.roll(edges, cols - 2 * HALO * i, 1) if i else edges
        return jnp.concatenate(
            [ext[high * i : high * (i + 1), :], jnp.where(place < 2 * HALO, moved, 0.0)], axis=1
        )

    def around(x):
        return (
            pltpu.roll(x, 1, 0)
            + pltpu.roll(x, high - 1, 0)
            + pltpu.roll(x, 1, 1)
            + pltpu.roll(x, 2 * cols - 1, 1)
        )

    wet = wide(wet_field)
    keep = wet * (1.0 - MIXING * around(wet))
    mix = MIXING * wet
    out = []
    for i in fields:
        v = wet * wide(i)
        for sweep_index in range(STEPS):
            v = keep * v + mix * around(v)
        out.append(v[: high - 8, :cols])
    return wet[: high - 8, :cols], out


def bulk_adjoint(warmth_gap, flux_sens):
    transfer_rate = jnp.full_like(warmth_gap, TRANSFER)
    rates = [transfer_rate]
    slopes = []
    for sweep_index in range(BULK_ITERS):
        bent = jnp.tanh(transfer_rate * warmth_gap)
        slopes.append(TRANSFER * STABILITY * (1.0 - bent * bent))
        transfer_rate = TRANSFER * (1.0 + STABILITY * bent)
        rates.append(transfer_rate)
    contrast_sens = transfer_rate * flux_sens
    rate_sens = warmth_gap * flux_sens
    for sweep_index in reversed(range(BULK_ITERS)):
        inner_sens = rate_sens * slopes[sweep_index]
        contrast_sens = contrast_sens + inner_sens * rates[sweep_index]
        rate_sens = inner_sens * warmth_gap
    return contrast_sens


def onehot(index, count):
    cells = lax.broadcasted_iota(jnp.int32, (count, index.shape[1]), 0)
    return jnp.where(cells == index, 1.0, 0.0).astype(BF16)


def dot(a, b, ca, cb):
    return lax.dot_general(a, b, (((ca,), (cb,)), ((), ())), preferred_element_type=F32)


def slot_kernel(n, far_steps, *refs):
    surface, ext, msg, other, marine, weight, from_right, from_left = refs[:8]
    far_in = dict(zip(far_steps, refs[8 : 8 + len(far_steps)]))
    slots_out = refs[8 + len(far_steps)]
    returns = refs[9 + len(far_steps) : 9 + len(far_steps) + n]
    picks = refs[9 + len(far_steps) + n]
    sub, tile = lax.axis_index("sub"), lax.axis_index("tile")
    rows, cols = surface.shape
    high = rows + 8
    fields = ext.shape[0] // high
    wet, (heat,) = diffused(n, ext, from_right, from_left, [fields - 1], fields - 2, high, tile)
    heat = wet * heat
    table = jnp.concatenate([surface[...], heat], axis=1)
    table = jnp.concatenate(halves(table), axis=0)

    def air_in(step):
        if step == 0:
            return air_rows(n, msg, other, 0, sub, tile)
        if step in far_in:
            return [far_in[step][i : i + 1, :] for i in range(10)]
        ref = from_right if step == 1 else from_left
        return [
            jnp.concatenate(
                [ref[high + i : high + i + 1, :], ref[high + 10 + i : high + 11 + i, :]], axis=1
            )
            for i in range(10)
        ]

    owners = []
    tables = []
    for step in range(n):
        source = lax.rem(tile + step, n)
        air = air_in(step)
        for band in range(2):
            at = 2 * step + band
            cell = marine[pl.ds(2 * source + band, 1), :]
            row, col = cell // cols, lax.rem(cell, cols)
            row_hot = onehot(row, rows)
            spread = dot(table, jnp.concatenate([row_hot, row_hot], axis=0), 0, 0)
            col_mask = lax.broadcasted_iota(jnp.int32, (cols, cell.shape[1]), 0) == col
            for i in range(2):
                piece = jnp.where(col_mask, spread[cols * i : cols * (i + 1)], 0.0)
                picks[i, at : at + 1, :] = jnp.sum(piece, axis=0, keepdims=True)
            sky_hot = onehot(air[band].astype(jnp.int32), air[band].shape[1])
            values = jnp.concatenate([air[4 + band], air[6 + band], air[8 + band]], axis=0)
            found = dot(jnp.concatenate(halves(values), axis=0), sky_hot, 1, 0)
            for i in range(3):
                picks[2 + i, at : at + 1, :] = found[i : i + 1] + found[3 + i : 4 + i]
            picks[5, at : at + 1, :] = air[2 + band]
            picks[6, at : at + 1, :] = weight[pl.ds(2 * source + band, 1), :]
            owners.append((row_hot, col_mask))
            tables.append(sky_hot)

    difference = picks[0] - picks[2]
    wind = picks[3]
    flux_sens = picks[6] * picks[1] + picks[5] * picks[4]
    contrast_sens = bulk_adjoint(wind * difference, flux_sens)
    surface_sens = contrast_sens * wind
    wind_sens = contrast_sens * difference
    total = jnp.zeros((rows, 2 * cols), F32)
    for step in range(n):
        for band in range(2):
            at = 2 * step + band
            row_hot, col_mask = owners[at]
            ocean = surface_sens[at : at + 1]
            spread = jnp.concatenate(
                [jnp.where(col_mask, x.astype(F32), 0.0).astype(BF16) for x in halves(ocean)], axis=0
            )
            total += dot(row_hot, spread, 1, 1)
            values = jnp.concatenate([ocean, wind_sens[at : at + 1]], axis=0)
            sums = dot(jnp.concatenate(halves(values), axis=0), tables[at], 1, 1)
            returns[step][2 * band : 2 * band + 2, :] = sums[0:2] + sums[2:4]
        returns[step][4:8, :] = jnp.zeros((4, returns[step].shape[1]), F32)
    slots_out[...] = total[:, :cols] + total[:, cols:]


def adjoint_kernel(n, ext, from_right, from_left, out):
    tile = lax.axis_index("tile")
    levels = out.shape[0]
    high = out.shape[1] + 8
    wet, adjoint = diffused(
        n, ext, from_right, from_left, list(range(levels)), levels, high, tile
    )
    for z in range(levels):
        out[z] = wet * adjoint[z]


def final_kernel(count, *refs):
    slots = refs[:count]
    adjoint, shares, sums, other, state_out, air_out, wind_out = refs[count:]
    sub = lax.axis_index("sub")
    gradient = sum(ref[...] for ref in slots)
    for z in range(adjoint.shape[0]):
        state_out[z] = adjoint[z] + shares[z] * gradient
    both = sums[...] + other[...]
    own = jnp.where(sub == 0, both[0:2], both[2:4])
    air_out[...] = -own[0:1]
    wind_out[...] = own[1:2]


def shifted(x, axis, step):
    count = lax.axis_size(axis)
    return lax.ppermute(x, axis, [(i, (i + step) % count) for i in range(count)])


def lev_parts(x):
    if lax.axis_size("lev") == 2:
        return [x, shifted(x, "lev", 1)]
    return [lax.psum(x, "lev")]


def per_device(
    marine_layered_warmth,
    bottom_sky_warmth,
    bottom_breeze_magnitude,
    depth_shares,
    piece_sky_box,
    sky_share_fraction,
    piece_marine_box,
    marine_share_fraction,
    marine_indicator,
    marine_result_adjoint,
    energy_transport_adjoint,
):
    n = lax.axis_size("tile")
    levels, rows, cols = marine_layered_warmth.shape
    cells = bottom_sky_warmth.shape[0]
    air = [
        x.reshape(1, cells)
        for x in (bottom_sky_warmth, bottom_breeze_magnitude, energy_transport_adjoint)
    ]
    high = rows + 8
    far_steps = list(range(2, n - 1))
    msg, part = call(
        functools.partial(pack_kernel, n),
        [(4 * n + 16, cells), (2 * rows, cols)],
        [marine_layered_warmth, marine_result_adjoint, marine_indicator, *air, depth_shares]
        + [piece_sky_box[0], sky_share_fraction[0]],
        [VMEM] * 6 + [SMEM] + [VMEM] * 2,
    )
    other = shifted(msg, "sub", 1)
    lev_msg, *far_out = call(
        functools.partial(send_kernel, n, far_steps),
        [(2 * rows + 8, cols)] + [(16, cells)] * len(far_steps),
        [msg, other, part],
    )
    lev_in = lev_parts(lev_msg)
    far_in = [shifted(x, "tile", step) for step, x in zip(far_steps, far_out)]
    far_in = far_in[::-1]
    surface, ext, right_out, left_out = call(
        functools.partial(edge_kernel, n, len(lev_in)),
        [(rows, cols), ((levels + 2) * high, cols)] + [(high + 24, cols)] * 2,
        [*lev_in, marine_result_adjoint, marine_indicator, msg, other],
    )
    from_left = shifted(right_out, "tile", 1)
    from_right = shifted(left_out, "tile", n - 1)
    slots, *returns = call(
        functools.partial(slot_kernel, n, far_steps),
        [(rows, cols)] + [(8, cells)] * n,
        [surface, ext, msg, other, piece_marine_box[0], marine_share_fraction[0]]
        + [from_right, from_left, *far_in],
        scratch=[pltpu.VMEM((7, 2 * n, cells), F32)],
    )
    back = [shifted(returns[step], "tile", step) for step in range(1, n)]
    slot_parts = lev_parts(slots)
    (adjoint,) = call(
        functools.partial(adjoint_kernel, n),
        [(levels, rows, cols)],
        [ext, from_right, from_left],
    )
    sums = returns[0]
    for x in back:
        sums = sums + x
    sums_far = shifted(sums, "sub", 1)
    state, air_gradient, wind_gradient = call(
        functools.partial(final_kernel, len(slot_parts)),
        [(levels, rows, cols), (1, cells), (1, cells)],
        [*slot_parts, adjoint, depth_shares, sums, sums_far],
        [VMEM] * (len(slot_parts) + 1) + [SMEM] + [VMEM] * 2,
    )
    return (state, air_gradient.reshape(cells), wind_gradient.reshape(cells))


def solution(mesh):
    return jax.shard_map(
        per_device,
        mesh=mesh,
        in_specs=(
            P(("ens", "lev"), "sub", "tile"),
            P(("ens", "tile", "lev", "sub")),
            P(("ens", "tile", "lev", "sub")),
            P("lev"),
            P(("tile", "lev", "sub"), None, None),
            P(("tile", "lev", "sub"), None, None),
            P(("tile", "lev", "sub"), None, None),
            P(("tile", "lev", "sub"), None, None),
            P("sub", "tile"),
            P(("ens", "lev"), "sub", "tile"),
            P(("ens", "tile", "lev", "sub")),
        ),
        out_specs=(
            P(("ens", "lev"), "sub", "tile"),
            P(("ens", "tile", "lev", "sub")),
            P(("ens", "tile", "lev", "sub")),
        ),
        check_vma=False,
    )
```

```python
import functools

import jax
import jax.numpy as jnp
from jax import lax
from jax.experimental import pallas as pl
from jax.experimental.pallas import tpu as pltpu
from jax.sharding import PartitionSpec as P

BULK_ITERS = 3
STEPS = 3
HALO = STEPS
MIXING = 0.2
TRANSFER = 1.0
STABILITY = 0.5
F32 = jnp.float32
BF16 = jnp.bfloat16
VMEM = pl.BlockSpec(memory_space=pltpu.VMEM)
HBM = pl.BlockSpec(memory_space=pltpu.HBM)


def call(kernel, outs, operands, specs=None, out_specs=None, scratch=(), aliases=None):
    outs = [jax.ShapeDtypeStruct(x, F32) if isinstance(x, tuple) else x for x in outs]
    return pl.pallas_call(
        kernel,
        out_shape=outs,
        in_specs=specs or [VMEM] * len(operands),
        out_specs=out_specs or [VMEM] * len(outs),
        scratch_shapes=list(scratch),
        input_output_aliases=aliases or {},
        compiler_params=pltpu.CompilerParams(vmem_limit_bytes=24 * 1024 * 1024),
    )(*operands)


def halves(x):
    high = x.astype(BF16)
    low = (x - high.astype(F32)).astype(BF16)
    return high, low


def pack_kernel(n, *refs):
    warm, cot, sea, shares, sky, breeze, energy, sky_index, sky_weight = refs[:9]
    msg, ext, surface, share_rows = refs[9:13]
    warm_in, sea_in, shares_in, sky_in, breeze_in, energy_in, index_in, weight_in, sems = refs[13:]
    rows, cols = sea.shape
    levels = warm.shape[0]
    high = rows + 8
    pairs = [(cot.at[z], ext.at[pl.ds(high * z, rows)]) for z in range(levels)]
    pairs += [(sea, sea_in), (sky_index, index_in), (sky_weight, weight_in)]
    pairs += [(sky, sky_in), (breeze, breeze_in), (energy, energy_in)]
    pairs += [(shares, shares_in), (warm, warm_in)]
    copies = [pltpu.make_async_copy(a, b, sems.at[i]) for i, (a, b) in enumerate(pairs)]
    for copy in copies:
        copy.start()
    sub = lax.axis_index("sub")
    msg[...] = jnp.zeros_like(msg)
    for z in range(levels + 1):
        ext[high * z + rows : high * (z + 1), :] = jnp.zeros((8, cols), F32)
    for copy in copies:
        copy.wait()
    ext[high * levels : high * levels + rows, :] = sea_in[...].astype(F32)
    msg[0 : 2 * n, :] = index_in[...].astype(F32)
    msg[2 * n : 4 * n, :] = weight_in[...]
    for i, ref in enumerate((sky_in, breeze_in, energy_in)):
        msg[4 * n + i : 4 * n + i + 1, :] = ref[...]
    base = 4 * n + 8
    for i in range(levels + 1):
        at, top, left = high * i, base + HALO * (i // 2), cols * (i % 2)
        outer = jnp.where(sub == 0, ext[at + rows - HALO : at + rows], ext[at : at + HALO])
        msg[top : top + HALO, left : left + cols] = outer
    surface[...] = sum(shares_in[z] * warm_in[z] for z in range(levels))
    for z in range(levels):
        share_rows[z : z + 1, :] = jnp.full((1, cols), shares_in[z], F32)


def halo_rows(n, msg, i, cols):
    top, left = 4 * n + 8 + HALO * (i // 2), cols * (i % 2)
    return msg[top : top + HALO, left : left + cols]


def both_bands(msg, other, index, sub):
    own, far = msg[pl.ds(index, 1), :], other[pl.ds(index, 1), :]
    return [jnp.where(sub == 0, own, far), jnp.where(sub == 0, far, own)]


def air_rows(n, msg, other, target, band, sub):
    row = 2 * target + band
    places = [row, 2 * n + row] + [4 * n + i for i in range(3)]
    return [x for place in places for x in both_bands(msg, other, place, sub)]


def edge_place(shape):
    lane = lax.broadcasted_iota(jnp.int32, shape, 1)
    return lax.rem(lane + HALO, shape[1])


def send_kernel(n, fields, edge_steps, swap_steps, msg, other, ext_in, ext, *outs):
    sub, tile = lax.axis_index("sub"), lax.axis_index("tile")
    cols = ext.shape[1]
    high = ext.shape[0] // fields
    rows = high - 8
    place = edge_place((high, cols))
    edges = jnp.zeros((high, cols), F32)
    for i in range(fields):
        base = high * i
        strip = halo_rows(n, other, i, cols)
        ext[base : base + rows, :] = ext_in[base : base + rows, :]
        ext[base + rows : base + high, :] = jnp.zeros((8, cols), F32)
        ext[base + rows : base + rows + HALO, :] = jnp.where(sub == 0, strip, 0.0)
        ext[base + high - HALO : base + high, :] = jnp.where(sub == 0, 0.0, strip)
        field = ext[base : base + high, :]
        moved = pltpu.roll(field, 2 * HALO * i, 1) if i else field
        edges = jnp.where(place // (2 * HALO) == i, moved, edges)
    edge_outs, swap_outs = outs[: len(edge_steps)], outs[len(edge_steps) :]
    for step, out in zip(edge_steps, edge_outs):
        out[0:high, :] = edges
        if step:
            for i, row in enumerate(air_rows(n, msg, other, tile ^ step, sub, sub)):
                out[high + i : high + i + 1, :] = row[:, :cols]
                out[high + 10 + i : high + 11 + i, :] = row[:, cols:]
            out[high + 20 : high + 24, :] = jnp.zeros((4, cols), F32)
    for step, out in zip(swap_steps, swap_outs):
        for i, row in enumerate(air_rows(n, msg, other, tile ^ step, 1 - sub, sub)):
            out[i : i + 1, :] = row
        out[10:16, :] = jnp.zeros((6, out.shape[1]), F32)


def diffuse_kernel(n, levels, ext, near_in, edge_in, surface, share_rows, adjoint_out, lev_out):
    tile = lax.axis_index("tile")
    rows, cols = surface.shape
    high = rows + 8
    place = edge_place((high, cols))
    near, beyond = near_in[0:high, :], edge_in[0:high, :]
    even = tile % 2 == 0
    right = jnp.where(tile < n - 1, jnp.where(even, near, beyond), 0.0)
    left = jnp.where(tile > 0, jnp.where(even, beyond, near), 0.0)
    edges = jnp.where(lax.rem(place, 2 * HALO) >= HALO, right, left)

    def wide(i):
        moved = pltpu.roll(edges, cols - 2 * HALO * i, 1) if i else edges
        return jnp.concatenate(
            [ext[high * i : high * (i + 1), :], jnp.where(place < 2 * HALO, moved, 0.0)], axis=1
        )

    def around(x):
        return (
            pltpu.roll(x, 1, 0)
            + pltpu.roll(x, high - 1, 0)
            + pltpu.roll(x, 1, 1)
            + pltpu.roll(x, 2 * cols - 1, 1)
        )

    wet = wide(levels)
    keep = wet * (1.0 - MIXING * around(wet))
    mix = MIXING * wet
    own_wet = wet[:rows, :cols]
    heat = jnp.zeros((rows, cols), F32)
    for z in range(levels):
        v = wet * wide(z)
        for sweep_index in range(STEPS):
            v = keep * v + mix * around(v)
        adjoint = own_wet * v[:rows, :cols]
        adjoint_out[z] = adjoint
        heat += share_rows[z : z + 1, :] * adjoint
    lev_out[0:rows, :] = surface[...]
    lev_out[rows : 2 * rows, :] = own_wet * heat


def bulk_adjoint(warmth_gap, flux_sens):
    transfer_rate = jnp.full_like(warmth_gap, TRANSFER)
    rates = [transfer_rate]
    slopes = []
    for sweep_index in range(BULK_ITERS):
        bent = jnp.tanh(transfer_rate * warmth_gap)
        slopes.append(TRANSFER * STABILITY * (1.0 - bent * bent))
        transfer_rate = TRANSFER * (1.0 + STABILITY * bent)
        rates.append(transfer_rate)
    contrast_sens = transfer_rate * flux_sens
    rate_sens = warmth_gap * flux_sens
    for sweep_index in reversed(range(BULK_ITERS)):
        inner_sens = rate_sens * slopes[sweep_index]
        contrast_sens = contrast_sens + inner_sens * rates[sweep_index]
        rate_sens = inner_sens * warmth_gap
    return contrast_sens


def onehot(index, count):
    cells = lax.broadcasted_iota(jnp.int32, (count, index.shape[1]), 0)
    return jnp.where(cells == index, 1.0, 0.0).astype(BF16)


def dot(a, b, ca, cb):
    return lax.dot_general(a, b, (((ca,), (cb,)), ((), ())), preferred_element_type=F32)


def air_kernel(n, edge_steps, swap_steps, high, msg, other, *refs):
    sub, tile = lax.axis_index("sub"), lax.axis_index("tile")
    edge_in = dict(zip(edge_steps, refs))
    swap_in = dict(zip(swap_steps, refs[len(edge_steps) :]))
    picks, tables = refs[-2:]
    for step in range(n):
        if step == 0:
            air = air_rows(n, msg, other, tile, sub, sub)
        elif step in swap_in:
            air = [swap_in[step][i : i + 1, :] for i in range(10)]
        else:
            ref = edge_in[step]
            air = [
                jnp.concatenate(
                    [ref[high + i : high + i + 1, :], ref[high + 10 + i : high + 11 + i, :]], axis=1
                )
                for i in range(10)
            ]
        for band in range(2):
            at = 2 * step + band
            hot = onehot(air[band].astype(jnp.int32), air[band].shape[1])
            tables[at] = hot
            values = jnp.concatenate([air[4 + band], air[6 + band], air[8 + band]], axis=0)
            found = dot(jnp.concatenate(halves(values), axis=0), hot, 1, 0)
            found = found[0:3] + found[3:6]
            picks[0, at : at + 1, :] = found[0:1]
            picks[1, at : at + 1, :] = found[1:2]
            picks[2, at : at + 1, :] = air[2 + band] * found[2:3]


def slot_kernel(n, count, *refs):
    lev_parts = refs[:count]
    picks, tables, marine, weight, slots_out = refs[count : count + 5]
    returns, held = refs[count + 5 : count + 5 + n], refs[count + 5 + n]
    tile = lax.axis_index("tile")
    rows, cols = slots_out.shape
    table = jnp.concatenate(
        [sum(ref[rows * i : rows * (i + 1), :] for ref in lev_parts) for i in range(2)], axis=1
    )
    table = jnp.concatenate(halves(table), axis=0)
    owners = []
    for step in range(n):
        for band in range(2):
            at, place = 2 * step + band, 2 * (tile ^ step) + band
            cell = marine[pl.ds(place, 1), :]
            row, col = cell // cols, lax.rem(cell, cols)
            row_hot = onehot(row, rows)
            spread = dot(table, jnp.concatenate([row_hot, row_hot], axis=0), 0, 0)
            col_mask = lax.broadcasted_iota(jnp.int32, (cols, cell.shape[1]), 0) == col
            for i in range(2):
                piece = jnp.where(col_mask, spread[cols * i : cols * (i + 1)], 0.0)
                held[i, at : at + 1, :] = jnp.sum(piece, axis=0, keepdims=True)
            held[2, at : at + 1, :] = weight[pl.ds(place, 1), :]
            owners.append((row_hot, col_mask))

    difference = held[0] - picks[0]
    wind = picks[1]
    flux_sens = held[2] * held[1] + picks[2]
    contrast_sens = bulk_adjoint(wind * difference, flux_sens)
    surface_sens = contrast_sens * wind
    wind_sens = contrast_sens * difference
    total = jnp.zeros((rows, 2 * cols), F32)
    for step in range(n):
        for band in range(2):
            at = 2 * step + band
            row_hot, col_mask = owners[at]
            ocean = surface_sens[at : at + 1]
            spread = jnp.concatenate(
                [jnp.where(col_mask, x.astype(F32), 0.0).astype(BF16) for x in halves(ocean)], axis=0
            )
            total += dot(row_hot, spread, 1, 1)
            values = jnp.concatenate([ocean, wind_sens[at : at + 1]], axis=0)
            sums = dot(jnp.concatenate(halves(values), axis=0), tables[at], 1, 1)
            returns[step][2 * band : 2 * band + 2, :] = sums[0:2] + sums[2:4]
        returns[step][4:8, :] = jnp.zeros((4, returns[step].shape[1]), F32)
    slots_out[...] = total[:, :cols] + total[:, cols:]


def final_kernel(count, *refs):
    slots = refs[:count]
    adjoint, share_rows, sums, other, state_out, air_out, wind_out, state, air, wind, sems = refs[count:]
    sub = lax.axis_index("sub")
    gradient = sum(ref[...] for ref in slots)
    for z in range(adjoint.shape[0]):
        state[z] = adjoint[z] + share_rows[z : z + 1, :] * gradient
    copies = [pltpu.make_async_copy(state, state_out, sems.at[0])]
    copies[0].start()
    both = sums[...] + other[...]
    own = jnp.where(sub == 0, both[0:2], both[2:4])
    air[...] = -own[0:1]
    wind[...] = own[1:2]
    for i, (a, b) in enumerate(((air, air_out), (wind, wind_out))):
        copies.append(pltpu.make_async_copy(a, b, sems.at[1 + i]))
        copies[-1].start()
    for copy in copies:
        copy.wait()


def traded(x, step, swap=0):
    n, bands = lax.axis_size("tile"), lax.axis_size("sub")
    pairs = [
        (t * bands + s, (t ^ step) * bands + (s ^ swap)) for t in range(n) for s in range(bands)
    ]
    return lax.ppermute(x, ("tile", "sub"), pairs)


def lev_parts(x):
    if lax.axis_size("lev") == 2:
        return [x, lax.ppermute(x, "lev", [(0, 1), (1, 0)])]
    return [lax.psum(x, "lev")]


def per_device(
    marine_layered_warmth,
    bottom_sky_warmth,
    bottom_breeze_magnitude,
    depth_shares,
    piece_sky_box,
    sky_share_fraction,
    piece_marine_box,
    marine_share_fraction,
    marine_indicator,
    marine_result_adjoint,
    energy_transport_adjoint,
):
    n = lax.axis_size("tile")
    levels, rows, cols = marine_layered_warmth.shape
    cells = bottom_sky_warmth.shape[0]
    high = rows + 8
    if n == 4:
        edge_steps = [1, 3]
    else:
        edge_steps = [1, 0]
    swap_steps = [step for step in range(1, n) if step not in edge_steps]

    raw = [marine_layered_warmth, marine_result_adjoint, marine_indicator, depth_shares]
    raw += [
        x.reshape(1, cells)
        for x in (bottom_sky_warmth, bottom_breeze_magnitude, energy_transport_adjoint)
    ]
    raw += [piece_sky_box[0], sky_share_fraction[0]]
    raw = [pltpu.with_memory_space_constraint(x, pltpu.HBM) for x in raw]
    held = [pltpu.VMEM(x.shape, x.dtype) for x in [raw[0], raw[2]]]
    held += [pltpu.SMEM(depth_shares.shape, F32)]
    held += [pltpu.VMEM(x.shape, x.dtype) for x in raw[4:]]
    msg, ext, surface, share_rows = call(
        functools.partial(pack_kernel, n),
        [(4 * n + 16, cells), ((levels + 1) * high, cols), (rows, cols), (8, cols)],
        raw,
        [HBM] * len(raw),
        scratch=held + [pltpu.SemaphoreType.DMA((8 + levels,))],
    )
    other = traded(msg, 0, 1)
    ext, *sent = call(
        functools.partial(send_kernel, n, levels + 1, edge_steps, swap_steps),
        [ext.shape]
        + [(high + 24 if step else high, cols) for step in edge_steps]
        + [(16, cells)] * len(swap_steps),
        [msg, other, ext],
    )
    near_in = traded(sent[0], 1)
    if n == 4:
        edge_in = traded(sent[1], 3)
    else:
        pairs = [(i, (i + 1) % n) for i in range(1, n, 2)]
        edge_in = lax.ppermute(sent[1], "tile", pairs + [(b, a) for a, b in pairs])
    swapped = [traded(x, step, 1) for step, x in zip(swap_steps, sent[2:])]
    adjoint, lev_msg = call(
        functools.partial(diffuse_kernel, n, levels),
        [(levels, rows, cols), (2 * rows, cols)],
        [ext, near_in, edge_in, surface, share_rows],
    )
    lev_in = lev_parts(lev_msg)
    picks, tables = call(
        functools.partial(air_kernel, n, edge_steps, swap_steps, high),
        [(3, 2 * n, cells), jax.ShapeDtypeStruct((2 * n, cells, cells), BF16)],
        [msg, other, near_in, edge_in, *swapped],
    )
    slots, *returns = call(
        functools.partial(slot_kernel, n, len(lev_in)),
        [(rows, cols)] + [(8, cells)] * n,
        [*lev_in, picks, tables, piece_marine_box[0], marine_share_fraction[0]],
        scratch=[pltpu.VMEM((3, 2 * n, cells), F32)],
    )
    back = [traded(returns[step], step, 1) for step in range(1, n)]
    slot_parts = lev_parts(slots)
    sums = returns[0]
    for x in back:
        sums = sums + x
    sums_far = traded(sums, 0, 1)
    results = [(levels, rows, cols), (1, cells), (1, cells)]
    state, air_gradient, wind_gradient = call(
        functools.partial(final_kernel, len(slot_parts)),
        results,
        [*slot_parts, adjoint, share_rows, sums, sums_far],
        out_specs=[HBM] * 3,
        scratch=[pltpu.VMEM(x, F32) for x in results] + [pltpu.SemaphoreType.DMA((3,))],
    )
    return (state, air_gradient.reshape(cells), wind_gradient.reshape(cells))


def solution(mesh):
    return jax.shard_map(
        per_device,
        mesh=mesh,
        in_specs=(
            P(("ens", "lev"), "sub", "tile"),
            P(("ens", "tile", "lev", "sub")),
            P(("ens", "tile", "lev", "sub")),
            P("lev"),
            P(("tile", "lev", "sub"), None, None),
            P(("tile", "lev", "sub"), None, None),
            P(("tile", "lev", "sub"), None, None),
            P(("tile", "lev", "sub"), None, None),
            P("sub", "tile"),
            P(("ens", "lev"), "sub", "tile"),
            P(("ens", "tile", "lev", "sub")),
        ),
        out_specs=(
            P(("ens", "lev"), "sub", "tile"),
            P(("ens", "tile", "lev", "sub")),
            P(("ens", "tile", "lev", "sub")),
        ),
        check_vma=False,
    )
```

```python
import functools

import jax
import jax.numpy as jnp
from jax import lax
from jax.experimental import pallas as pl
from jax.experimental.pallas import tpu as pltpu
from jax.sharding import PartitionSpec as P

BULK_ITERS = 3
STEPS = 3
HALO = STEPS
MIXING = 0.2
TRANSFER = 1.0
STABILITY = 0.5
F32 = jnp.float32
BF16 = jnp.bfloat16
VMEM = pl.BlockSpec(memory_space=pltpu.VMEM)
HBM = pl.BlockSpec(memory_space=pltpu.HBM)


def call(kernel, outs, operands, specs=None, out_specs=None, scratch=(), aliases=None):
    outs = [jax.ShapeDtypeStruct(x, F32) if isinstance(x, tuple) else x for x in outs]
    return pl.pallas_call(
        kernel,
        out_shape=outs,
        in_specs=specs or [VMEM] * len(operands),
        out_specs=out_specs or [VMEM] * len(outs),
        scratch_shapes=list(scratch),
        input_output_aliases=aliases or {},
        compiler_params=pltpu.CompilerParams(vmem_limit_bytes=24 * 1024 * 1024),
    )(*operands)


def halves(x):
    high = x.astype(BF16)
    low = (x - high.astype(F32)).astype(BF16)
    return high, low


def pack_kernel(n, *refs):
    warm, cot, sea, shares, sky, breeze, energy, sky_index, sky_weight, marine, marine_weight = refs[:11]
    msg, ext, surface, share_rows, marine_out, marine_weight_out = refs[11:17]
    warm_in, sea_in, shares_in, sky_in, breeze_in, energy_in, index_in, weight_in, sems = refs[17:]
    rows, cols = sea.shape
    levels = warm.shape[0]
    high = rows + 8
    pairs = [(cot.at[z], ext.at[pl.ds(high * z, rows)]) for z in range(levels)]
    pairs += [(sea, sea_in), (sky_index, index_in), (sky_weight, weight_in)]
    pairs += [(sky, sky_in), (breeze, breeze_in), (energy, energy_in)]
    pairs += [(shares, shares_in), (warm, warm_in)]
    pairs += [(marine, marine_out), (marine_weight, marine_weight_out)]
    copies = [pltpu.make_async_copy(a, b, sems.at[i]) for i, (a, b) in enumerate(pairs)]
    for copy in copies:
        copy.start()
    sub = lax.axis_index("sub")
    msg[...] = jnp.zeros_like(msg)
    for z in range(levels + 1):
        ext[high * z + rows : high * (z + 1), :] = jnp.zeros((8, cols), F32)
    for copy in copies:
        copy.wait()
    ext[high * levels : high * levels + rows, :] = sea_in[...].astype(F32)
    msg[0 : 2 * n, :] = index_in[...].astype(F32)
    msg[2 * n : 4 * n, :] = weight_in[...]
    for i, ref in enumerate((sky_in, breeze_in, energy_in)):
        msg[4 * n + i : 4 * n + i + 1, :] = ref[...]
    base = 4 * n + 8
    for i in range(levels + 1):
        at, top, left = high * i, base + HALO * (i // 2), cols * (i % 2)
        outer = jnp.where(sub == 0, ext[at + rows - HALO : at + rows], ext[at : at + HALO])
        msg[top : top + HALO, left : left + cols] = outer
    surface[...] = sum(shares_in[z] * warm_in[z] for z in range(levels))
    for z in range(levels):
        share_rows[z : z + 1, :] = jnp.full((1, cols), shares_in[z], F32)


def halo_rows(n, msg, i, cols):
    top, left = 4 * n + 8 + HALO * (i // 2), cols * (i % 2)
    return msg[top : top + HALO, left : left + cols]


def both_bands(msg, other, index, sub):
    own, far = msg[pl.ds(index, 1), :], other[pl.ds(index, 1), :]
    return [jnp.where(sub == 0, own, far), jnp.where(sub == 0, far, own)]


def table_rows(n, msg, other, target, band, sub):
    row = 2 * target + band
    return both_bands(msg, other, row, sub) + both_bands(msg, other, 2 * n + row, sub)


def value_rows(n, msg, other, sub):
    return [x for i in range(3) for x in both_bands(msg, other, 4 * n + i, sub)]


def write_pairs(out, at, rows):
    cols = out.shape[1]
    for i, row in enumerate(rows):
        out[at + i : at + i + 1, :] = row[:, :cols]
        out[at + len(rows) + i : at + len(rows) + i + 1, :] = row[:, cols:]


def read_pairs(ref, at, count):
    return [
        jnp.concatenate([ref[at + i : at + i + 1, :], ref[at + count + i : at + count + i + 1, :]], axis=1)
        for i in range(count)
    ]


def edge_place(shape):
    lane = lax.broadcasted_iota(jnp.int32, shape, 1)
    return lax.rem(lane + HALO, shape[1])


def send_kernel(n, fields, msg, other, ext_in, ext, edge_out, near_out):
    sub, tile = lax.axis_index("sub"), lax.axis_index("tile")
    cols = ext.shape[1]
    high = ext.shape[0] // fields
    rows = high - 8
    place = edge_place((high, cols))
    edges = jnp.zeros((high, cols), F32)
    for i in range(fields):
        base = high * i
        strip = halo_rows(n, other, i, cols)
        ext[base : base + rows, :] = ext_in[base : base + rows, :]
        ext[base + rows : base + high, :] = jnp.zeros((8, cols), F32)
        ext[base + rows : base + rows + HALO, :] = jnp.where(sub == 0, strip, 0.0)
        ext[base + high - HALO : base + high, :] = jnp.where(sub == 0, 0.0, strip)
        field = ext[base : base + high, :]
        moved = pltpu.roll(field, 2 * HALO * i, 1) if i else field
        edges = jnp.where(place // (2 * HALO) == i, moved, edges)
    edge_out[...] = edges
    near_out[0:high, :] = edges
    near = tile ^ 1
    air = table_rows(n, msg, other, near, sub, sub) + value_rows(n, msg, other, sub)
    write_pairs(near_out, high, air)
    at = high + 20
    for step in range(2, n, 2):
        write_pairs(near_out, at, table_rows(n, msg, other, near ^ step, 1 - sub, sub))
        at += 8
    near_out[at : near_out.shape[0], :] = jnp.zeros((near_out.shape[0] - at, cols), F32)


def diffuse_kernel(n, levels, *refs):
    ext, near_in, edge_in, surface, share_rows, msg, other, adjoint_out, lev_out = refs[:9]
    sub, tile = lax.axis_index("sub"), lax.axis_index("tile")
    rows, cols = surface.shape
    high = rows + 8
    own_values = value_rows(n, msg, other, sub)
    near_values = read_pairs(near_in, high, 10)[4:]
    for i, out in enumerate(refs[9:]):
        air = table_rows(n, msg, other, tile ^ (2 * i + 2), 1 - sub, sub) + own_values
        air += read_pairs(near_in, high + 20 + 8 * i, 4) + near_values
        for at, row in enumerate(air):
            out[at : at + 1, :] = row
        out[20:24, :] = jnp.zeros((4, out.shape[1]), F32)
    place = edge_place((high, cols))
    near, beyond = near_in[0:high, :], edge_in[0:high, :]
    even = tile % 2 == 0
    right = jnp.where(tile < n - 1, jnp.where(even, near, beyond), 0.0)
    left = jnp.where(tile > 0, jnp.where(even, beyond, near), 0.0)
    edges = jnp.where(lax.rem(place, 2 * HALO) >= HALO, right, left)

    def wide(i):
        moved = pltpu.roll(edges, cols - 2 * HALO * i, 1) if i else edges
        return jnp.concatenate(
            [ext[high * i : high * (i + 1), :], jnp.where(place < 2 * HALO, moved, 0.0)], axis=1
        )

    def around(x):
        return (
            pltpu.roll(x, 1, 0)
            + pltpu.roll(x, high - 1, 0)
            + pltpu.roll(x, 1, 1)
            + pltpu.roll(x, 2 * cols - 1, 1)
        )

    wet = wide(levels)
    keep = wet * (1.0 - MIXING * around(wet))
    mix = MIXING * wet
    own_wet = wet[:rows, :cols]
    heat = jnp.zeros((rows, cols), F32)
    for z in range(levels):
        v = wet * wide(z)
        for sweep_index in range(STEPS):
            v = keep * v + mix * around(v)
        adjoint = own_wet * v[:rows, :cols]
        adjoint_out[z] = adjoint
        heat += share_rows[z : z + 1, :] * adjoint
    lev_out[0:rows, :] = surface[...]
    lev_out[rows : 2 * rows, :] = own_wet * heat


def bulk_adjoint(warmth_gap, flux_sens):
    transfer_rate = jnp.full_like(warmth_gap, TRANSFER)
    rates = [transfer_rate]
    slopes = []
    for sweep_index in range(BULK_ITERS):
        bent = jnp.tanh(transfer_rate * warmth_gap)
        slopes.append(TRANSFER * STABILITY * (1.0 - bent * bent))
        transfer_rate = TRANSFER * (1.0 + STABILITY * bent)
        rates.append(transfer_rate)
    contrast_sens = transfer_rate * flux_sens
    rate_sens = warmth_gap * flux_sens
    for sweep_index in reversed(range(BULK_ITERS)):
        inner_sens = rate_sens * slopes[sweep_index]
        contrast_sens = contrast_sens + inner_sens * rates[sweep_index]
        rate_sens = inner_sens * warmth_gap
    return contrast_sens


def onehot(index, count):
    cells = lax.broadcasted_iota(jnp.int32, (count, index.shape[1]), 0)
    return jnp.where(cells == index, 1.0, 0.0).astype(BF16)


def dot(a, b, ca, cb):
    return lax.dot_general(a, b, (((ca,), (cb,)), ((), ())), preferred_element_type=F32)


def look_up(air, at, picks, tables):
    for band in range(2):
        hot = onehot(air[band].astype(jnp.int32), air[band].shape[1])
        tables[at + band] = hot
        values = jnp.concatenate([air[4 + band], air[6 + band], air[8 + band]], axis=0)
        found = dot(jnp.concatenate(halves(values), axis=0), hot, 1, 0)
        found = found[0:3] + found[3:6]
        picks[0, at + band : at + band + 1, :] = found[0:1]
        picks[1, at + band : at + band + 1, :] = found[1:2]
        picks[2, at + band : at + band + 1, :] = air[2 + band] * found[2:3]


def near_kernel(n, high, msg, other, near_in, picks, tables):
    sub, tile = lax.axis_index("sub"), lax.axis_index("tile")
    own = table_rows(n, msg, other, tile, sub, sub) + value_rows(n, msg, other, sub)
    look_up(own, 0, picks, tables)
    look_up(read_pairs(near_in, high, 10), 2, picks, tables)


def slot_kernel(n, count, *refs):
    lev_parts, refs = refs[:count], refs[count:]
    near_picks, near_tables, marine, weight = refs[:4]
    far_in, refs = refs[4 : 3 + n // 2], refs[3 + n // 2 :]
    slots_out, returns, (held, picks, tables) = refs[0], refs[1 : 1 + n], refs[1 + n :]
    tile = lax.axis_index("tile")
    picks[:, 0:4, :] = near_picks[...]
    for i, ref in enumerate(far_in):
        for j in range(2):
            air = [ref[10 * j + k : 10 * j + k + 1, :] for k in range(10)]
            look_up(air, 4 * i + 4 + 2 * j, picks, tables)
    rows, cols = slots_out.shape
    table = jnp.concatenate(
        [sum(ref[rows * i : rows * (i + 1), :] for ref in lev_parts) for i in range(2)], axis=1
    )
    table = jnp.concatenate(halves(table), axis=0)
    owners = []
    for step in range(n):
        for band in range(2):
            at, place = 2 * step + band, 2 * (tile ^ step) + band
            cell = marine[pl.ds(place, 1), :]
            row, col = cell // cols, lax.rem(cell, cols)
            row_hot = onehot(row, rows)
            spread = dot(table, jnp.concatenate([row_hot, row_hot], axis=0), 0, 0)
            col_mask = lax.broadcasted_iota(jnp.int32, (cols, cell.shape[1]), 0) == col
            for i in range(2):
                piece = jnp.where(col_mask, spread[cols * i : cols * (i + 1)], 0.0)
                held[i, at : at + 1, :] = jnp.sum(piece, axis=0, keepdims=True)
            held[2, at : at + 1, :] = weight[pl.ds(place, 1), :]
            owners.append((row_hot, col_mask))

    difference = held[0] - picks[0]
    wind = picks[1]
    flux_sens = held[2] * held[1] + picks[2]
    contrast_sens = bulk_adjoint(wind * difference, flux_sens)
    surface_sens = contrast_sens * wind
    wind_sens = contrast_sens * difference
    total = jnp.zeros((rows, 2 * cols), F32)
    for step in range(n):
        for band in range(2):
            at = 2 * step + band
            row_hot, col_mask = owners[at]
            ocean = surface_sens[at : at + 1]
            spread = jnp.concatenate(
                [jnp.where(col_mask, x.astype(F32), 0.0).astype(BF16) for x in halves(ocean)], axis=0
            )
            total += dot(row_hot, spread, 1, 1)
            hot = near_tables[at] if at < 4 else tables[at]
            values = jnp.concatenate([ocean, wind_sens[at : at + 1]], axis=0)
            sums = dot(jnp.concatenate(halves(values), axis=0), hot, 1, 1)
            returns[step][2 * band : 2 * band + 2, :] = sums[0:2] + sums[2:4]
        returns[step][4:8, :] = jnp.zeros((4, returns[step].shape[1]), F32)
    slots_out[...] = total[:, :cols] + total[:, cols:]


def final_kernel(count, *refs):
    slots = refs[:count]
    adjoint, share_rows, sums, other, state_out, air_out, wind_out, state, air, wind, sems = refs[count:]
    sub = lax.axis_index("sub")
    gradient = sum(ref[...] for ref in slots)
    for z in range(adjoint.shape[0]):
        state[z] = adjoint[z] + share_rows[z : z + 1, :] * gradient
    copies = [pltpu.make_async_copy(state, state_out, sems.at[0])]
    copies[0].start()
    both = sums[...] + other[...]
    own = jnp.where(sub == 0, both[0:2], both[2:4])
    air[...] = -own[0:1]
    wind[...] = own[1:2]
    for i, (a, b) in enumerate(((air, air_out), (wind, wind_out))):
        copies.append(pltpu.make_async_copy(a, b, sems.at[1 + i]))
        copies[-1].start()
    for copy in copies:
        copy.wait()


def traded(x, step, swap=0):
    n, bands = lax.axis_size("tile"), lax.axis_size("sub")
    pairs = [
        (t * bands + s, (t ^ step) * bands + (s ^ swap)) for t in range(n) for s in range(bands)
    ]
    return lax.ppermute(x, ("tile", "sub"), pairs)


def beyond(x):
    n, levs, bands = (lax.axis_size(axis) for axis in ("tile", "lev", "sub"))

    def place(t, l, s):
        return (t * levs + l) * bands + s

    pairs = []
    for l in range(levs):
        for s in range(bands):
            for t in range(1, n - 1, 2):
                pairs += [(place(t, l, s), place(t + 1, l, s)), (place(t + 1, l, s), place(t, l, s))]
            pairs += [(place(t, l, s), place(t, l ^ 1, s ^ 1)) for t in (0, n - 1)]
    return lax.ppermute(x, ("tile", "lev", "sub"), pairs)


def lev_parts(x):
    if lax.axis_size("lev") == 2:
        return [x, lax.ppermute(x, "lev", [(0, 1), (1, 0)])]
    return [lax.psum(x, "lev")]


def per_device(
    marine_layered_warmth,
    bottom_sky_warmth,
    bottom_breeze_magnitude,
    depth_shares,
    piece_sky_box,
    sky_share_fraction,
    piece_marine_box,
    marine_share_fraction,
    marine_indicator,
    marine_result_adjoint,
    energy_transport_adjoint,
):
    n = lax.axis_size("tile")
    levels, rows, cols = marine_layered_warmth.shape
    cells = bottom_sky_warmth.shape[0]
    high = rows + 8
    raw = [marine_layered_warmth, marine_result_adjoint, marine_indicator, depth_shares]
    raw += [
        x.reshape(1, cells)
        for x in (bottom_sky_warmth, bottom_breeze_magnitude, energy_transport_adjoint)
    ]
    raw += [piece_sky_box[0], sky_share_fraction[0], piece_marine_box[0], marine_share_fraction[0]]
    raw = [pltpu.with_memory_space_constraint(x, pltpu.HBM) for x in raw]
    held = [pltpu.VMEM(x.shape, x.dtype) for x in [raw[0], raw[2]]]
    held += [pltpu.SMEM(depth_shares.shape, F32)]
    held += [pltpu.VMEM(x.shape, x.dtype) for x in raw[4:9]]
    msg, ext, surface, share_rows, marine, marine_weight = call(
        functools.partial(pack_kernel, n),
        [(4 * n + 16, cells), ((levels + 1) * high, cols), (rows, cols), (8, cols)]
        + [jax.ShapeDtypeStruct(x.shape, x.dtype) for x in raw[9:]],
        raw,
        [HBM] * len(raw),
        scratch=held + [pltpu.SemaphoreType.DMA((10 + levels,))],
    )
    other = traded(msg, 0, 1)
    ext, edge_out, near_out = call(
        functools.partial(send_kernel, n, levels + 1),
        [ext.shape, (high, cols), ((high + 20 + 4 * (n - 2) + 7) // 8 * 8, cols)],
        [msg, other, ext],
    )
    edge_in = beyond(edge_out)
    near_in = traded(near_out, 1)
    adjoint, lev_msg, *far_out = call(
        functools.partial(diffuse_kernel, n, levels),
        [(levels, rows, cols), (2 * rows, cols)] + [(24, cells)] * (n // 2 - 1),
        [ext, near_in, edge_in, surface, share_rows, msg, other],
    )
    lev_in = lev_parts(lev_msg)
    far_in = [traded(x, 2 * i + 2, 1) for i, x in enumerate(far_out)]
    picks, tables = call(
        functools.partial(near_kernel, n, high),
        [(3, 4, cells), jax.ShapeDtypeStruct((4, cells, cells), BF16)],
        [msg, other, near_in],
    )
    slots, *returns = call(
        functools.partial(slot_kernel, n, len(lev_in)),
        [(rows, cols)] + [(8, cells)] * n,
        [*lev_in, picks, tables, marine, marine_weight, *far_in],
        scratch=[pltpu.VMEM((3, 2 * n, cells), F32)] * 2
        + [pltpu.VMEM((2 * n, cells, cells), BF16)],
    )
    back = [traded(returns[step], step, 1) for step in range(1, n)]
    slot_parts = lev_parts(slots)
    sums = returns[0]
    for x in back:
        sums = sums + x
    sums_far = traded(sums, 0, 1)
    results = [(levels, rows, cols), (1, cells), (1, cells)]
    state, air_gradient, wind_gradient = call(
        functools.partial(final_kernel, len(slot_parts)),
        results,
        [*slot_parts, adjoint, share_rows, sums, sums_far],
        out_specs=[HBM] * 3,
        scratch=[pltpu.VMEM(x, F32) for x in results] + [pltpu.SemaphoreType.DMA((3,))],
    )
    return (state, air_gradient.reshape(cells), wind_gradient.reshape(cells))


def solution(mesh):
    return jax.shard_map(
        per_device,
        mesh=mesh,
        in_specs=(
            P(("ens", "lev"), "sub", "tile"),
            P(("ens", "tile", "lev", "sub")),
            P(("ens", "tile", "lev", "sub")),
            P("lev"),
            P(("tile", "lev", "sub"), None, None),
            P(("tile", "lev", "sub"), None, None),
            P(("tile", "lev", "sub"), None, None),
            P(("tile", "lev", "sub"), None, None),
            P("sub", "tile"),
            P(("ens", "lev"), "sub", "tile"),
            P(("ens", "tile", "lev", "sub")),
        ),
        out_specs=(
            P(("ens", "lev"), "sub", "tile"),
            P(("ens", "tile", "lev", "sub")),
            P(("ens", "tile", "lev", "sub")),
        ),
        check_vma=False,
    )
```

```python
import functools

import jax
import jax.numpy as jnp
from jax import lax
from jax.experimental import pallas as pl
from jax.experimental.pallas import tpu as pltpu
from jax.sharding import PartitionSpec as P

BULK_ITERS = 3
STEPS = 3
HALO = STEPS
MIXING = 0.2
TRANSFER = 1.0
STABILITY = 0.5
F32 = jnp.float32
BF16 = jnp.bfloat16
VMEM = pl.BlockSpec(memory_space=pltpu.VMEM)
HBM = pl.BlockSpec(memory_space=pltpu.HBM)


def call(kernel, outs, operands, specs=None, out_specs=None, scratch=(), aliases=None):
    outs = [jax.ShapeDtypeStruct(x, F32) if isinstance(x, tuple) else x for x in outs]
    return pl.pallas_call(
        kernel,
        out_shape=outs,
        in_specs=specs or [VMEM] * len(operands),
        out_specs=out_specs or [VMEM] * len(outs),
        scratch_shapes=list(scratch),
        input_output_aliases=aliases or {},
        compiler_params=pltpu.CompilerParams(vmem_limit_bytes=24 * 1024 * 1024),
    )(*operands)


def halves(x):
    high = x.astype(BF16)
    low = (x - high.astype(F32)).astype(BF16)
    return high, low


def pack_kernel(n, *refs):
    warm, cot, sea, shares, sky, breeze, energy, sky_index, sky_weight, marine, marine_weight = refs[:11]
    msg, ext, surface, share_rows, marine_out, marine_weight_out = refs[11:17]
    warm_in, sea_in, shares_in, sky_in, breeze_in, energy_in, index_in, weight_in, sems = refs[17:]
    rows, cols = sea.shape
    levels = warm.shape[0]
    high = rows + 8
    pairs = [(cot.at[z], ext.at[pl.ds(high * z, rows)]) for z in range(levels)]
    pairs += [(sea, sea_in), (sky_index, index_in), (sky_weight, weight_in)]
    pairs += [(sky, sky_in), (breeze, breeze_in), (energy, energy_in)]
    pairs += [(shares, shares_in), (warm, warm_in)]
    pairs += [(marine, marine_out), (marine_weight, marine_weight_out)]
    copies = [pltpu.make_async_copy(a, b, sems.at[i]) for i, (a, b) in enumerate(pairs)]
    for copy in copies:
        copy.start()
    sub = lax.axis_index("sub")
    msg[...] = jnp.zeros_like(msg)
    for z in range(levels + 1):
        ext[high * z + rows : high * (z + 1), :] = jnp.zeros((8, cols), F32)
    for copy in copies:
        copy.wait()
    ext[high * levels : high * levels + rows, :] = sea_in[...].astype(F32)
    msg[0 : 2 * n, :] = index_in[...].astype(F32)
    msg[2 * n : 4 * n, :] = weight_in[...]
    for i, ref in enumerate((sky_in, breeze_in, energy_in)):
        msg[4 * n + i : 4 * n + i + 1, :] = ref[...]
    base = 4 * n + 8
    for i in range(levels + 1):
        at, top, left = high * i, base + HALO * (i // 2), cols * (i % 2)
        outer = jnp.where(sub == 0, ext[at + rows - HALO : at + rows], ext[at : at + HALO])
        msg[top : top + HALO, left : left + cols] = outer
    surface[...] = sum(shares_in[z] * warm_in[z] for z in range(levels))
    for z in range(levels):
        share_rows[z : z + 1, :] = jnp.full((1, cols), shares_in[z], F32)


def halo_rows(n, msg, i, cols):
    top, left = 4 * n + 8 + HALO * (i // 2), cols * (i % 2)
    return msg[top : top + HALO, left : left + cols]


def both_bands(msg, other, index, sub):
    own, far = msg[pl.ds(index, 1), :], other[pl.ds(index, 1), :]
    return [jnp.where(sub == 0, own, far), jnp.where(sub == 0, far, own)]


def table_rows(n, msg, other, target, band, sub):
    row = 2 * target + band
    return both_bands(msg, other, row, sub) + both_bands(msg, other, 2 * n + row, sub)


def value_rows(n, msg, other, sub):
    return [x for i in range(3) for x in both_bands(msg, other, 4 * n + i, sub)]


def write_pairs(out, at, rows):
    cols = out.shape[1]
    for i, row in enumerate(rows):
        out[at + i : at + i + 1, :] = row[:, :cols]
        out[at + len(rows) + i : at + len(rows) + i + 1, :] = row[:, cols:]


def read_pairs(ref, at, count):
    return [
        jnp.concatenate([ref[at + i : at + i + 1, :], ref[at + count + i : at + count + i + 1, :]], axis=1)
        for i in range(count)
    ]


def fold_place(cols):
    lane = lax.broadcasted_iota(jnp.int32, (8, cols), 1)
    return lax.rem(lane + HALO, cols)


def fold_slots(high, cols, fields):
    each = cols // (2 * HALO * fields)
    groups = high // 8
    return [(g // each, g % each) for g in range(groups)], -(-groups // each)


def folded(ext, high, fields):
    cols = ext.shape[1]
    place = fold_place(cols) // (2 * HALO)
    slots, tiles = fold_slots(high, cols, fields)
    out = [jnp.zeros((8, cols), F32)] * tiles
    for g, (k, at) in enumerate(slots):
        for i in range(fields):
            slot = at * fields + i
            rows = ext[high * i + 8 * g : high * i + 8 * g + 8, :]
            moved = pltpu.roll(rows, 2 * HALO * slot, 1) if slot else rows
            out[k] = jnp.where(place == slot, moved, out[k])
    return jnp.concatenate(out, axis=0)


def unfolded(tiles, i, high, fields):
    cols = tiles[0].shape[1]
    place = fold_place(cols)
    out = []
    for k, at in fold_slots(high, cols, fields)[0]:
        slot = at * fields + i
        moved = pltpu.roll(tiles[k], cols - 2 * HALO * slot, 1) if slot else tiles[k]
        out.append(jnp.where(place < 2 * HALO, moved, 0.0))
    return jnp.concatenate(out, axis=0)


def send_kernel(n, fields, msg, other, ext_in, ext, edge_out, near_out):
    sub, tile = lax.axis_index("sub"), lax.axis_index("tile")
    cols = ext.shape[1]
    high = ext.shape[0] // fields
    rows = high - 8
    for i in range(fields):
        base = high * i
        strip = halo_rows(n, other, i, cols)
        ext[base : base + rows, :] = ext_in[base : base + rows, :]
        ext[base + rows : base + high, :] = jnp.zeros((8, cols), F32)
        ext[base + rows : base + rows + HALO, :] = jnp.where(sub == 0, strip, 0.0)
        ext[base + high - HALO : base + high, :] = jnp.where(sub == 0, 0.0, strip)
    edges = folded(ext, high, fields)
    fold = edges.shape[0]
    edge_out[...] = edges
    near_out[0:fold, :] = edges
    near = tile ^ 1
    air = table_rows(n, msg, other, near, sub, sub) + value_rows(n, msg, other, sub)
    write_pairs(near_out, fold, air)
    at = fold + 20
    for step in range(2, n, 2):
        write_pairs(near_out, at, table_rows(n, msg, other, near ^ step, 1 - sub, sub))
        at += 8
    near_out[at : near_out.shape[0], :] = jnp.zeros((near_out.shape[0] - at, cols), F32)


def diffuse_kernel(n, levels, *refs):
    ext, near_in, edge_in, surface, share_rows, msg, other, adjoint_out, lev_out = refs[:9]
    sub, tile = lax.axis_index("sub"), lax.axis_index("tile")
    rows, cols = surface.shape
    high = rows + 8
    fold = edge_in.shape[0]
    own_values = value_rows(n, msg, other, sub)
    near_values = read_pairs(near_in, fold, 10)[4:]
    for i, out in enumerate(refs[9:]):
        air = table_rows(n, msg, other, tile ^ (2 * i + 2), 1 - sub, sub) + own_values
        air += read_pairs(near_in, fold + 20 + 8 * i, 4) + near_values
        for at, row in enumerate(air):
            out[at : at + 1, :] = row
        out[20:24, :] = jnp.zeros((4, out.shape[1]), F32)
    even = tile % 2 == 0
    place = fold_place(cols)
    tiles = []
    for k in range(0, fold, 8):
        near, far = near_in[k : k + 8, :], edge_in[k : k + 8, :]
        right = jnp.where(tile < n - 1, jnp.where(even, near, far), 0.0)
        left = jnp.where(tile > 0, jnp.where(even, far, near), 0.0)
        tiles.append(jnp.where(lax.rem(place, 2 * HALO) >= HALO, right, left))

    def wide(i):
        return jnp.concatenate(
            [ext[high * i : high * (i + 1), :], unfolded(tiles, i, high, levels + 1)], axis=1
        )

    def around(x):
        return (
            pltpu.roll(x, 1, 0)
            + pltpu.roll(x, high - 1, 0)
            + pltpu.roll(x, 1, 1)
            + pltpu.roll(x, 2 * cols - 1, 1)
        )

    wet = wide(levels)
    keep = wet * (1.0 - MIXING * around(wet))
    mix = MIXING * wet
    own_wet = wet[:rows, :cols]
    heat = jnp.zeros((rows, cols), F32)
    for z in range(levels):
        v = wet * wide(z)
        for sweep_index in range(STEPS):
            v = keep * v + mix * around(v)
        adjoint = own_wet * v[:rows, :cols]
        adjoint_out[z] = adjoint
        heat += share_rows[z : z + 1, :] * adjoint
    lev_out[0:rows, :] = surface[...]
    lev_out[rows : 2 * rows, :] = own_wet * heat


def bulk_adjoint(warmth_gap, flux_sens):
    transfer_rate = jnp.full_like(warmth_gap, TRANSFER)
    rates = [transfer_rate]
    slopes = []
    for sweep_index in range(BULK_ITERS):
        bent = jnp.tanh(transfer_rate * warmth_gap)
        slopes.append(TRANSFER * STABILITY * (1.0 - bent * bent))
        transfer_rate = TRANSFER * (1.0 + STABILITY * bent)
        rates.append(transfer_rate)
    contrast_sens = transfer_rate * flux_sens
    rate_sens = warmth_gap * flux_sens
    for sweep_index in reversed(range(BULK_ITERS)):
        inner_sens = rate_sens * slopes[sweep_index]
        contrast_sens = contrast_sens + inner_sens * rates[sweep_index]
        rate_sens = inner_sens * warmth_gap
    return contrast_sens


def onehot(index, count):
    cells = lax.broadcasted_iota(jnp.int32, (count, index.shape[1]), 0)
    return jnp.where(cells == index, 1.0, 0.0).astype(BF16)


def dot(a, b, ca, cb):
    return lax.dot_general(a, b, (((ca,), (cb,)), ((), ())), preferred_element_type=F32)


def look_up(air, at, picks, tables):
    for band in range(2):
        hot = onehot(air[band].astype(jnp.int32), air[band].shape[1])
        tables[at + band] = hot
        values = jnp.concatenate([air[4 + band], air[6 + band], air[8 + band]], axis=0)
        found = dot(jnp.concatenate(halves(values), axis=0), hot, 1, 0)
        found = found[0:3] + found[3:6]
        picks[0, at + band : at + band + 1, :] = found[0:1]
        picks[1, at + band : at + band + 1, :] = found[1:2]
        picks[2, at + band : at + band + 1, :] = air[2 + band] * found[2:3]


def near_kernel(n, fold, msg, other, near_in, picks, tables):
    sub, tile = lax.axis_index("sub"), lax.axis_index("tile")
    own = table_rows(n, msg, other, tile, sub, sub) + value_rows(n, msg, other, sub)
    look_up(own, 0, picks, tables)
    look_up(read_pairs(near_in, fold, 10), 2, picks, tables)


def slot_kernel(n, count, *refs):
    lev_parts, refs = refs[:count], refs[count:]
    near_picks, near_tables, marine, weight = refs[:4]
    far_in, refs = refs[4 : 3 + n // 2], refs[3 + n // 2 :]
    slots_out, returns, (held, picks, tables) = refs[0], refs[1 : 1 + n], refs[1 + n :]
    tile = lax.axis_index("tile")
    picks[:, 0:4, :] = near_picks[...]
    for i, ref in enumerate(far_in):
        for j in range(2):
            air = [ref[10 * j + k : 10 * j + k + 1, :] for k in range(10)]
            look_up(air, 4 * i + 4 + 2 * j, picks, tables)
    rows, cols = slots_out.shape
    table = jnp.concatenate(
        [sum(ref[rows * i : rows * (i + 1), :] for ref in lev_parts) for i in range(2)], axis=1
    )
    table = jnp.concatenate(halves(table), axis=0)
    owners = []
    for step in range(n):
        for band in range(2):
            at, place = 2 * step + band, 2 * (tile ^ step) + band
            cell = marine[pl.ds(place, 1), :]
            row, col = cell // cols, lax.rem(cell, cols)
            row_hot = onehot(row, rows)
            spread = dot(table, jnp.concatenate([row_hot, row_hot], axis=0), 0, 0)
            col_mask = lax.broadcasted_iota(jnp.int32, (cols, cell.shape[1]), 0) == col
            for i in range(2):
                piece = jnp.where(col_mask, spread[cols * i : cols * (i + 1)], 0.0)
                held[i, at : at + 1, :] = jnp.sum(piece, axis=0, keepdims=True)
            held[2, at : at + 1, :] = weight[pl.ds(place, 1), :]
            owners.append((row_hot, col_mask))

    difference = held[0] - picks[0]
    wind = picks[1]
    flux_sens = held[2] * held[1] + picks[2]
    contrast_sens = bulk_adjoint(wind * difference, flux_sens)
    surface_sens = contrast_sens * wind
    wind_sens = contrast_sens * difference
    total = jnp.zeros((rows, 2 * cols), F32)
    for step in range(n):
        for band in range(2):
            at = 2 * step + band
            row_hot, col_mask = owners[at]
            ocean = surface_sens[at : at + 1]
            spread = jnp.concatenate(
                [jnp.where(col_mask, x.astype(F32), 0.0).astype(BF16) for x in halves(ocean)], axis=0
            )
            total += dot(row_hot, spread, 1, 1)
            hot = near_tables[at] if at < 4 else tables[at]
            values = jnp.concatenate([ocean, wind_sens[at : at + 1]], axis=0)
            sums = dot(jnp.concatenate(halves(values), axis=0), hot, 1, 1)
            returns[step][2 * band : 2 * band + 2, :] = sums[0:2] + sums[2:4]
        returns[step][4:8, :] = jnp.zeros((4, returns[step].shape[1]), F32)
    slots_out[...] = total[:, :cols] + total[:, cols:]


def final_kernel(count, *refs):
    slots = refs[:count]
    adjoint, share_rows, sums, other, state_out, air_out, wind_out, state, air, wind, sems = refs[count:]
    sub = lax.axis_index("sub")
    gradient = sum(ref[...] for ref in slots)
    for z in range(adjoint.shape[0]):
        state[z] = adjoint[z] + share_rows[z : z + 1, :] * gradient
    copies = [pltpu.make_async_copy(state, state_out, sems.at[0])]
    copies[0].start()
    both = sums[...] + other[...]
    own = jnp.where(sub == 0, both[0:2], both[2:4])
    air[...] = -own[0:1]
    wind[...] = own[1:2]
    for i, (a, b) in enumerate(((air, air_out), (wind, wind_out))):
        copies.append(pltpu.make_async_copy(a, b, sems.at[1 + i]))
        copies[-1].start()
    for copy in copies:
        copy.wait()


def traded(x, step, swap=0):
    n, bands = lax.axis_size("tile"), lax.axis_size("sub")
    pairs = [
        (t * bands + s, (t ^ step) * bands + (s ^ swap)) for t in range(n) for s in range(bands)
    ]
    return lax.ppermute(x, ("tile", "sub"), pairs)


def beyond(x):
    n, levs, bands = (lax.axis_size(axis) for axis in ("tile", "lev", "sub"))

    def place(t, l, s):
        return (t * levs + l) * bands + s

    pairs = []
    for l in range(levs):
        for s in range(bands):
            for t in range(1, n - 1, 2):
                pairs += [(place(t, l, s), place(t + 1, l, s)), (place(t + 1, l, s), place(t, l, s))]
            pairs += [(place(t, l, s), place(t, l ^ 1, s ^ 1)) for t in (0, n - 1)]
    return lax.ppermute(x, ("tile", "lev", "sub"), pairs)


def lev_parts(x):
    if lax.axis_size("lev") == 2:
        return [x, lax.ppermute(x, "lev", [(0, 1), (1, 0)])]
    return [lax.psum(x, "lev")]


def per_device(
    marine_layered_warmth,
    bottom_sky_warmth,
    bottom_breeze_magnitude,
    depth_shares,
    piece_sky_box,
    sky_share_fraction,
    piece_marine_box,
    marine_share_fraction,
    marine_indicator,
    marine_result_adjoint,
    energy_transport_adjoint,
):
    n = lax.axis_size("tile")
    levels, rows, cols = marine_layered_warmth.shape
    cells = bottom_sky_warmth.shape[0]
    high = rows + 8
    raw = [marine_layered_warmth, marine_result_adjoint, marine_indicator, depth_shares]
    raw += [
        x.reshape(1, cells)
        for x in (bottom_sky_warmth, bottom_breeze_magnitude, energy_transport_adjoint)
    ]
    raw += [piece_sky_box[0], sky_share_fraction[0], piece_marine_box[0], marine_share_fraction[0]]
    raw = [pltpu.with_memory_space_constraint(x, pltpu.HBM) for x in raw]
    held = [pltpu.VMEM(x.shape, x.dtype) for x in [raw[0], raw[2]]]
    held += [pltpu.SMEM(depth_shares.shape, F32)]
    held += [pltpu.VMEM(x.shape, x.dtype) for x in raw[4:9]]
    msg, ext, surface, share_rows, marine, marine_weight = call(
        functools.partial(pack_kernel, n),
        [(4 * n + 16, cells), ((levels + 1) * high, cols), (rows, cols), (8, cols)]
        + [jax.ShapeDtypeStruct(x.shape, x.dtype) for x in raw[9:]],
        raw,
        [HBM] * len(raw),
        scratch=held + [pltpu.SemaphoreType.DMA((10 + levels,))],
    )
    other = traded(msg, 0, 1)
    fold = 8 * fold_slots(high, cols, levels + 1)[1]
    ext, edge_out, near_out = call(
        functools.partial(send_kernel, n, levels + 1),
        [ext.shape, (fold, cols), ((fold + 20 + 4 * (n - 2) + 7) // 8 * 8, cols)],
        [msg, other, ext],
    )
    edge_in = beyond(edge_out)
    near_in = traded(near_out, 1)
    adjoint, lev_msg, *far_out = call(
        functools.partial(diffuse_kernel, n, levels),
        [(levels, rows, cols), (2 * rows, cols)] + [(24, cells)] * (n // 2 - 1),
        [ext, near_in, edge_in, surface, share_rows, msg, other],
    )
    lev_in = lev_parts(lev_msg)
    far_in = [traded(x, 2 * i + 2, 1) for i, x in enumerate(far_out)]
    picks, tables = call(
        functools.partial(near_kernel, n, fold),
        [(3, 4, cells), jax.ShapeDtypeStruct((4, cells, cells), BF16)],
        [msg, other, near_in],
    )
    slots, *returns = call(
        functools.partial(slot_kernel, n, len(lev_in)),
        [(rows, cols)] + [(8, cells)] * n,
        [*lev_in, picks, tables, marine, marine_weight, *far_in],
        scratch=[pltpu.VMEM((3, 2 * n, cells), F32)] * 2
        + [pltpu.VMEM((2 * n, cells, cells), BF16)],
    )
    back = [traded(returns[step], step, 1) for step in range(1, n)]
    slot_parts = lev_parts(slots)
    sums = returns[0]
    for x in back:
        sums = sums + x
    sums_far = traded(sums, 0, 1)
    results = [(levels, rows, cols), (1, cells), (1, cells)]
    state, air_gradient, wind_gradient = call(
        functools.partial(final_kernel, len(slot_parts)),
        results,
        [*slot_parts, adjoint, share_rows, sums, sums_far],
        out_specs=[HBM] * 3,
        scratch=[pltpu.VMEM(x, F32) for x in results] + [pltpu.SemaphoreType.DMA((3,))],
    )
    return (state, air_gradient.reshape(cells), wind_gradient.reshape(cells))


def solution(mesh):
    return jax.shard_map(
        per_device,
        mesh=mesh,
        in_specs=(
            P(("ens", "lev"), "sub", "tile"),
            P(("ens", "tile", "lev", "sub")),
            P(("ens", "tile", "lev", "sub")),
            P("lev"),
            P(("tile", "lev", "sub"), None, None),
            P(("tile", "lev", "sub"), None, None),
            P(("tile", "lev", "sub"), None, None),
            P(("tile", "lev", "sub"), None, None),
            P("sub", "tile"),
            P(("ens", "lev"), "sub", "tile"),
            P(("ens", "tile", "lev", "sub")),
        ),
        out_specs=(
            P(("ens", "lev"), "sub", "tile"),
            P(("ens", "tile", "lev", "sub")),
            P(("ens", "tile", "lev", "sub")),
        ),
        check_vma=False,
    )
```

```python
import functools

import jax
import jax.numpy as jnp
from jax import lax
from jax.experimental import pallas as pl
from jax.experimental.pallas import tpu as pltpu
from jax.sharding import PartitionSpec as P

BULK_ITERS = 3
STEPS = 3
HALO = STEPS
MIXING = 0.2
TRANSFER = 1.0
STABILITY = 0.5
F32 = jnp.float32
BF16 = jnp.bfloat16
VMEM = pl.BlockSpec(memory_space=pltpu.VMEM)
HBM = pl.BlockSpec(memory_space=pltpu.HBM)


def call(kernel, outs, operands, specs=None, out_specs=None, scratch=(), aliases=None):
    outs = [jax.ShapeDtypeStruct(x, F32) if isinstance(x, tuple) else x for x in outs]
    return pl.pallas_call(
        kernel,
        out_shape=outs,
        in_specs=specs or [VMEM] * len(operands),
        out_specs=out_specs or [VMEM] * len(outs),
        scratch_shapes=list(scratch),
        input_output_aliases=aliases or {},
        compiler_params=pltpu.CompilerParams(vmem_limit_bytes=24 * 1024 * 1024),
    )(*operands)


def halves(x):
    high = x.astype(BF16)
    low = (x - high.astype(F32)).astype(BF16)
    return high, low


def pack_kernel(n, *refs):
    warm, cot, sea, shares, sky, breeze, energy, sky_index, sky_weight, marine, marine_weight = refs[:11]
    msg, ext, surface, share_rows, marine_out, marine_weight_out = refs[11:17]
    warm_in, sea_in, shares_in, sky_in, breeze_in, energy_in, index_in, weight_in, sems = refs[17:]
    rows, cols = sea.shape
    levels = warm.shape[0]
    high = rows + 8
    pairs = [(cot.at[z], ext.at[pl.ds(high * z, rows)]) for z in range(levels)]
    pairs += [(sea, sea_in), (sky_index, index_in), (sky_weight, weight_in)]
    pairs += [(sky, sky_in), (breeze, breeze_in), (energy, energy_in)]
    pairs += [(shares, shares_in), (warm, warm_in)]
    pairs += [(marine, marine_out), (marine_weight, marine_weight_out)]
    copies = [pltpu.make_async_copy(a, b, sems.at[i]) for i, (a, b) in enumerate(pairs)]
    for copy in copies:
        copy.start()
    sub = lax.axis_index("sub")
    msg[...] = jnp.zeros_like(msg)
    for z in range(levels + 1):
        ext[high * z + rows : high * (z + 1), :] = jnp.zeros((8, cols), F32)
    for copy in copies:
        copy.wait()
    ext[high * levels : high * levels + rows, :] = sea_in[...].astype(F32)
    msg[0 : 2 * n, :] = index_in[...].astype(F32)
    msg[2 * n : 4 * n, :] = weight_in[...]
    for i, ref in enumerate((sky_in, breeze_in, energy_in)):
        msg[4 * n + i : 4 * n + i + 1, :] = ref[...]
    base = 4 * n + 8
    for i in range(levels + 1):
        at, top, left = high * i, base + HALO * (i // 2), cols * (i % 2)
        outer = jnp.where(sub == 0, ext[at + rows - HALO : at + rows], ext[at : at + HALO])
        msg[top : top + HALO, left : left + cols] = outer
    surface[...] = sum(shares_in[z] * warm_in[z] for z in range(levels))
    for z in range(levels):
        share_rows[z : z + 1, :] = jnp.full((1, cols), shares_in[z], F32)


def halo_rows(n, msg, i, cols):
    top, left = 4 * n + 8 + HALO * (i // 2), cols * (i % 2)
    return msg[top : top + HALO, left : left + cols]


def both_bands(msg, other, index, sub):
    own, far = msg[pl.ds(index, 1), :], other[pl.ds(index, 1), :]
    return [jnp.where(sub == 0, own, far), jnp.where(sub == 0, far, own)]


def table_rows(n, msg, other, target, band, sub):
    row = 2 * target + band
    return both_bands(msg, other, row, sub) + both_bands(msg, other, 2 * n + row, sub)


def value_rows(n, msg, other, sub):
    return [x for i in range(3) for x in both_bands(msg, other, 4 * n + i, sub)]


def write_pairs(out, at, rows):
    cols = out.shape[1]
    for i, row in enumerate(rows):
        out[at + i : at + i + 1, :] = row[:, :cols]
        out[at + len(rows) + i : at + len(rows) + i + 1, :] = row[:, cols:]


def write_halves(out, at, x):
    count, cols = x.shape[0], out.shape[1]
    out[at : at + count, :] = x[:, :cols]
    out[at + count : at + 2 * count, :] = x[:, cols:]


def read_halves(ref, at, count):
    return jnp.concatenate([ref[at : at + count, :], ref[at + count : at + 2 * count, :]], axis=1)


def read_pairs(ref, at, count):
    return [
        jnp.concatenate([ref[at + i : at + i + 1, :], ref[at + count + i : at + count + i + 1, :]], axis=1)
        for i in range(count)
    ]


def fold_place(cols):
    lane = lax.broadcasted_iota(jnp.int32, (8, cols), 1)
    return lax.rem(lane + HALO, cols)


def fold_slots(high, cols, fields):
    each = cols // (2 * HALO * fields)
    groups = high // 8
    return [(g // each, g % each) for g in range(groups)], -(-groups // each)


def folded(ext, high, fields):
    cols = ext.shape[1]
    place = fold_place(cols) // (2 * HALO)
    slots, tiles = fold_slots(high, cols, fields)
    out = [jnp.zeros((8, cols), F32)] * tiles
    for g, (k, at) in enumerate(slots):
        for i in range(fields):
            slot = at * fields + i
            rows = ext[high * i + 8 * g : high * i + 8 * g + 8, :]
            moved = pltpu.roll(rows, 2 * HALO * slot, 1) if slot else rows
            out[k] = jnp.where(place == slot, moved, out[k])
    return jnp.concatenate(out, axis=0)


def unfolded(tiles, i, high, fields):
    cols = tiles[0].shape[1]
    place = fold_place(cols)
    out = []
    for k, at in fold_slots(high, cols, fields)[0]:
        slot = at * fields + i
        moved = pltpu.roll(tiles[k], cols - 2 * HALO * slot, 1) if slot else tiles[k]
        out.append(jnp.where(place < 2 * HALO, moved, 0.0))
    return jnp.concatenate(out, axis=0)


def send_kernel(n, fields, msg, other, ext_in, ext, edge_out, near_out):
    sub, tile = lax.axis_index("sub"), lax.axis_index("tile")
    cols = ext.shape[1]
    high = ext.shape[0] // fields
    rows = high - 8
    for i in range(fields):
        base = high * i
        strip = halo_rows(n, other, i, cols)
        ext[base : base + rows, :] = ext_in[base : base + rows, :]
        ext[base + rows : base + high, :] = jnp.zeros((8, cols), F32)
        ext[base + rows : base + rows + HALO, :] = jnp.where(sub == 0, strip, 0.0)
        ext[base + high - HALO : base + high, :] = jnp.where(sub == 0, 0.0, strip)
    edges = folded(ext, high, fields)
    fold = edges.shape[0]
    edge_out[...] = edges
    near_out[0:fold, :] = edges
    near = tile ^ 1
    air = table_rows(n, msg, other, near, sub, sub) + value_rows(n, msg, other, sub)
    write_pairs(near_out, fold, air)
    at = fold + 20
    for step in range(2, n, 2):
        write_pairs(near_out, at, table_rows(n, msg, other, near ^ step, 1 - sub, sub))
        at += 8
    near_out[at : near_out.shape[0], :] = jnp.zeros((near_out.shape[0] - at, cols), F32)


def diffuse_kernel(n, levels, *refs):
    ext, near_in, edge_in, surface, share_rows, msg, other, marine, adjoint_out, lev_out = refs[:10]
    sub, tile = lax.axis_index("sub"), lax.axis_index("tile")
    rows, cols = surface.shape
    high = rows + 8
    fold = edge_in.shape[0]
    own_values = value_rows(n, msg, other, sub)
    near_values = read_pairs(near_in, fold, 10)[4:]
    for i, out in enumerate(refs[10:]):
        air = table_rows(n, msg, other, tile ^ (2 * i + 2), 1 - sub, sub) + own_values
        air += read_pairs(near_in, fold + 20 + 8 * i, 4) + near_values
        for at, row in enumerate(air):
            out[at : at + 1, :] = row
        out[20:24, :] = jnp.zeros((4, out.shape[1]), F32)
    even = tile % 2 == 0
    place = fold_place(cols)
    tiles = []
    for k in range(0, fold, 8):
        near, far = near_in[k : k + 8, :], edge_in[k : k + 8, :]
        right = jnp.where(tile < n - 1, jnp.where(even, near, far), 0.0)
        left = jnp.where(tile > 0, jnp.where(even, far, near), 0.0)
        tiles.append(jnp.where(lax.rem(place, 2 * HALO) >= HALO, right, left))

    def wide(i):
        return jnp.concatenate(
            [ext[high * i : high * (i + 1), :], unfolded(tiles, i, high, levels + 1)], axis=1
        )

    def around(x):
        return (
            pltpu.roll(x, 1, 0)
            + pltpu.roll(x, high - 1, 0)
            + pltpu.roll(x, 1, 1)
            + pltpu.roll(x, 2 * cols - 1, 1)
        )

    wet = wide(levels)
    keep = wet * (1.0 - MIXING * around(wet))
    mix = MIXING * wet
    own_wet = wet[:rows, :cols]
    heat = jnp.zeros((rows, cols), F32)
    for z in range(levels):
        v = wet * wide(z)
        for sweep_index in range(STEPS):
            v = keep * v + mix * around(v)
        adjoint = own_wet * v[:rows, :cols]
        adjoint_out[z] = adjoint
        heat += share_rows[z : z + 1, :] * adjoint
    lev_out[0:rows, :] = surface[...]
    lev_out[rows : 2 * rows, :] = own_wet * heat
    if lev_out.shape[0] > 2 * rows:
        write_halves(lev_out, 2 * rows, marine[...].astype(F32))


def bulk_adjoint(warmth_gap, flux_sens):
    transfer_rate = jnp.full_like(warmth_gap, TRANSFER)
    rates = [transfer_rate]
    slopes = []
    for sweep_index in range(BULK_ITERS):
        bent = jnp.tanh(transfer_rate * warmth_gap)
        slopes.append(TRANSFER * STABILITY * (1.0 - bent * bent))
        transfer_rate = TRANSFER * (1.0 + STABILITY * bent)
        rates.append(transfer_rate)
    contrast_sens = transfer_rate * flux_sens
    rate_sens = warmth_gap * flux_sens
    for sweep_index in reversed(range(BULK_ITERS)):
        inner_sens = rate_sens * slopes[sweep_index]
        contrast_sens = contrast_sens + inner_sens * rates[sweep_index]
        rate_sens = inner_sens * warmth_gap
    return contrast_sens


def onehot(index, count):
    cells = lax.broadcasted_iota(jnp.int32, (count, index.shape[1]), 0)
    return jnp.where(cells == index, 1.0, 0.0).astype(BF16)


def dot(a, b, ca, cb):
    return lax.dot_general(a, b, (((ca,), (cb,)), ((), ())), preferred_element_type=F32)


def look_up(air, at, picks, tables):
    for band in range(2):
        hot = onehot(air[band].astype(jnp.int32), air[band].shape[1])
        tables[at + band] = hot
        values = jnp.concatenate([air[4 + band], air[6 + band], air[8 + band]], axis=0)
        found = dot(jnp.concatenate(halves(values), axis=0), hot, 1, 0)
        found = found[0:3] + found[3:6]
        picks[0, at + band : at + band + 1, :] = found[0:1]
        picks[1, at + band : at + band + 1, :] = found[1:2]
        picks[2, at + band : at + band + 1, :] = air[2 + band] * found[2:3]


def near_kernel(n, fold, msg, other, near_in, picks, tables):
    sub, tile = lax.axis_index("sub"), lax.axis_index("tile")
    own = table_rows(n, msg, other, tile, sub, sub) + value_rows(n, msg, other, sub)
    look_up(own, 0, picks, tables)
    look_up(read_pairs(near_in, fold, 10), 2, picks, tables)


def slot_kernel(n, count, rows, *refs):
    lev_parts, refs = refs[:count], refs[count:]
    near_picks, near_tables, marine, weight = refs[:4]
    far_in, refs = refs[4 : 3 + n // 2], refs[3 + n // 2 :]
    values_out, chip_out, returns = refs[0], refs[1], refs[2 : 2 + n]
    held, picks, tables = refs[2 + n :]
    sub, tile = lax.axis_index("sub"), lax.axis_index("tile")
    cols = chip_out.shape[1]
    picks[:, 0:4, :] = near_picks[...]
    for i, ref in enumerate(far_in):
        for j in range(2):
            air = [ref[10 * j + k : 10 * j + k + 1, :] for k in range(10)]
            look_up(air, 4 * i + 4 + 2 * j, picks, tables)
    table = jnp.concatenate(
        [sum(ref[rows * i : rows * (i + 1), :] for ref in lev_parts) for i in range(2)], axis=1
    )
    table = jnp.concatenate(halves(table), axis=0)
    for step in range(n):
        for band in range(2):
            at, place = 2 * step + band, 2 * (tile ^ step) + band
            cell = marine[pl.ds(place, 1), :]
            row, col = cell // cols, lax.rem(cell, cols)
            row_hot = onehot(row, rows)
            spread = dot(table, jnp.concatenate([row_hot, row_hot], axis=0), 0, 0)
            col_mask = lax.broadcasted_iota(jnp.int32, (cols, cell.shape[1]), 0) == col
            for i in range(2):
                piece = jnp.where(col_mask, spread[cols * i : cols * (i + 1)], 0.0)
                held[i, at : at + 1, :] = jnp.sum(piece, axis=0, keepdims=True)
            held[2, at : at + 1, :] = weight[pl.ds(place, 1), :]

    difference = held[0] - picks[0]
    wind = picks[1]
    flux_sens = held[2] * held[1] + picks[2]
    contrast_sens = bulk_adjoint(wind * difference, flux_sens)
    surface_sens = contrast_sens * wind
    wind_sens = contrast_sens * difference
    values_out[...] = surface_sens
    for step in range(n):
        for band in range(2):
            at = 2 * step + band
            hot = near_tables[at] if at < 4 else tables[at]
            values = jnp.concatenate([surface_sens[at : at + 1], wind_sens[at : at + 1]], axis=0)
            sums = dot(jnp.concatenate(halves(values), axis=0), hot, 1, 1)
            sums = sums[0:2] + sums[2:4]
            returns[step][2 * band : 2 * band + 2, :] = sums[:, :cols]
            returns[step][2 * band + 4 : 2 * band + 6, :] = sums[:, cols:]
    if n == 4:
        chip_out[0:8, :] = jnp.where(sub == 0, returns[2][...], returns[1][...])
        write_halves(chip_out, 8, surface_sens)
        chip_out[8:16, :] = jnp.where(sub == 0, returns[3][...], chip_out[8:16, :])
        chip_out[24:40, :] = lev_parts[-1][2 * rows : 2 * rows + 16, :]


def scatter(n, rows, cols, tile, cell_of, value_of):
    total = jnp.zeros((rows, 2 * cols), F32)
    for step in range(n):
        for band in range(2):
            cell = cell_of(2 * (tile ^ step) + band)
            row, col = cell // cols, lax.rem(cell, cols)
            col_mask = lax.broadcasted_iota(jnp.int32, (cols, cell.shape[1]), 0) == col
            value = value_of(2 * step + band)
            spread = jnp.concatenate(
                [jnp.where(col_mask, x.astype(F32), 0.0).astype(BF16) for x in halves(value)], axis=0
            )
            total += dot(onehot(row, rows), spread, 1, 1)
    return total[:, :cols] + total[:, cols:]


def own_kernel(n, marine, values, out):
    tile = lax.axis_index("tile")
    rows, cols = out.shape
    out[...] = scatter(
        n, rows, cols, tile, lambda i: marine[pl.ds(i, 1), :], lambda i: values[i : i + 1, :]
    )


def post_kernel(n, first, second, own, slots, lev_in, theirs, gradient, out, cells, values):
    even = lax.axis_index("sub") == 0
    tile = lax.axis_index("tile")
    rows, cols = gradient.shape
    out[0:8, :] = first[0:8, :] + own[...] + jnp.where(even, 0.0, second[0:8, :])

    @pl.when(even)
    def _():
        for band, (ref, at) in enumerate(((lev_in, 2 * rows), (theirs, 24))):
            cells[...] = read_halves(ref, at, 2 * n).astype(jnp.int32)
            values[...] = read_halves(second, 4 * n * band, 2 * n)
            total = scatter(
                n, rows, cols, tile, lambda i: cells[pl.ds(i, 1), :], lambda i: values[i : i + 1, :]
            )
            if band == 0:
                gradient[...] = slots[...] + total
            else:
                out[8 : rows + 8, :] = total

    @pl.when(jnp.logical_not(even))
    def _():
        gradient[...] = slots[...]
        out[8 : rows + 8, :] = jnp.zeros_like(slots)


def merge_kernel(values, near, two, three, theirs, first, second):
    even = lax.axis_index("sub") == 0
    first[...] = jnp.zeros_like(first)
    first[0:8, :] = jnp.where(even, near[...] + theirs[0:8, :], three[...] + theirs[8:16, :])
    write_halves(second, 0, values[...])
    second[0:8, :] = jnp.where(even, second[0:8, :], two[...] + theirs[0:8, :])
    second[16:32, :] = theirs[8:24, :]


def final_kernel(merged, slots, adjoint, share_rows, sums, other, *refs):
    state_out, air_out, wind_out, state, air, wind, sems = refs
    sub = lax.axis_index("sub")
    gradient = slots[...]
    if merged:
        gradient += jnp.where(sub == 0, 0.0, other[8 : slots.shape[0] + 8, :])
    for z in range(adjoint.shape[0]):
        state[z] = adjoint[z] + share_rows[z : z + 1, :] * gradient
    copies = [pltpu.make_async_copy(state, state_out, sems.at[0])]
    copies[0].start()
    both = sums[0:8, :] + other[0:8, :]
    own = [jnp.where(sub == 0, both[i : i + 2], both[i + 2 : i + 4]) for i in (0, 4)]
    own = jnp.concatenate(own, axis=1)
    air[...] = -own[0:1]
    wind[...] = own[1:2]
    for i, (a, b) in enumerate(((air, air_out), (wind, wind_out))):
        copies.append(pltpu.make_async_copy(a, b, sems.at[1 + i]))
        copies[-1].start()
    for copy in copies:
        copy.wait()


def traded(x, step, swap=0):
    n, bands = lax.axis_size("tile"), lax.axis_size("sub")
    pairs = [
        (t * bands + s, (t ^ step) * bands + (s ^ swap)) for t in range(n) for s in range(bands)
    ]
    return lax.ppermute(x, ("tile", "sub"), pairs)


def beyond(x):
    n, levs, bands = (lax.axis_size(axis) for axis in ("tile", "lev", "sub"))

    def place(t, l, s):
        return (t * levs + l) * bands + s

    pairs = []
    for l in range(levs):
        for s in range(bands):
            for t in range(1, n - 1, 2):
                pairs += [(place(t, l, s), place(t + 1, l, s)), (place(t + 1, l, s), place(t, l, s))]
            pairs += [(place(t, l, s), place(t, l ^ 1, s ^ 1)) for t in (0, n - 1)]
    return lax.ppermute(x, ("tile", "lev", "sub"), pairs)


def by_core(x, even, odd):
    n, levs, bands = (lax.axis_size(axis) for axis in ("tile", "lev", "sub"))
    pairs = []
    for t in range(n):
        for l in range(levs):
            for s in range(bands):
                tx, lx = odd if s else even
                pairs.append(((t * levs + l) * bands + s, ((t ^ tx) * levs + (l ^ lx)) * bands + s))
    return lax.ppermute(x, ("tile", "lev", "sub"), pairs)


def lev_parts(x):
    if lax.axis_size("lev") == 2:
        return [x, lax.ppermute(x, "lev", [(0, 1), (1, 0)])]
    return [lax.psum(x, "lev")]


def per_device(
    marine_layered_warmth,
    bottom_sky_warmth,
    bottom_breeze_magnitude,
    depth_shares,
    piece_sky_box,
    sky_share_fraction,
    piece_marine_box,
    marine_share_fraction,
    marine_indicator,
    marine_result_adjoint,
    energy_transport_adjoint,
):
    n, levs = lax.axis_size("tile"), lax.axis_size("lev")
    levels, rows, cols = marine_layered_warmth.shape
    cells = bottom_sky_warmth.shape[0]
    high = rows + 8
    raw = [marine_layered_warmth, marine_result_adjoint, marine_indicator, depth_shares]
    raw += [
        x.reshape(1, cells)
        for x in (bottom_sky_warmth, bottom_breeze_magnitude, energy_transport_adjoint)
    ]
    raw += [piece_sky_box[0], sky_share_fraction[0], piece_marine_box[0], marine_share_fraction[0]]
    raw = [pltpu.with_memory_space_constraint(x, pltpu.HBM) for x in raw]
    held = [pltpu.VMEM(x.shape, x.dtype) for x in [raw[0], raw[2]]]
    held += [pltpu.SMEM(depth_shares.shape, F32)]
    held += [pltpu.VMEM(x.shape, x.dtype) for x in raw[4:9]]
    msg, ext, surface, share_rows, marine, marine_weight = call(
        functools.partial(pack_kernel, n),
        [(4 * n + 16, cells), ((levels + 1) * high, cols), (rows, cols), (8, cols)]
        + [jax.ShapeDtypeStruct(x.shape, x.dtype) for x in raw[9:]],
        raw,
        [HBM] * len(raw),
        scratch=held + [pltpu.SemaphoreType.DMA((10 + levels,))],
    )
    other = traded(msg, 0, 1)
    fold = 8 * fold_slots(high, cols, levels + 1)[1]
    ext, edge_out, near_out = call(
        functools.partial(send_kernel, n, levels + 1),
        [ext.shape, (fold, cols), ((fold + 20 + 4 * (n - 2) + 7) // 8 * 8, cols)],
        [msg, other, ext],
    )
    edge_in = beyond(edge_out)
    near_in = traded(near_out, 1)
    merged = n == 4 and levs == 2
    adjoint, lev_msg, *far_out = call(
        functools.partial(diffuse_kernel, n, levels),
        [(levels, rows, cols), (2 * rows + (16 if merged else 0), cols)] + [(24, cells)] * (n // 2 - 1),
        [ext, near_in, edge_in, surface, share_rows, msg, other, marine],
    )
    lev_in = lev_parts(lev_msg)
    far_in = [traded(x, 2 * i + 2, 1) for i, x in enumerate(far_out)]
    picks, tables = call(
        functools.partial(near_kernel, n, fold),
        [(3, 4, cells), jax.ShapeDtypeStruct((4, cells, cells), BF16)],
        [msg, other, near_in],
    )
    values, chip, *returns = call(
        functools.partial(slot_kernel, n, len(lev_in), rows),
        [(2 * n, cells), (40, cols)] + [(8, cols)] * n,
        [*lev_in, picks, tables, marine, marine_weight, *far_in],
        scratch=[pltpu.VMEM((3, 2 * n, cells), F32)] * 2
        + [pltpu.VMEM((2 * n, cells, cells), BF16)],
    )
    (slots,) = call(functools.partial(own_kernel, n), [(rows, cols)], [marine, values])
    if merged:
        theirs = traded(chip, 0, 1)
        first, second = call(
            merge_kernel, [(32, cols), (32, cols)], [values, *returns[1:], theirs]
        )
        first = by_core(first, (1, 0), (3, 0))
        second = by_core(second, (0, 1), (2, 0))
        gradient, sums = call(
            functools.partial(post_kernel, n),
            [(rows, cols), (rows + 8, cols)],
            [first, second, returns[0], slots, lev_in[1], theirs],
            scratch=[pltpu.VMEM((2 * n, cells), jnp.int32), pltpu.VMEM((2 * n, cells), F32)],
        )
    else:
        gradient = sum(lev_parts(slots))
        sums = returns[0]
        for step in range(1, n):
            sums = sums + traded(returns[step], step, 1)
    results = [(levels, rows, cols), (1, cells), (1, cells)]
    state, air_gradient, wind_gradient = call(
        functools.partial(final_kernel, merged),
        results,
        [gradient, adjoint, share_rows, sums, traded(sums, 0, 1)],
        out_specs=[HBM] * 3,
        scratch=[pltpu.VMEM(x, F32) for x in results] + [pltpu.SemaphoreType.DMA((3,))],
    )
    return (state, air_gradient.reshape(cells), wind_gradient.reshape(cells))


def solution(mesh):
    return jax.shard_map(
        per_device,
        mesh=mesh,
        in_specs=(
            P(("ens", "lev"), "sub", "tile"),
            P(("ens", "tile", "lev", "sub")),
            P(("ens", "tile", "lev", "sub")),
            P("lev"),
            P(("tile", "lev", "sub"), None, None),
            P(("tile", "lev", "sub"), None, None),
            P(("tile", "lev", "sub"), None, None),
            P(("tile", "lev", "sub"), None, None),
            P("sub", "tile"),
            P(("ens", "lev"), "sub", "tile"),
            P(("ens", "tile", "lev", "sub")),
        ),
        out_specs=(
            P(("ens", "lev"), "sub", "tile"),
            P(("ens", "tile", "lev", "sub")),
            P(("ens", "tile", "lev", "sub")),
        ),
        check_vma=False,
    )
```

```python
import functools

import jax
import jax.numpy as jnp
from jax import lax
from jax.experimental import pallas as pl
from jax.experimental.pallas import tpu as pltpu
from jax.sharding import PartitionSpec as P

BULK_ITERS = 3
STEPS = 3
HALO = STEPS
MIXING = 0.2
TRANSFER = 1.0
STABILITY = 0.5
F32 = jnp.float32
BF16 = jnp.bfloat16
VMEM = pl.BlockSpec(memory_space=pltpu.VMEM)
HBM = pl.BlockSpec(memory_space=pltpu.HBM)


def call(kernel, outs, operands, specs=None, out_specs=None, scratch=(), aliases=None):
    outs = [jax.ShapeDtypeStruct(x, F32) if isinstance(x, tuple) else x for x in outs]
    return pl.pallas_call(
        kernel,
        out_shape=outs,
        in_specs=specs or [VMEM] * len(operands),
        out_specs=out_specs or [VMEM] * len(outs),
        scratch_shapes=list(scratch),
        input_output_aliases=aliases or {},
        compiler_params=pltpu.CompilerParams(vmem_limit_bytes=24 * 1024 * 1024),
    )(*operands)


def halves(x):
    high = x.astype(BF16)
    low = (x - high.astype(F32)).astype(BF16)
    return high, low


def pack_kernel(n, *refs):
    warm, cot, sea, shares, sky, breeze, energy, sky_index, sky_weight, marine, marine_weight = refs[:11]
    msg, ext, surface, share_rows, marine_out, marine_weight_out = refs[11:17]
    warm_in, sea_in, shares_in, sky_in, breeze_in, energy_in, index_in, weight_in, sems = refs[17:]
    rows, cols = sea.shape
    levels = warm.shape[0]
    high = rows + 8
    pairs = [(cot.at[z], ext.at[pl.ds(high * z, rows)]) for z in range(levels)]
    pairs += [(sea, sea_in), (sky_index, index_in), (sky_weight, weight_in)]
    pairs += [(sky, sky_in), (breeze, breeze_in), (energy, energy_in)]
    pairs += [(shares, shares_in), (warm, warm_in)]
    pairs += [(marine, marine_out), (marine_weight, marine_weight_out)]
    copies = [pltpu.make_async_copy(a, b, sems.at[i]) for i, (a, b) in enumerate(pairs)]
    for copy in copies:
        copy.start()
    sub = lax.axis_index("sub")
    msg[...] = jnp.zeros_like(msg)
    for z in range(levels + 1):
        ext[high * z + rows : high * (z + 1), :] = jnp.zeros((8, cols), F32)
    for copy in copies:
        copy.wait()
    ext[high * levels : high * levels + rows, :] = sea_in[...].astype(F32)
    msg[0 : 2 * n, :] = index_in[...].astype(F32)
    msg[2 * n : 4 * n, :] = weight_in[...]
    for i, ref in enumerate((sky_in, breeze_in, energy_in)):
        msg[4 * n + i : 4 * n + i + 1, :] = ref[...]
    base = 4 * n + 8
    for i in range(levels + 1):
        at, top, left = high * i, base + HALO * (i // 2), cols * (i % 2)
        outer = jnp.where(sub == 0, ext[at + rows - HALO : at + rows], ext[at : at + HALO])
        msg[top : top + HALO, left : left + cols] = outer
    surface[...] = sum(shares_in[z] * warm_in[z] for z in range(levels))
    for z in range(levels):
        share_rows[z : z + 1, :] = jnp.full((1, cols), shares_in[z], F32)


def halo_rows(n, msg, i, cols):
    top, left = 4 * n + 8 + HALO * (i // 2), cols * (i % 2)
    return msg[top : top + HALO, left : left + cols]


def both_bands(msg, other, index, sub):
    own, far = msg[pl.ds(index, 1), :], other[pl.ds(index, 1), :]
    return [jnp.where(sub == 0, own, far), jnp.where(sub == 0, far, own)]


def table_rows(n, msg, other, target, band, sub):
    row = 2 * target + band
    return both_bands(msg, other, row, sub) + both_bands(msg, other, 2 * n + row, sub)


def value_rows(n, msg, other, sub):
    return [x for i in range(3) for x in both_bands(msg, other, 4 * n + i, sub)]


def write_pairs(out, at, rows):
    cols = out.shape[1]
    for i, row in enumerate(rows):
        out[at + i : at + i + 1, :] = row[:, :cols]
        out[at + len(rows) + i : at + len(rows) + i + 1, :] = row[:, cols:]


def write_halves(out, at, x):
    count, cols = x.shape[0], out.shape[1]
    out[at : at + count, :] = x[:, :cols]
    out[at + count : at + 2 * count, :] = x[:, cols:]


def read_halves(ref, at, count):
    return jnp.concatenate([ref[at : at + count, :], ref[at + count : at + 2 * count, :]], axis=1)


def read_pairs(ref, at, count):
    return [
        jnp.concatenate([ref[at + i : at + i + 1, :], ref[at + count + i : at + count + i + 1, :]], axis=1)
        for i in range(count)
    ]


def fold_place(cols):
    lane = lax.broadcasted_iota(jnp.int32, (8, cols), 1)
    return lax.rem(lane + HALO, cols)


def fold_slots(high, cols, fields):
    each = cols // (2 * HALO * fields)
    groups = high // 8
    return [(g // each, g % each) for g in range(groups)], -(-groups // each)


def folded(ext, high, fields):
    cols = ext.shape[1]
    place = fold_place(cols) // (2 * HALO)
    slots, tiles = fold_slots(high, cols, fields)
    out = [jnp.zeros((8, cols), F32)] * tiles
    for g, (k, at) in enumerate(slots):
        for i in range(fields):
            slot = at * fields + i
            rows = ext[high * i + 8 * g : high * i + 8 * g + 8, :]
            moved = pltpu.roll(rows, 2 * HALO * slot, 1) if slot else rows
            out[k] = jnp.where(place == slot, moved, out[k])
    return jnp.concatenate(out, axis=0)


def unfolded(tiles, i, high, fields):
    cols = tiles[0].shape[1]
    place = fold_place(cols)
    out = []
    for k, at in fold_slots(high, cols, fields)[0]:
        slot = at * fields + i
        moved = pltpu.roll(tiles[k], cols - 2 * HALO * slot, 1) if slot else tiles[k]
        out.append(jnp.where(place < 2 * HALO, moved, 0.0))
    return jnp.concatenate(out, axis=0)


def send_kernel(n, fields, msg, other, ext_in, ext, edge_out, near_out):
    sub, tile = lax.axis_index("sub"), lax.axis_index("tile")
    cols = ext.shape[1]
    high = ext.shape[0] // fields
    rows = high - 8
    for i in range(fields):
        base = high * i
        strip = halo_rows(n, other, i, cols)
        ext[base : base + rows, :] = ext_in[base : base + rows, :]
        ext[base + rows : base + high, :] = jnp.zeros((8, cols), F32)
        ext[base + rows : base + rows + HALO, :] = jnp.where(sub == 0, strip, 0.0)
        ext[base + high - HALO : base + high, :] = jnp.where(sub == 0, 0.0, strip)
    edges = folded(ext, high, fields)
    fold = edges.shape[0]
    edge_out[...] = edges
    near_out[0:fold, :] = edges
    near = tile ^ 1
    air = table_rows(n, msg, other, near, sub, sub) + value_rows(n, msg, other, sub)
    write_pairs(near_out, fold, air)
    at = fold + 20
    for step in range(2, n, 2):
        write_pairs(near_out, at, table_rows(n, msg, other, near ^ step, 1 - sub, sub))
        at += 8
    near_out[at : near_out.shape[0], :] = jnp.zeros((near_out.shape[0] - at, cols), F32)


def diffuse_kernel(n, levels, *refs):
    ext, near_in, edge_in, surface, share_rows, msg, other, marine, adjoint_out, lev_out = refs[:10]
    sub, tile = lax.axis_index("sub"), lax.axis_index("tile")
    rows, cols = surface.shape
    high = rows + 8
    fold = edge_in.shape[0]
    own_values = value_rows(n, msg, other, sub)
    near_values = read_pairs(near_in, fold, 10)[4:]
    for i, out in enumerate(refs[10:]):
        air = table_rows(n, msg, other, tile ^ (2 * i + 2), 1 - sub, sub) + own_values
        air += read_pairs(near_in, fold + 20 + 8 * i, 4) + near_values
        for at, row in enumerate(air):
            out[at : at + 1, :] = row
        out[20:24, :] = jnp.zeros((4, out.shape[1]), F32)
    even = tile % 2 == 0
    place = fold_place(cols)
    tiles = []
    for k in range(0, fold, 8):
        near, far = near_in[k : k + 8, :], edge_in[k : k + 8, :]
        right = jnp.where(tile < n - 1, jnp.where(even, near, far), 0.0)
        left = jnp.where(tile > 0, jnp.where(even, far, near), 0.0)
        tiles.append(jnp.where(lax.rem(place, 2 * HALO) >= HALO, right, left))

    def wide(i):
        return jnp.concatenate(
            [ext[high * i : high * (i + 1), :], unfolded(tiles, i, high, levels + 1)], axis=1
        )

    def around(x):
        return (
            pltpu.roll(x, 1, 0)
            + pltpu.roll(x, high - 1, 0)
            + pltpu.roll(x, 1, 1)
            + pltpu.roll(x, 2 * cols - 1, 1)
        )

    wet = wide(levels)
    keep = wet * (1.0 - MIXING * around(wet))
    mix = MIXING * wet
    own_wet = wet[:rows, :cols]
    heat = jnp.zeros((rows, cols), F32)
    for z in range(levels):
        v = wet * wide(z)
        for sweep_index in range(STEPS):
            v = keep * v + mix * around(v)
        adjoint = own_wet * v[:rows, :cols]
        adjoint_out[z] = adjoint
        heat += share_rows[z : z + 1, :] * adjoint
    lev_out[0:rows, :] = surface[...]
    lev_out[rows : 2 * rows, :] = own_wet * heat
    if lev_out.shape[0] > 2 * rows:
        write_halves(lev_out, 2 * rows, marine[...].astype(F32))


def bulk_adjoint(warmth_gap, flux_sens):
    transfer_rate = jnp.full_like(warmth_gap, TRANSFER)
    rates = [transfer_rate]
    slopes = []
    for sweep_index in range(BULK_ITERS):
        bent = jnp.tanh(transfer_rate * warmth_gap)
        slopes.append(TRANSFER * STABILITY * (1.0 - bent * bent))
        transfer_rate = TRANSFER * (1.0 + STABILITY * bent)
        rates.append(transfer_rate)
    contrast_sens = transfer_rate * flux_sens
    rate_sens = warmth_gap * flux_sens
    for sweep_index in reversed(range(BULK_ITERS)):
        inner_sens = rate_sens * slopes[sweep_index]
        contrast_sens = contrast_sens + inner_sens * rates[sweep_index]
        rate_sens = inner_sens * warmth_gap
    return contrast_sens


def onehot(index, count):
    cells = lax.broadcasted_iota(jnp.int32, (count, index.shape[1]), 0)
    return jnp.where(cells == index, 1.0, 0.0).astype(BF16)


def dot(a, b, ca, cb):
    return lax.dot_general(a, b, (((ca,), (cb,)), ((), ())), preferred_element_type=F32)


def look_up(air, at, picks, tables):
    for band in range(2):
        hot = onehot(air[band].astype(jnp.int32), air[band].shape[1])
        tables[at + band] = hot
        values = jnp.concatenate([air[4 + band], air[6 + band], air[8 + band]], axis=0)
        found = dot(jnp.concatenate(halves(values), axis=0), hot, 1, 0)
        found = found[0:3] + found[3:6]
        picks[0, at + band : at + band + 1, :] = found[0:1]
        picks[1, at + band : at + band + 1, :] = found[1:2]
        picks[2, at + band : at + band + 1, :] = air[2 + band] * found[2:3]


def near_kernel(n, fold, msg, other, near_in, picks, tables):
    sub, tile = lax.axis_index("sub"), lax.axis_index("tile")
    own = table_rows(n, msg, other, tile, sub, sub) + value_rows(n, msg, other, sub)
    look_up(own, 0, picks, tables)
    look_up(read_pairs(near_in, fold, 10), 2, picks, tables)


def slot_kernel(n, count, rows, *refs):
    lev_parts, refs = refs[:count], refs[count:]
    near_picks, near_tables, marine, weight = refs[:4]
    far_in, refs = refs[4 : 3 + n // 2], refs[3 + n // 2 :]
    values_out, chip_out, returns = refs[0], refs[1], refs[2 : 2 + n]
    held, picks, tables = refs[2 + n :]
    sub, tile = lax.axis_index("sub"), lax.axis_index("tile")
    cols = chip_out.shape[1]
    picks[:, 0:4, :] = near_picks[...]
    for i, ref in enumerate(far_in):
        for j in range(2):
            air = [ref[10 * j + k : 10 * j + k + 1, :] for k in range(10)]
            look_up(air, 4 * i + 4 + 2 * j, picks, tables)
    table = sum(ref[0 : 2 * rows, :] for ref in lev_parts)
    table = jnp.concatenate(halves(table), axis=1)
    for step in range(n):
        for band in range(2):
            at, place = 2 * step + band, 2 * (tile ^ step) + band
            cell = marine[pl.ds(place, 1), :]
            row, col = cell // cols, lax.rem(cell, cols)
            col_hot = onehot(col, cols)
            spread = dot(table, jnp.concatenate([col_hot, col_hot], axis=0), 1, 0)
            row_mask = lax.broadcasted_iota(jnp.int32, (rows, cell.shape[1]), 0) == row
            for i in range(2):
                piece = jnp.where(row_mask, spread[rows * i : rows * (i + 1)], 0.0)
                held[i, at : at + 1, :] = jnp.sum(piece, axis=0, keepdims=True)
            held[2, at : at + 1, :] = weight[pl.ds(place, 1), :]

    difference = held[0] - picks[0]
    wind = picks[1]
    flux_sens = held[2] * held[1] + picks[2]
    contrast_sens = bulk_adjoint(wind * difference, flux_sens)
    surface_sens = contrast_sens * wind
    wind_sens = contrast_sens * difference
    values_out[...] = surface_sens
    for step in range(n):
        for band in range(2):
            at = 2 * step + band
            hot = near_tables[at] if at < 4 else tables[at]
            values = jnp.concatenate([surface_sens[at : at + 1], wind_sens[at : at + 1]], axis=0)
            sums = dot(jnp.concatenate(halves(values), axis=0), hot, 1, 1)
            sums = sums[0:2] + sums[2:4]
            returns[step][2 * band : 2 * band + 2, :] = sums[:, :cols]
            returns[step][2 * band + 4 : 2 * band + 6, :] = sums[:, cols:]
    if n == 4:
        chip_out[0:8, :] = jnp.where(sub == 0, returns[2][...], returns[1][...])
        write_halves(chip_out, 8, surface_sens)
        chip_out[8:16, :] = jnp.where(sub == 0, returns[3][...], chip_out[8:16, :])
        chip_out[24:40, :] = lev_parts[-1][2 * rows : 2 * rows + 16, :]


def scatter(n, rows, cols, tile, cell_of, value_of):
    total = jnp.zeros((2 * rows, cols), F32)
    for step in range(n):
        for band in range(2):
            cell = cell_of(2 * (tile ^ step) + band)
            row, col = cell // cols, lax.rem(cell, cols)
            row_mask = lax.broadcasted_iota(jnp.int32, (rows, cell.shape[1]), 0) == row
            spread = jnp.concatenate(
                [
                    jnp.where(row_mask, x.astype(F32), 0.0).astype(BF16)
                    for x in halves(value_of(2 * step + band))
                ],
                axis=0,
            )
            total += dot(spread, onehot(col, cols), 1, 1)
    return total[:rows] + total[rows:]


def own_kernel(n, marine, values, out):
    tile = lax.axis_index("tile")
    rows, cols = out.shape
    out[...] = scatter(
        n, rows, cols, tile, lambda i: marine[pl.ds(i, 1), :], lambda i: values[i : i + 1, :]
    )


def post_kernel(n, first, second, own, slots, lev_in, theirs, gradient, out, cells, values):
    even = lax.axis_index("sub") == 0
    tile = lax.axis_index("tile")
    rows, cols = gradient.shape
    out[0:8, :] = first[0:8, :] + own[...] + jnp.where(even, 0.0, second[0:8, :])

    @pl.when(even)
    def _():
        for band, (ref, at) in enumerate(((lev_in, 2 * rows), (theirs, 24))):
            cells[...] = read_halves(ref, at, 2 * n).astype(jnp.int32)
            values[...] = read_halves(second, 4 * n * band, 2 * n)
            total = scatter(
                n, rows, cols, tile, lambda i: cells[pl.ds(i, 1), :], lambda i: values[i : i + 1, :]
            )
            if band == 0:
                gradient[...] = slots[...] + total
            else:
                out[8 : rows + 8, :] = total

    @pl.when(jnp.logical_not(even))
    def _():
        gradient[...] = slots[...]
        out[8 : rows + 8, :] = jnp.zeros_like(slots)


def merge_kernel(values, near, two, three, theirs, first, second):
    even = lax.axis_index("sub") == 0
    first[...] = jnp.zeros_like(first)
    first[0:8, :] = jnp.where(even, near[...] + theirs[0:8, :], three[...] + theirs[8:16, :])
    write_halves(second, 0, values[...])
    second[0:8, :] = jnp.where(even, second[0:8, :], two[...] + theirs[0:8, :])
    second[16:32, :] = theirs[8:24, :]


def final_kernel(merged, slots, adjoint, share_rows, sums, other, *refs):
    state_out, air_out, wind_out, state, air, wind, sems = refs
    sub = lax.axis_index("sub")
    gradient = slots[...]
    if merged:
        gradient += jnp.where(sub == 0, 0.0, other[8 : slots.shape[0] + 8, :])
    for z in range(adjoint.shape[0]):
        state[z] = adjoint[z] + share_rows[z : z + 1, :] * gradient
    copies = [pltpu.make_async_copy(state, state_out, sems.at[0])]
    copies[0].start()
    both = sums[0:8, :] + other[0:8, :]
    own = [jnp.where(sub == 0, both[i : i + 2], both[i + 2 : i + 4]) for i in (0, 4)]
    own = jnp.concatenate(own, axis=1)
    air[...] = -own[0:1]
    wind[...] = own[1:2]
    for i, (a, b) in enumerate(((air, air_out), (wind, wind_out))):
        copies.append(pltpu.make_async_copy(a, b, sems.at[1 + i]))
        copies[-1].start()
    for copy in copies:
        copy.wait()


def traded(x, step, swap=0):
    n, bands = lax.axis_size("tile"), lax.axis_size("sub")
    pairs = [
        (t * bands + s, (t ^ step) * bands + (s ^ swap)) for t in range(n) for s in range(bands)
    ]
    return lax.ppermute(x, ("tile", "sub"), pairs)


def beyond(x):
    n, levs, bands = (lax.axis_size(axis) for axis in ("tile", "lev", "sub"))

    def place(t, l, s):
        return (t * levs + l) * bands + s

    pairs = []
    for l in range(levs):
        for s in range(bands):
            for t in range(1, n - 1, 2):
                pairs += [(place(t, l, s), place(t + 1, l, s)), (place(t + 1, l, s), place(t, l, s))]
            pairs += [(place(t, l, s), place(t, l ^ 1, s ^ 1)) for t in (0, n - 1)]
    return lax.ppermute(x, ("tile", "lev", "sub"), pairs)


def by_core(x, even, odd):
    n, levs, bands = (lax.axis_size(axis) for axis in ("tile", "lev", "sub"))
    pairs = []
    for t in range(n):
        for l in range(levs):
            for s in range(bands):
                tx, lx = odd if s else even
                pairs.append(((t * levs + l) * bands + s, ((t ^ tx) * levs + (l ^ lx)) * bands + s))
    return lax.ppermute(x, ("tile", "lev", "sub"), pairs)


def lev_parts(x):
    if lax.axis_size("lev") == 2:
        return [x, lax.ppermute(x, "lev", [(0, 1), (1, 0)])]
    return [lax.psum(x, "lev")]


def per_device(
    marine_layered_warmth,
    bottom_sky_warmth,
    bottom_breeze_magnitude,
    depth_shares,
    piece_sky_box,
    sky_share_fraction,
    piece_marine_box,
    marine_share_fraction,
    marine_indicator,
    marine_result_adjoint,
    energy_transport_adjoint,
):
    n, levs = lax.axis_size("tile"), lax.axis_size("lev")
    levels, rows, cols = marine_layered_warmth.shape
    cells = bottom_sky_warmth.shape[0]
    high = rows + 8
    raw = [marine_layered_warmth, marine_result_adjoint, marine_indicator, depth_shares]
    raw += [
        x.reshape(1, cells)
        for x in (bottom_sky_warmth, bottom_breeze_magnitude, energy_transport_adjoint)
    ]
    raw += [piece_sky_box[0], sky_share_fraction[0], piece_marine_box[0], marine_share_fraction[0]]
    raw = [pltpu.with_memory_space_constraint(x, pltpu.HBM) for x in raw]
    held = [pltpu.VMEM(x.shape, x.dtype) for x in [raw[0], raw[2]]]
    held += [pltpu.SMEM(depth_shares.shape, F32)]
    held += [pltpu.VMEM(x.shape, x.dtype) for x in raw[4:9]]
    msg, ext, surface, share_rows, marine, marine_weight = call(
        functools.partial(pack_kernel, n),
        [(4 * n + 16, cells), ((levels + 1) * high, cols), (rows, cols), (8, cols)]
        + [jax.ShapeDtypeStruct(x.shape, x.dtype) for x in raw[9:]],
        raw,
        [HBM] * len(raw),
        scratch=held + [pltpu.SemaphoreType.DMA((10 + levels,))],
    )
    other = traded(msg, 0, 1)
    fold = 8 * fold_slots(high, cols, levels + 1)[1]
    ext, edge_out, near_out = call(
        functools.partial(send_kernel, n, levels + 1),
        [ext.shape, (fold, cols), ((fold + 20 + 4 * (n - 2) + 7) // 8 * 8, cols)],
        [msg, other, ext],
    )
    edge_in = beyond(edge_out)
    near_in = traded(near_out, 1)
    merged = n == 4 and levs == 2
    adjoint, lev_msg, *far_out = call(
        functools.partial(diffuse_kernel, n, levels),
        [(levels, rows, cols), (2 * rows + (16 if merged else 0), cols)] + [(24, cells)] * (n // 2 - 1),
        [ext, near_in, edge_in, surface, share_rows, msg, other, marine],
    )
    lev_in = lev_parts(lev_msg)
    far_in = [traded(x, 2 * i + 2, 1) for i, x in enumerate(far_out)]
    picks, tables = call(
        functools.partial(near_kernel, n, fold),
        [(3, 4, cells), jax.ShapeDtypeStruct((4, cells, cells), BF16)],
        [msg, other, near_in],
    )
    values, chip, *returns = call(
        functools.partial(slot_kernel, n, len(lev_in), rows),
        [(2 * n, cells), (40, cols)] + [(8, cols)] * n,
        [*lev_in, picks, tables, marine, marine_weight, *far_in],
        scratch=[pltpu.VMEM((3, 2 * n, cells), F32)] * 2
        + [pltpu.VMEM((2 * n, cells, cells), BF16)],
    )
    (slots,) = call(functools.partial(own_kernel, n), [(rows, cols)], [marine, values])
    if merged:
        theirs = traded(chip, 0, 1)
        first, second = call(
            merge_kernel, [(32, cols), (32, cols)], [values, *returns[1:], theirs]
        )
        first = by_core(first, (1, 0), (3, 0))
        second = by_core(second, (0, 1), (2, 0))
        gradient, sums = call(
            functools.partial(post_kernel, n),
            [(rows, cols), (rows + 8, cols)],
            [first, second, returns[0], slots, lev_in[1], theirs],
            scratch=[pltpu.VMEM((2 * n, cells), jnp.int32), pltpu.VMEM((2 * n, cells), F32)],
        )
    else:
        gradient = sum(lev_parts(slots))
        sums = returns[0]
        for step in range(1, n):
            sums = sums + traded(returns[step], step, 1)
    results = [(levels, rows, cols), (1, cells), (1, cells)]
    state, air_gradient, wind_gradient = call(
        functools.partial(final_kernel, merged),
        results,
        [gradient, adjoint, share_rows, sums, traded(sums, 0, 1)],
        out_specs=[HBM] * 3,
        scratch=[pltpu.VMEM(x, F32) for x in results] + [pltpu.SemaphoreType.DMA((3,))],
    )
    return (state, air_gradient.reshape(cells), wind_gradient.reshape(cells))


def solution(mesh):
    return jax.shard_map(
        per_device,
        mesh=mesh,
        in_specs=(
            P(("ens", "lev"), "sub", "tile"),
            P(("ens", "tile", "lev", "sub")),
            P(("ens", "tile", "lev", "sub")),
            P("lev"),
            P(("tile", "lev", "sub"), None, None),
            P(("tile", "lev", "sub"), None, None),
            P(("tile", "lev", "sub"), None, None),
            P(("tile", "lev", "sub"), None, None),
            P("sub", "tile"),
            P(("ens", "lev"), "sub", "tile"),
            P(("ens", "tile", "lev", "sub")),
        ),
        out_specs=(
            P(("ens", "lev"), "sub", "tile"),
            P(("ens", "tile", "lev", "sub")),
            P(("ens", "tile", "lev", "sub")),
        ),
        check_vma=False,
    )
```

```python
import functools

import jax
import jax.numpy as jnp
from jax import lax
from jax.experimental import pallas as pl
from jax.experimental.pallas import tpu as pltpu
from jax.sharding import PartitionSpec as P

BULK_ITERS = 3
STEPS = 3
HALO = STEPS
MIXING = 0.2
TRANSFER = 1.0
STABILITY = 0.5
F32 = jnp.float32
BF16 = jnp.bfloat16
VMEM = pl.BlockSpec(memory_space=pltpu.VMEM)
HBM = pl.BlockSpec(memory_space=pltpu.HBM)


def call(kernel, outs, operands, specs=None, out_specs=None, scratch=(), aliases=None):
    outs = [jax.ShapeDtypeStruct(x, F32) if isinstance(x, tuple) else x for x in outs]
    return pl.pallas_call(
        kernel,
        out_shape=outs,
        in_specs=specs or [VMEM] * len(operands),
        out_specs=out_specs or [VMEM] * len(outs),
        scratch_shapes=list(scratch),
        input_output_aliases=aliases or {},
        compiler_params=pltpu.CompilerParams(vmem_limit_bytes=24 * 1024 * 1024),
    )(*operands)


def halves(x):
    high = x.astype(BF16)
    low = (x - high.astype(F32)).astype(BF16)
    return high, low


def fold_place(cols):
    lane = lax.broadcasted_iota(jnp.int32, (8, cols), 1)
    return lax.rem(lane + HALO, cols)


def fold_slots(high, cols, fields):
    each = cols // (2 * HALO * fields)
    groups = high // 8
    return [(g // each, g % each) for g in range(groups)], -(-groups // each)


def folded(ext, high, fields):
    cols = ext.shape[1]
    place = fold_place(cols) // (2 * HALO)
    slots, tiles = fold_slots(high, cols, fields)
    out = [jnp.zeros((8, cols), F32)] * tiles
    for g, (k, at) in enumerate(slots):
        for i in range(fields):
            slot = at * fields + i
            rows = ext[high * i + 8 * g : high * i + 8 * g + 8, :]
            moved = pltpu.roll(rows, 2 * HALO * slot, 1) if slot else rows
            out[k] = jnp.where(place == slot, moved, out[k])
    return jnp.concatenate(out, axis=0)


def unfolded(tiles, i, high, fields):
    cols = tiles[0].shape[1]
    place = fold_place(cols)
    out = []
    for k, at in fold_slots(high, cols, fields)[0]:
        slot = at * fields + i
        moved = pltpu.roll(tiles[k], cols - 2 * HALO * slot, 1) if slot else tiles[k]
        out.append(jnp.where(place < 2 * HALO, moved, 0.0))
    return jnp.concatenate(out, axis=0)


def pack_kernel(n, *refs):
    warm, cot, sea, shares, sky, breeze, energy, sky_index, sky_weight, marine, marine_weight = refs[:11]
    msg, ext, surface, share_rows, marine_out, marine_weight_out = refs[11:17]
    warm_in, sea_in, shares_in, sky_in, breeze_in, energy_in, index_in, weight_in, sems = refs[17:]
    rows, cols = sea.shape
    levels = warm.shape[0]
    high = rows + 8
    pairs = [(cot.at[z], ext.at[pl.ds(high * z, rows)]) for z in range(levels)]
    pairs += [(sea, sea_in), (sky_index, index_in), (sky_weight, weight_in)]
    pairs += [(sky, sky_in), (breeze, breeze_in), (energy, energy_in)]
    pairs += [(shares, shares_in), (warm, warm_in)]
    pairs += [(marine, marine_out), (marine_weight, marine_weight_out)]
    copies = [pltpu.make_async_copy(a, b, sems.at[i]) for i, (a, b) in enumerate(pairs)]
    for copy in copies:
        copy.start()
    sub = lax.axis_index("sub")
    msg[...] = jnp.zeros_like(msg)
    for z in range(levels + 1):
        ext[high * z + rows : high * (z + 1), :] = jnp.zeros((8, cols), F32)
    for copy in copies:
        copy.wait()
    ext[high * levels : high * levels + rows, :] = sea_in[...].astype(F32)
    msg[0 : 2 * n, :] = index_in[...].astype(F32)
    msg[2 * n : 4 * n, :] = weight_in[...]
    for i, ref in enumerate((sky_in, breeze_in, energy_in)):
        msg[4 * n + i : 4 * n + i + 1, :] = ref[...]
    base = 4 * n + 8
    for i in range(levels + 1):
        at, top, left = high * i, base + HALO * (i // 2), cols * (i % 2)
        outer = jnp.where(sub == 0, ext[at + rows - HALO : at + rows], ext[at : at + HALO])
        msg[top : top + HALO, left : left + cols] = outer
    edges = folded(ext, high, levels + 1)
    for k in range(2):
        msg[4 * n + 16 : 4 * n + 24, cols * k : cols * (k + 1)] = edges[8 * k : 8 * k + 8]
    surface[...] = sum(shares_in[z] * warm_in[z] for z in range(levels))
    for z in range(levels):
        share_rows[z : z + 1, :] = jnp.full((1, cols), shares_in[z], F32)


def halo_rows(n, msg, i, cols):
    top, left = 4 * n + 8 + HALO * (i // 2), cols * (i % 2)
    return msg[top : top + HALO, left : left + cols]


def both_bands(msg, other, index, sub):
    own, far = msg[pl.ds(index, 1), :], other[pl.ds(index, 1), :]
    return [jnp.where(sub == 0, own, far), jnp.where(sub == 0, far, own)]


def table_rows(n, msg, other, target, band, sub):
    row = 2 * target + band
    return both_bands(msg, other, row, sub) + both_bands(msg, other, 2 * n + row, sub)


def value_rows(n, msg, other, sub):
    return [x for i in range(3) for x in both_bands(msg, other, 4 * n + i, sub)]


def write_pairs(out, at, rows):
    cols = out.shape[1]
    for i, row in enumerate(rows):
        out[at + i : at + i + 1, :] = row[:, :cols]
        out[at + len(rows) + i : at + len(rows) + i + 1, :] = row[:, cols:]


def write_halves(out, at, x):
    count, cols = x.shape[0], out.shape[1]
    out[at : at + count, :] = x[:, :cols]
    out[at + count : at + 2 * count, :] = x[:, cols:]


def read_halves(ref, at, count):
    return jnp.concatenate([ref[at : at + count, :], ref[at + count : at + 2 * count, :]], axis=1)


def read_pairs(ref, at, count):
    return [
        jnp.concatenate([ref[at + i : at + i + 1, :], ref[at + count + i : at + count + i + 1, :]], axis=1)
        for i in range(count)
    ]


def send_kernel(n, fields, msg, other, ext_in, ext, edge_out, near_out):
    sub, tile = lax.axis_index("sub"), lax.axis_index("tile")
    cols = ext.shape[1]
    high = ext.shape[0] // fields
    rows = high - 8
    for i in range(fields):
        base = high * i
        strip = halo_rows(n, other, i, cols)
        ext[base : base + rows, :] = ext_in[base : base + rows, :]
        ext[base + rows : base + high, :] = jnp.zeros((8, cols), F32)
        ext[base + rows : base + rows + HALO, :] = jnp.where(sub == 0, strip, 0.0)
        ext[base + high - HALO : base + high, :] = jnp.where(sub == 0, 0.0, strip)
    slots, count = fold_slots(high, cols, fields)
    tile_at, at = slots[-1]
    place = fold_place(cols) // (2 * HALO)
    tiles = [other[4 * n + 16 : 4 * n + 24, cols * k : cols * (k + 1)] for k in range(count)]
    for i in range(fields):
        strip = halo_rows(n, msg, i, cols)
        blank = jnp.zeros((8 - 2 * HALO, cols), F32)
        rows_beyond = [jnp.where(sub == 1, strip, 0.0), blank, jnp.where(sub == 1, 0.0, strip)]
        slot = at * fields + i
        moved = pltpu.roll(jnp.concatenate(rows_beyond, axis=0), 2 * HALO * slot, 1)
        tiles[tile_at] = jnp.where(place == slot, moved, tiles[tile_at])
    edges = jnp.concatenate(tiles, axis=0)
    fold = edges.shape[0]
    edge_out[...] = edges
    near_out[0:fold, :] = edges
    near = tile ^ 1
    air = table_rows(n, msg, other, near, 1 - sub, sub) + value_rows(n, msg, other, sub)
    write_pairs(near_out, fold, air)
    at = fold + 20
    for step in range(2, n, 2):
        write_pairs(near_out, at, table_rows(n, msg, other, near ^ step, sub, sub))
        at += 8
    near_out[at : near_out.shape[0], :] = jnp.zeros((near_out.shape[0] - at, cols), F32)


def diffuse_kernel(n, levels, *refs):
    ext, near_in, edge_in, surface, share_rows, msg, other, marine, adjoint_out, lev_out = refs[:10]
    sub, tile = lax.axis_index("sub"), lax.axis_index("tile")
    rows, cols = surface.shape
    high = rows + 8
    fold = edge_in.shape[0]
    own_values = value_rows(n, msg, other, sub)
    near_values = read_pairs(near_in, fold, 10)[4:]
    for i, out in enumerate(refs[10:]):
        air = table_rows(n, msg, other, tile ^ (2 * i + 2), 1 - sub, sub) + own_values
        air += read_pairs(near_in, fold + 20 + 8 * i, 4) + near_values
        write_pairs(out, 0, air)
    even = tile % 2 == 0
    place = fold_place(cols)
    tiles = []
    for k in range(0, fold, 8):
        near, far = near_in[k : k + 8, :], edge_in[k : k + 8, :]
        right = jnp.where(tile < n - 1, jnp.where(even, near, far), 0.0)
        left = jnp.where(tile > 0, jnp.where(even, far, near), 0.0)
        tiles.append(jnp.where(lax.rem(place, 2 * HALO) >= HALO, right, left))

    def wide(i):
        return jnp.concatenate(
            [ext[high * i : high * (i + 1), :], unfolded(tiles, i, high, levels + 1)], axis=1
        )

    def around(x):
        return (
            pltpu.roll(x, 1, 0)
            + pltpu.roll(x, high - 1, 0)
            + pltpu.roll(x, 1, 1)
            + pltpu.roll(x, 2 * cols - 1, 1)
        )

    wet = wide(levels)
    keep = wet * (1.0 - MIXING * around(wet))
    mix = MIXING * wet
    own_wet = wet[:rows, :cols]
    heat = jnp.zeros((rows, cols), F32)
    for z in range(levels):
        v = wet * wide(z)
        for sweep_index in range(STEPS):
            v = keep * v + mix * around(v)
        adjoint = own_wet * v[:rows, :cols]
        adjoint_out[z] = adjoint
        heat += share_rows[z : z + 1, :] * adjoint
    lev_out[0:rows, :] = surface[...]
    lev_out[rows : 2 * rows, :] = own_wet * heat
    if lev_out.shape[0] > 2 * rows:
        write_halves(lev_out, 2 * rows, marine[...].astype(F32))


def bulk_adjoint(warmth_gap, flux_sens):
    transfer_rate = jnp.full_like(warmth_gap, TRANSFER)
    rates = [transfer_rate]
    slopes = []
    for sweep_index in range(BULK_ITERS):
        bent = jnp.tanh(transfer_rate * warmth_gap)
        slopes.append(TRANSFER * STABILITY * (1.0 - bent * bent))
        transfer_rate = TRANSFER * (1.0 + STABILITY * bent)
        rates.append(transfer_rate)
    contrast_sens = transfer_rate * flux_sens
    rate_sens = warmth_gap * flux_sens
    for sweep_index in reversed(range(BULK_ITERS)):
        inner_sens = rate_sens * slopes[sweep_index]
        contrast_sens = contrast_sens + inner_sens * rates[sweep_index]
        rate_sens = inner_sens * warmth_gap
    return contrast_sens


def onehot(index, count):
    cells = lax.broadcasted_iota(jnp.int32, (count, index.shape[1]), 0)
    return jnp.where(cells == index, 1.0, 0.0).astype(BF16)


def dot(a, b, ca, cb):
    return lax.dot_general(a, b, (((ca,), (cb,)), ((), ())), preferred_element_type=F32)


def look_up(air, at, picks, tables):
    for band in range(2):
        hot = onehot(air[band].astype(jnp.int32), air[band].shape[1])
        tables[at + band] = hot
        values = jnp.concatenate([air[4 + band], air[6 + band], air[8 + band]], axis=0)
        found = dot(jnp.concatenate(halves(values), axis=0), hot, 1, 0)
        found = found[0:3] + found[3:6]
        picks[0, at + band : at + band + 1, :] = found[0:1]
        picks[1, at + band : at + band + 1, :] = found[1:2]
        picks[2, at + band : at + band + 1, :] = air[2 + band] * found[2:3]


def near_kernel(n, fold, msg, other, near_in, picks, tables):
    sub, tile = lax.axis_index("sub"), lax.axis_index("tile")
    own = table_rows(n, msg, other, tile, sub, sub) + value_rows(n, msg, other, sub)
    look_up(own, 0, picks, tables)
    look_up(read_pairs(near_in, fold, 10), 2, picks, tables)


def slot_kernel(n, count, rows, *refs):
    lev_parts, refs = refs[:count], refs[count:]
    near_picks, near_tables, marine, weight = refs[:4]
    far_in, refs = refs[4 : 3 + n // 2], refs[3 + n // 2 :]
    values_out, chip_out, returns = refs[0], refs[1], refs[2 : 2 + n]
    held, picks, tables = refs[2 + n :]
    sub, tile = lax.axis_index("sub"), lax.axis_index("tile")
    cols = chip_out.shape[1]
    picks[:, 0:4, :] = near_picks[...]
    for i, ref in enumerate(far_in):
        air = read_pairs(ref, 0, 20)
        for j in range(2):
            look_up(air[10 * j : 10 * j + 10], 4 * i + 4 + 2 * j, picks, tables)
    table = sum(ref[0 : 2 * rows, :] for ref in lev_parts)
    table = jnp.concatenate(halves(table), axis=1)
    for step in range(n):
        for band in range(2):
            at, place = 2 * step + band, 2 * (tile ^ step) + band
            cell = marine[pl.ds(place, 1), :]
            row, col = cell // cols, lax.rem(cell, cols)
            col_hot = onehot(col, cols)
            spread = dot(table, jnp.concatenate([col_hot, col_hot], axis=0), 1, 0)
            row_mask = lax.broadcasted_iota(jnp.int32, (rows, cell.shape[1]), 0) == row
            for i in range(2):
                piece = jnp.where(row_mask, spread[rows * i : rows * (i + 1)], 0.0)
                held[i, at : at + 1, :] = jnp.sum(piece, axis=0, keepdims=True)
            held[2, at : at + 1, :] = weight[pl.ds(place, 1), :]

    difference = held[0] - picks[0]
    wind = picks[1]
    flux_sens = held[2] * held[1] + picks[2]
    contrast_sens = bulk_adjoint(wind * difference, flux_sens)
    surface_sens = contrast_sens * wind
    wind_sens = contrast_sens * difference
    values_out[...] = surface_sens
    for step in range(n):
        for band in range(2):
            at = 2 * step + band
            hot = near_tables[at] if at < 4 else tables[at]
            values = jnp.concatenate([surface_sens[at : at + 1], wind_sens[at : at + 1]], axis=0)
            sums = dot(jnp.concatenate(halves(values), axis=0), hot, 1, 1)
            sums = sums[0:2] + sums[2:4]
            returns[step][2 * band : 2 * band + 2, :] = sums[:, :cols]
            returns[step][2 * band + 4 : 2 * band + 6, :] = sums[:, cols:]
    if n == 4:
        chip_out[0:8, :] = jnp.where(sub == 0, returns[2][...], returns[1][...])
        write_halves(chip_out, 8, surface_sens)
        chip_out[8:16, :] = jnp.where(sub == 0, returns[3][...], chip_out[8:16, :])
        chip_out[24:40, :] = lev_parts[-1][2 * rows : 2 * rows + 16, :]


def scatter(n, rows, cols, tile, cell_of, value_of):
    total = jnp.zeros((2 * rows, cols), F32)
    for step in range(n):
        for band in range(2):
            cell = cell_of(2 * (tile ^ step) + band)
            row, col = cell // cols, lax.rem(cell, cols)
            row_mask = lax.broadcasted_iota(jnp.int32, (rows, cell.shape[1]), 0) == row
            spread = jnp.concatenate(
                [
                    jnp.where(row_mask, x.astype(F32), 0.0).astype(BF16)
                    for x in halves(value_of(2 * step + band))
                ],
                axis=0,
            )
            total += dot(spread, onehot(col, cols), 1, 1)
    return total[:rows] + total[rows:]


def own_kernel(n, marine, values, out):
    tile = lax.axis_index("tile")
    rows, cols = out.shape
    out[...] = scatter(
        n, rows, cols, tile, lambda i: marine[pl.ds(i, 1), :], lambda i: values[i : i + 1, :]
    )


def post_kernel(n, first, second, own, slots, lev_in, theirs, gradient, out, cells, values):
    even = lax.axis_index("sub") == 0
    tile = lax.axis_index("tile")
    rows, cols = gradient.shape
    out[0:8, :] = first[0:8, :] + own[...] + jnp.where(even, 0.0, second[0:8, :])

    @pl.when(even)
    def _():
        for band, (ref, at) in enumerate(((lev_in, 2 * rows), (theirs, 24))):
            cells[...] = read_halves(ref, at, 2 * n).astype(jnp.int32)
            values[...] = read_halves(second, 4 * n * band, 2 * n)
            total = scatter(
                n, rows, cols, tile, lambda i: cells[pl.ds(i, 1), :], lambda i: values[i : i + 1, :]
            )
            if band == 0:
                gradient[...] = slots[...] + total
            else:
                out[8 : rows + 8, :] = total

    @pl.when(jnp.logical_not(even))
    def _():
        gradient[...] = slots[...]
        out[8 : rows + 8, :] = jnp.zeros_like(slots)


def merge_kernel(values, near, two, three, theirs, first, second):
    even = lax.axis_index("sub") == 0
    first[...] = jnp.zeros_like(first)
    first[0:8, :] = jnp.where(even, near[...] + theirs[0:8, :], three[...] + theirs[8:16, :])
    write_halves(second, 0, values[...])
    second[0:8, :] = jnp.where(even, second[0:8, :], two[...] + theirs[0:8, :])
    second[16:32, :] = theirs[8:24, :]


def final_kernel(merged, slots, adjoint, share_rows, sums, other, *refs):
    state_out, air_out, wind_out, state, air, wind, sems = refs
    sub = lax.axis_index("sub")
    gradient = slots[...]
    if merged:
        gradient += jnp.where(sub == 0, 0.0, other[8 : slots.shape[0] + 8, :])
    for z in range(adjoint.shape[0]):
        state[z] = adjoint[z] + share_rows[z : z + 1, :] * gradient
    copies = [pltpu.make_async_copy(state, state_out, sems.at[0])]
    copies[0].start()
    both = sums[0:8, :] + other[0:8, :]
    own = [jnp.where(sub == 0, both[i : i + 2], both[i + 2 : i + 4]) for i in (0, 4)]
    own = jnp.concatenate(own, axis=1)
    air[...] = -own[0:1]
    wind[...] = own[1:2]
    for i, (a, b) in enumerate(((air, air_out), (wind, wind_out))):
        copies.append(pltpu.make_async_copy(a, b, sems.at[1 + i]))
        copies[-1].start()
    for copy in copies:
        copy.wait()


def traded(x, step, swap=0):
    n, bands = lax.axis_size("tile"), lax.axis_size("sub")
    pairs = [
        (t * bands + s, (t ^ step) * bands + (s ^ swap)) for t in range(n) for s in range(bands)
    ]
    return lax.ppermute(x, ("tile", "sub"), pairs)


def beyond(x):
    n, bands = lax.axis_size("tile"), lax.axis_size("sub")
    pairs = []
    for t in range(n):
        to = t if t in (0, n - 1) else ((t + 1) ^ 1) - 1
        pairs += [(t * bands + s, to * bands + (s ^ 1)) for s in range(bands)]
    return lax.ppermute(x, ("tile", "sub"), pairs)


def by_core(x, even, odd):
    n, levs, bands = (lax.axis_size(axis) for axis in ("tile", "lev", "sub"))
    pairs = []
    for t in range(n):
        for l in range(levs):
            for s in range(bands):
                tx, lx = odd if s else even
                pairs.append(((t * levs + l) * bands + s, ((t ^ tx) * levs + (l ^ lx)) * bands + s))
    return lax.ppermute(x, ("tile", "lev", "sub"), pairs)


def lev_parts(x):
    if lax.axis_size("lev") == 2:
        return [x, lax.ppermute(x, "lev", [(0, 1), (1, 0)])]
    return [lax.psum(x, "lev")]


def per_device(
    marine_layered_warmth,
    bottom_sky_warmth,
    bottom_breeze_magnitude,
    depth_shares,
    piece_sky_box,
    sky_share_fraction,
    piece_marine_box,
    marine_share_fraction,
    marine_indicator,
    marine_result_adjoint,
    energy_transport_adjoint,
):
    n, levs = lax.axis_size("tile"), lax.axis_size("lev")
    levels, rows, cols = marine_layered_warmth.shape
    cells = bottom_sky_warmth.shape[0]
    high = rows + 8
    raw = [marine_layered_warmth, marine_result_adjoint, marine_indicator, depth_shares]
    raw += [
        x.reshape(1, cells)
        for x in (bottom_sky_warmth, bottom_breeze_magnitude, energy_transport_adjoint)
    ]
    raw += [piece_sky_box[0], sky_share_fraction[0], piece_marine_box[0], marine_share_fraction[0]]
    raw = [pltpu.with_memory_space_constraint(x, pltpu.HBM) for x in raw]
    held = [pltpu.VMEM(x.shape, x.dtype) for x in [raw[0], raw[2]]]
    held += [pltpu.SMEM(depth_shares.shape, F32)]
    held += [pltpu.VMEM(x.shape, x.dtype) for x in raw[4:9]]
    msg, ext, surface, share_rows, marine, marine_weight = call(
        functools.partial(pack_kernel, n),
        [(4 * n + 24, cells), ((levels + 1) * high, cols), (rows, cols), (8, cols)]
        + [jax.ShapeDtypeStruct(x.shape, x.dtype) for x in raw[9:]],
        raw,
        [HBM] * len(raw),
        scratch=held + [pltpu.SemaphoreType.DMA((10 + levels,))],
    )
    other = traded(msg, 0, 1)
    fold = 8 * fold_slots(high, cols, levels + 1)[1]
    ext, edge_out, near_out = call(
        functools.partial(send_kernel, n, levels + 1),
        [ext.shape, (fold, cols), ((fold + 20 + 4 * (n - 2) + 7) // 8 * 8, cols)],
        [msg, other, ext],
    )
    edge_in = beyond(edge_out)
    near_in = traded(near_out, 1, 1)
    merged = n == 4 and levs == 2
    adjoint, lev_msg, *far_out = call(
        functools.partial(diffuse_kernel, n, levels),
        [(levels, rows, cols), (2 * rows + (16 if merged else 0), cols)] + [(40, cols)] * (n // 2 - 1),
        [ext, near_in, edge_in, surface, share_rows, msg, other, marine],
    )
    lev_in = lev_parts(lev_msg)
    far_in = [traded(x, 2 * i + 2, 1) for i, x in enumerate(far_out)]
    picks, tables = call(
        functools.partial(near_kernel, n, fold),
        [(3, 4, cells), jax.ShapeDtypeStruct((4, cells, cells), BF16)],
        [msg, other, near_in],
    )
    values, chip, *returns = call(
        functools.partial(slot_kernel, n, len(lev_in), rows),
        [(2 * n, cells), (40, cols)] + [(8, cols)] * n,
        [*lev_in, picks, tables, marine, marine_weight, *far_in],
        scratch=[pltpu.VMEM((3, 2 * n, cells), F32)] * 2
        + [pltpu.VMEM((2 * n, cells, cells), BF16)],
    )
    (slots,) = call(functools.partial(own_kernel, n), [(rows, cols)], [marine, values])
    if merged:
        theirs = traded(chip, 0, 1)
        first, second = call(
            merge_kernel, [(32, cols), (32, cols)], [values, *returns[1:], theirs]
        )
        first = by_core(first, (1, 0), (3, 0))
        second = by_core(second, (0, 1), (2, 0))
        gradient, sums = call(
            functools.partial(post_kernel, n),
            [(rows, cols), (rows + 8, cols)],
            [first, second, returns[0], slots, lev_in[1], theirs],
            scratch=[pltpu.VMEM((2 * n, cells), jnp.int32), pltpu.VMEM((2 * n, cells), F32)],
        )
    else:
        gradient = sum(lev_parts(slots))
        sums = returns[0]
        for step in range(1, n):
            sums = sums + traded(returns[step], step, 1)
    results = [(levels, rows, cols), (1, cells), (1, cells)]
    state, air_gradient, wind_gradient = call(
        functools.partial(final_kernel, merged),
        results,
        [gradient, adjoint, share_rows, sums, traded(sums, 0, 1)],
        out_specs=[HBM] * 3,
        scratch=[pltpu.VMEM(x, F32) for x in results] + [pltpu.SemaphoreType.DMA((3,))],
    )
    return (state, air_gradient.reshape(cells), wind_gradient.reshape(cells))


def solution(mesh):
    return jax.shard_map(
        per_device,
        mesh=mesh,
        in_specs=(
            P(("ens", "lev"), "sub", "tile"),
            P(("ens", "tile", "lev", "sub")),
            P(("ens", "tile", "lev", "sub")),
            P("lev"),
            P(("tile", "lev", "sub"), None, None),
            P(("tile", "lev", "sub"), None, None),
            P(("tile", "lev", "sub"), None, None),
            P(("tile", "lev", "sub"), None, None),
            P("sub", "tile"),
            P(("ens", "lev"), "sub", "tile"),
            P(("ens", "tile", "lev", "sub")),
        ),
        out_specs=(
            P(("ens", "lev"), "sub", "tile"),
            P(("ens", "tile", "lev", "sub")),
            P(("ens", "tile", "lev", "sub")),
        ),
        check_vma=False,
    )
```

```python
import functools

import jax
import jax.numpy as jnp
from jax import lax
from jax.experimental import pallas as pl
from jax.experimental.pallas import tpu as pltpu
from jax.sharding import PartitionSpec as P

BULK_ITERS = 3
STEPS = 3
HALO = STEPS
MIXING = 0.2
TRANSFER = 1.0
STABILITY = 0.5
F32 = jnp.float32
BF16 = jnp.bfloat16
VMEM = pl.BlockSpec(memory_space=pltpu.VMEM)
HBM = pl.BlockSpec(memory_space=pltpu.HBM)


def call(kernel, outs, operands, specs=None, out_specs=None, scratch=(), aliases=None):
    outs = [jax.ShapeDtypeStruct(x, F32) if isinstance(x, tuple) else x for x in outs]
    return pl.pallas_call(
        kernel,
        out_shape=outs,
        in_specs=specs or [VMEM] * len(operands),
        out_specs=out_specs or [VMEM] * len(outs),
        scratch_shapes=list(scratch),
        input_output_aliases=aliases or {},
        compiler_params=pltpu.CompilerParams(vmem_limit_bytes=24 * 1024 * 1024),
    )(*operands)


def halves(x):
    high = x.astype(BF16)
    low = (x - high.astype(F32)).astype(BF16)
    return high, low


def fold_place(cols):
    lane = lax.broadcasted_iota(jnp.int32, (8, cols), 1)
    return lax.rem(lane + HALO, cols)


def fold_slots(high, cols, fields):
    each = cols // (2 * HALO * fields)
    groups = high // 8
    return [(g // each, g % each) for g in range(groups)], -(-groups // each)


def folded(ext, high, fields):
    cols = ext.shape[1]
    place = fold_place(cols) // (2 * HALO)
    slots, tiles = fold_slots(high, cols, fields)
    out = [jnp.zeros((8, cols), F32)] * tiles
    for g, (k, at) in enumerate(slots):
        for i in range(fields):
            slot = at * fields + i
            rows = ext[high * i + 8 * g : high * i + 8 * g + 8, :]
            moved = pltpu.roll(rows, 2 * HALO * slot, 1) if slot else rows
            out[k] = jnp.where(place == slot, moved, out[k])
    return jnp.concatenate(out, axis=0)


def lanes_from(shape, first, count):
    lane = lax.broadcasted_iota(jnp.int32, shape, 1)
    return (lane >= first) & (lane < first + count)


def turn_lanes(x, by):
    by = by % x.shape[1]
    return pltpu.roll(x, by, 1) if by else x


def own_strips(fields):
    width = 2 * HALO
    cols = fields[0].shape[1]
    out = jnp.zeros_like(fields[0])
    for z, x in enumerate(fields):
        base = 3 * width * z
        out = jnp.where(lanes_from(x.shape, base, width), turn_lanes(x, base + width), out)
        out = jnp.where(lanes_from(x.shape, base + 2 * width, width), turn_lanes(x, base + 2 * width), out)
    return out


def strips_beyond(tiles, own, fields, count):
    width = 2 * HALO
    high, cols = own.shape
    out = []
    for g, (k, at) in enumerate(fold_slots(high, cols, count)[0]):
        x = own[8 * g : 8 * g + 8]
        for z, i in enumerate(fields):
            base = width * (3 * z + 1)
            moved = turn_lanes(tiles[k], base - width * (at * count + i))
            x = jnp.where(lanes_from(x.shape, base, width), moved, x)
        out.append(x)
    return jnp.concatenate(out, axis=0)


def around(x):
    high, cols = x.shape
    return pltpu.roll(x, 1, 0) + pltpu.roll(x, high - 1, 0) + pltpu.roll(x, 1, 1) + pltpu.roll(x, cols - 1, 1)


def diffused(wet, fields):
    keep = wet * (1.0 - MIXING * around(wet))
    mix = MIXING * wet
    out = []
    for v in fields:
        v = wet * v
        for sweep_index in range(STEPS):
            v = keep * v + mix * around(v)
        out.append(v)
    return out


def pack_kernel(n, *refs):
    cot, sea, sky, breeze, energy, sky_index, sky_weight, msg, ext = refs[:9]
    sea_in, sky_in, breeze_in, energy_in, index_in, weight_in, sems = refs[9:]
    rows, cols = sea.shape
    levels = cot.shape[0]
    high = rows + 8
    pairs = [(cot.at[z], ext.at[pl.ds(high * z, rows)]) for z in range(levels)]
    pairs += [(sea, sea_in), (sky_index, index_in), (sky_weight, weight_in)]
    pairs += [(sky, sky_in), (breeze, breeze_in), (energy, energy_in)]
    copies = [pltpu.make_async_copy(a, b, sems.at[i]) for i, (a, b) in enumerate(pairs)]
    for copy in copies:
        copy.start()
    sub = lax.axis_index("sub")
    msg[...] = jnp.zeros_like(msg)
    for z in range(levels + 1):
        ext[high * z + rows : high * (z + 1), :] = jnp.zeros((8, cols), F32)
    for copy in copies:
        copy.wait()
    ext[high * levels : high * levels + rows, :] = sea_in[...].astype(F32)
    msg[0 : 2 * n, :] = index_in[...].astype(F32)
    msg[2 * n : 4 * n, :] = weight_in[...]
    for i, ref in enumerate((sky_in, breeze_in, energy_in)):
        msg[4 * n + i : 4 * n + i + 1, :] = ref[...]
    base = 4 * n + 8
    for i in range(levels + 1):
        at, top, left = high * i, base + HALO * (i // 2), cols * (i % 2)
        outer = jnp.where(sub == 0, ext[at + rows - HALO : at + rows], ext[at : at + HALO])
        msg[top : top + HALO, left : left + cols] = outer
    edges = folded(ext, high, levels + 1)
    for k in range(2):
        msg[4 * n + 16 : 4 * n + 24, cols * k : cols * (k + 1)] = edges[8 * k : 8 * k + 8]


def halo_rows(n, msg, i, cols):
    top, left = 4 * n + 8 + HALO * (i // 2), cols * (i % 2)
    return msg[top : top + HALO, left : left + cols]


def both_bands(msg, other, index, sub):
    own, far = msg[pl.ds(index, 1), :], other[pl.ds(index, 1), :]
    return [jnp.where(sub == 0, own, far), jnp.where(sub == 0, far, own)]


def table_rows(n, msg, other, target, band, sub):
    row = 2 * target + band
    return both_bands(msg, other, row, sub) + both_bands(msg, other, 2 * n + row, sub)


def value_rows(n, msg, other, sub):
    return [x for i in range(3) for x in both_bands(msg, other, 4 * n + i, sub)]


def write_pairs(out, at, rows):
    cols = out.shape[1]
    for i, row in enumerate(rows):
        out[at + i : at + i + 1, :] = row[:, :cols]
        out[at + len(rows) + i : at + len(rows) + i + 1, :] = row[:, cols:]


def write_halves(out, at, x):
    count, cols = x.shape[0], out.shape[1]
    out[at : at + count, :] = x[:, :cols]
    out[at + count : at + 2 * count, :] = x[:, cols:]


def read_halves(ref, at, count):
    return jnp.concatenate([ref[at : at + count, :], ref[at + count : at + 2 * count, :]], axis=1)


def read_pairs(ref, at, count):
    return [
        jnp.concatenate([ref[at + i : at + i + 1, :], ref[at + count + i : at + count + i + 1, :]], axis=1)
        for i in range(count)
    ]


def send_kernel(n, fields, msg, other, ext_in, ext, edge_out, near_out):
    sub, tile = lax.axis_index("sub"), lax.axis_index("tile")
    cols = ext.shape[1]
    high = ext.shape[0] // fields
    rows = high - 8
    for i in range(fields):
        base = high * i
        strip = halo_rows(n, other, i, cols)
        ext[base : base + rows, :] = ext_in[base : base + rows, :]
        ext[base + rows : base + high, :] = jnp.zeros((8, cols), F32)
        ext[base + rows : base + rows + HALO, :] = jnp.where(sub == 0, strip, 0.0)
        ext[base + high - HALO : base + high, :] = jnp.where(sub == 0, 0.0, strip)
    slots, count = fold_slots(high, cols, fields)
    tile_at, at = slots[-1]
    place = fold_place(cols) // (2 * HALO)
    tiles = [other[4 * n + 16 : 4 * n + 24, cols * k : cols * (k + 1)] for k in range(count)]
    for i in range(fields):
        strip = halo_rows(n, msg, i, cols)
        blank = jnp.zeros((8 - 2 * HALO, cols), F32)
        rows_beyond = [jnp.where(sub == 1, strip, 0.0), blank, jnp.where(sub == 1, 0.0, strip)]
        slot = at * fields + i
        moved = pltpu.roll(jnp.concatenate(rows_beyond, axis=0), 2 * HALO * slot, 1)
        tiles[tile_at] = jnp.where(place == slot, moved, tiles[tile_at])
    edges = jnp.concatenate(tiles, axis=0)
    fold = edges.shape[0]
    edge_out[...] = edges
    near_out[0:fold, :] = edges
    near = tile ^ 1
    air = table_rows(n, msg, other, near, 1 - sub, sub) + value_rows(n, msg, other, sub)
    write_pairs(near_out, fold, air)
    at = fold + 20
    for step in range(2, n, 2):
        write_pairs(near_out, at, table_rows(n, msg, other, near ^ step, sub, sub))
        at += 8
    near_out[at : near_out.shape[0], :] = jnp.zeros((near_out.shape[0] - at, cols), F32)


def side_kernel(levels, ext, *refs):
    warm, shares, marine, marine_weight = refs[:4]
    block, strips, surface, share_rows, marine_out, marine_weight_out = refs[4:10]
    warm_in, shares_in, sems = refs[10:]
    pairs = [(warm, warm_in), (shares, shares_in), (marine, marine_out), (marine_weight, marine_weight_out)]
    copies = [pltpu.make_async_copy(a, b, sems.at[i]) for i, (a, b) in enumerate(pairs)]
    for copy in copies:
        copy.start()
    rows, cols = surface.shape
    high = rows + 8
    fields = [ext[high * i : high * (i + 1), :] for i in range(levels + 1)]
    for z, x in enumerate(diffused(fields[levels], fields[:levels])):
        block[z] = x[:rows]
    strips[0:high, :] = own_strips(fields[:levels])
    strips[high : 2 * high, :] = own_strips([fields[levels]] * levels)
    for copy in copies:
        copy.wait()
    surface[...] = sum(shares_in[z] * warm_in[z] for z in range(levels))
    for z in range(levels):
        share_rows[z : z + 1, :] = jnp.full((1, cols), shares_in[z], F32)


def diffuse_kernel(n, levels, *refs):
    ext, near_in, edge_in, surface, share_rows, msg, other, marine, block, strips = refs[:10]
    adjoint_out, lev_out = refs[10:12]
    sub, tile = lax.axis_index("sub"), lax.axis_index("tile")
    rows, cols = surface.shape
    high = rows + 8
    fold = edge_in.shape[0]
    own_values = value_rows(n, msg, other, sub)
    near_values = read_pairs(near_in, fold, 10)[4:]
    for i, out in enumerate(refs[12:]):
        air = table_rows(n, msg, other, tile ^ (2 * i + 2), 1 - sub, sub) + own_values
        air += read_pairs(near_in, fold + 20 + 8 * i, 4) + near_values
        write_pairs(out, 0, air)
    even = tile % 2 == 0
    lane = lax.broadcasted_iota(jnp.int32, (8, cols), 1)
    tiles = []
    for k in range(0, fold, 8):
        near, far = near_in[k : k + 8, :], edge_in[k : k + 8, :]
        right = jnp.where(tile < n - 1, jnp.where(even, near, far), 0.0)
        left = jnp.where(tile > 0, jnp.where(even, far, near), 0.0)
        tiles.append(jnp.where(lax.rem(lane, 2 * HALO) < HALO, right, turn_lanes(left, 2 * HALO)))
    wet = strips_beyond(tiles, strips[high : 2 * high, :], [levels] * levels, levels + 1)
    strip = strips_beyond(tiles, strips[0:high, :], list(range(levels)), levels + 1)
    strip = diffused(wet, [strip])[0][:rows]
    own_wet = ext[high * levels : high * levels + rows, :]
    heat = jnp.zeros((rows, cols), F32)
    for z in range(levels):
        base = 6 * HALO * z
        v = jnp.where(lanes_from((rows, cols), 0, HALO), turn_lanes(strip, -base - 4 * HALO), block[z])
        last = turn_lanes(strip, -base - 2 * HALO)
        v = jnp.where(lanes_from((rows, cols), cols - HALO, HALO), last, v)
        adjoint = own_wet * v
        adjoint_out[z] = adjoint
        heat += share_rows[z : z + 1, :] * adjoint
    lev_out[0:rows, :] = surface[...]
    lev_out[rows : 2 * rows, :] = own_wet * heat
    if lev_out.shape[0] > 2 * rows:
        write_halves(lev_out, 2 * rows, marine[...].astype(F32))


def bulk_adjoint(warmth_gap, flux_sens):
    transfer_rate = jnp.full_like(warmth_gap, TRANSFER)
    rates = [transfer_rate]
    slopes = []
    for sweep_index in range(BULK_ITERS):
        bent = jnp.tanh(transfer_rate * warmth_gap)
        slopes.append(TRANSFER * STABILITY * (1.0 - bent * bent))
        transfer_rate = TRANSFER * (1.0 + STABILITY * bent)
        rates.append(transfer_rate)
    contrast_sens = transfer_rate * flux_sens
    rate_sens = warmth_gap * flux_sens
    for sweep_index in reversed(range(BULK_ITERS)):
        inner_sens = rate_sens * slopes[sweep_index]
        contrast_sens = contrast_sens + inner_sens * rates[sweep_index]
        rate_sens = inner_sens * warmth_gap
    return contrast_sens


def onehot(index, count):
    cells = lax.broadcasted_iota(jnp.int32, (count, index.shape[1]), 0)
    return jnp.where(cells == index, 1.0, 0.0).astype(BF16)


def dot(a, b, ca, cb):
    return lax.dot_general(a, b, (((ca,), (cb,)), ((), ())), preferred_element_type=F32)


def turned(x):
    return x.astype(F32).T.astype(BF16)


def look_up(air, at, picks, tables, uppers, turn=False):
    cols = tables.shape[2] if turn else tables.shape[1]
    for band in range(2):
        cell = air[band].astype(jnp.int32)
        hot = onehot(lax.rem(cell, cols), cols)
        tables[at + band] = turned(hot) if turn else hot
        values = [air[4 + band], air[6 + band], air[8 + band]]
        values = jnp.concatenate([x[:, :cols] for x in values] + [x[:, cols:] for x in values], axis=0)
        found = dot(jnp.concatenate(halves(values), axis=0), hot, 1, 0)
        found = found[0:6] + found[6:12]
        upper = cell >= cols
        found = jnp.where(upper, found[3:6], found[0:3])
        place = slice(at + band, at + band + 1)
        picks[0, place, :] = found[0:1]
        picks[1, place, :] = found[1:2]
        picks[2, place, :] = air[2 + band] * found[2:3]
        uppers[place, :] = upper.astype(F32)


def near_kernel(n, fold, msg, other, near_in, picks, tables, uppers):
    sub, tile = lax.axis_index("sub"), lax.axis_index("tile")
    own = table_rows(n, msg, other, tile, sub, sub) + value_rows(n, msg, other, sub)
    look_up(own, 0, picks, tables, uppers, True)
    look_up(read_pairs(near_in, fold, 10), 2, picks, tables, uppers, True)


def slot_kernel(n, count, rows, *refs):
    lev_parts, refs = refs[:count], refs[count:]
    near_picks, near_tables, near_uppers, marine, weight = refs[:5]
    far_in, refs = refs[5 : 4 + n // 2], refs[4 + n // 2 :]
    values_out, chip_out, returns = refs[0], refs[1], refs[2 : 2 + n]
    held, picks, tables, uppers = refs[2 + n :]
    sub, tile = lax.axis_index("sub"), lax.axis_index("tile")
    cols = chip_out.shape[1]
    picks[:, 0:4, :] = near_picks[...]
    uppers[0:4, :] = near_uppers[0:4, :]
    for i, ref in enumerate(far_in):
        air = read_pairs(ref, 0, 20)
        for j in range(2):
            look_up(air[10 * j : 10 * j + 10], 4 * i + 4 + 2 * j, picks, tables, uppers)
    table = sum(ref[0 : 2 * rows, :] for ref in lev_parts)
    table = jnp.concatenate(halves(table), axis=1)
    for step in range(n):
        for band in range(2):
            at, place = 2 * step + band, 2 * (tile ^ step) + band
            cell = marine[pl.ds(place, 1), :]
            row, col = cell // cols, lax.rem(cell, cols)
            col_hot = onehot(col, cols)
            spread = dot(table, jnp.concatenate([col_hot, col_hot], axis=0), 1, 0)
            row_mask = lax.broadcasted_iota(jnp.int32, (rows, cell.shape[1]), 0) == row
            for i in range(2):
                piece = jnp.where(row_mask, spread[rows * i : rows * (i + 1)], 0.0)
                held[i, at : at + 1, :] = jnp.sum(piece, axis=0, keepdims=True)
            held[2, at : at + 1, :] = weight[pl.ds(place, 1), :]

    difference = held[0] - picks[0]
    wind = picks[1]
    flux_sens = held[2] * held[1] + picks[2]
    contrast_sens = bulk_adjoint(wind * difference, flux_sens)
    surface_sens = contrast_sens * wind
    wind_sens = contrast_sens * difference
    values_out[...] = surface_sens
    for step in range(n):
        for band in range(2):
            at = 2 * step + band
            near = at < 4
            hot = near_tables[at] if near else tables[at]
            upper = uppers[at : at + 1, :]
            values = jnp.concatenate([surface_sens[at : at + 1], wind_sens[at : at + 1]], axis=0)
            values = jnp.concatenate([values * (1.0 - upper), values * upper], axis=0)
            sums = dot(jnp.concatenate(halves(values), axis=0), hot, 1, 0 if near else 1)
            sums = sums[0:4] + sums[4:8]
            returns[step][2 * band : 2 * band + 2, :] = sums[0:2]
            returns[step][2 * band + 4 : 2 * band + 6, :] = sums[2:4]
    if n == 4:
        chip_out[0:8, :] = jnp.where(sub == 0, returns[2][...], returns[1][...])
        write_halves(chip_out, 8, surface_sens)
        chip_out[8:16, :] = jnp.where(sub == 0, returns[3][...], chip_out[8:16, :])
        chip_out[24:40, :] = lev_parts[-1][2 * rows : 2 * rows + 16, :]


def scatter(n, rows, cols, tile, cell_of, value_of, col_hot_of=None):
    total = jnp.zeros((2 * rows, cols), F32)
    for step in range(n):
        for band in range(2):
            at = 2 * step + band
            cell = cell_of(2 * (tile ^ step) + band)
            row, col = cell // cols, lax.rem(cell, cols)
            row_mask = lax.broadcasted_iota(jnp.int32, (rows, cell.shape[1]), 0) == row
            spread = jnp.concatenate(
                [jnp.where(row_mask, x.astype(F32), 0.0).astype(BF16) for x in halves(value_of(at))],
                axis=0,
            )
            if col_hot_of:
                total += dot(spread, col_hot_of(at), 1, 0)
            else:
                total += dot(spread, onehot(col, cols), 1, 1)
    return total[:rows] + total[rows:]


def own_kernel(n, marine, values, *refs):
    tile = lax.axis_index("tile")
    if len(refs) > 1:
        lev_in, theirs, out, cells, tables = refs
        rows, cols = out.shape

        @pl.when(lax.axis_index("sub") == 0)
        def _():
            for band, (ref, at) in enumerate(((lev_in, 2 * rows), (theirs, 24))):
                cells[2 * n * band : 2 * n * (band + 1), :] = read_halves(ref, at, 2 * n).astype(jnp.int32)
                for i in range(2 * n):
                    place = 2 * n * band + 2 * (tile ^ (i // 2)) + i % 2
                    col = lax.rem(cells[pl.ds(place, 1), :], cols)
                    tables[2 * n * band + i] = turned(onehot(col, cols))

    out = refs[2] if len(refs) > 1 else refs[0]
    rows, cols = out.shape
    out[...] = scatter(
        n, rows, cols, tile, lambda i: marine[pl.ds(i, 1), :], lambda i: values[i : i + 1, :]
    )


def post_kernel(n, first, second, own, slots, cells, tables, gradient, out, values):
    even = lax.axis_index("sub") == 0
    tile = lax.axis_index("tile")
    rows, cols = gradient.shape
    out[0:8, :] = first[0:8, :] + own[...] + jnp.where(even, 0.0, second[0:8, :])

    @pl.when(even)
    def _():
        for band in range(2):
            base = 2 * n * band
            values[...] = read_halves(second, 4 * n * band, 2 * n)
            total = scatter(
                n,
                rows,
                cols,
                tile,
                lambda i: cells[pl.ds(base + i, 1), :],
                lambda i: values[i : i + 1, :],
                lambda i: tables[base + i],
            )
            if band == 0:
                gradient[...] = slots[...] + total
            else:
                out[8 : rows + 8, :] = total

    @pl.when(jnp.logical_not(even))
    def _():
        gradient[...] = slots[...]
        out[8 : rows + 8, :] = jnp.zeros_like(slots)


def merge_kernel(values, near, two, three, theirs, first, second):
    even = lax.axis_index("sub") == 0
    first[...] = jnp.zeros_like(first)
    first[0:8, :] = jnp.where(even, near[...] + theirs[0:8, :], three[...] + theirs[8:16, :])
    write_halves(second, 0, values[...])
    second[0:8, :] = jnp.where(even, second[0:8, :], two[...] + theirs[0:8, :])
    second[16:32, :] = theirs[8:24, :]


def final_kernel(merged, slots, adjoint, share_rows, sums, other, *refs):
    state_out, air_out, wind_out, state, air, wind, sems = refs
    sub = lax.axis_index("sub")
    gradient = slots[...]
    if merged:
        gradient += jnp.where(sub == 0, 0.0, other[8 : slots.shape[0] + 8, :])
    for z in range(adjoint.shape[0]):
        state[z] = adjoint[z] + share_rows[z : z + 1, :] * gradient
    copies = [pltpu.make_async_copy(state, state_out, sems.at[0])]
    copies[0].start()
    both = sums[0:8, :] + other[0:8, :]
    own = [jnp.where(sub == 0, both[i : i + 2], both[i + 2 : i + 4]) for i in (0, 4)]
    own = jnp.concatenate(own, axis=1)
    air[...] = -own[0:1]
    wind[...] = own[1:2]
    for i, (a, b) in enumerate(((air, air_out), (wind, wind_out))):
        copies.append(pltpu.make_async_copy(a, b, sems.at[1 + i]))
        copies[-1].start()
    for copy in copies:
        copy.wait()


def traded(x, step, swap=0):
    n, bands = lax.axis_size("tile"), lax.axis_size("sub")
    pairs = [
        (t * bands + s, (t ^ step) * bands + (s ^ swap)) for t in range(n) for s in range(bands)
    ]
    return lax.ppermute(x, ("tile", "sub"), pairs)


def beyond(x):
    n, bands = lax.axis_size("tile"), lax.axis_size("sub")
    pairs = []
    for t in range(n):
        to = t if t in (0, n - 1) else ((t + 1) ^ 1) - 1
        pairs += [(t * bands + s, to * bands + (s ^ 1)) for s in range(bands)]
    return lax.ppermute(x, ("tile", "sub"), pairs)


def by_core(x, even, odd):
    n, levs, bands = (lax.axis_size(axis) for axis in ("tile", "lev", "sub"))
    pairs = []
    for t in range(n):
        for l in range(levs):
            for s in range(bands):
                tx, lx = odd if s else even
                pairs.append(((t * levs + l) * bands + s, ((t ^ tx) * levs + (l ^ lx)) * bands + s))
    return lax.ppermute(x, ("tile", "lev", "sub"), pairs)


def lev_parts(x):
    if lax.axis_size("lev") == 2:
        return [x, lax.ppermute(x, "lev", [(0, 1), (1, 0)])]
    return [lax.psum(x, "lev")]


def per_device(
    marine_layered_warmth,
    bottom_sky_warmth,
    bottom_breeze_magnitude,
    depth_shares,
    piece_sky_box,
    sky_share_fraction,
    piece_marine_box,
    marine_share_fraction,
    marine_indicator,
    marine_result_adjoint,
    energy_transport_adjoint,
):
    n, levs = lax.axis_size("tile"), lax.axis_size("lev")
    levels, rows, cols = marine_layered_warmth.shape
    cells = bottom_sky_warmth.shape[0]
    high = rows + 8
    def pinned(*arrays):
        return [pltpu.with_memory_space_constraint(x, pltpu.HBM) for x in arrays]

    def like(x):
        return jax.ShapeDtypeStruct(x.shape, x.dtype)

    def buffers(arrays):
        return [pltpu.VMEM(x.shape, x.dtype) for x in arrays]

    air = [
        x.reshape(1, cells)
        for x in (bottom_sky_warmth, bottom_breeze_magnitude, energy_transport_adjoint)
    ]
    raw = pinned(
        marine_result_adjoint, marine_indicator, *air, piece_sky_box[0], sky_share_fraction[0]
    )
    msg, ext = call(
        functools.partial(pack_kernel, n),
        [(4 * n + 24, cells), ((levels + 1) * high, cols)],
        raw,
        [HBM] * len(raw),
        scratch=buffers(raw[1:]) + [pltpu.SemaphoreType.DMA((len(raw) - 1 + levels,))],
    )
    other = traded(msg, 0, 1)
    fold = 8 * fold_slots(high, cols, levels + 1)[1]
    ext, edge_out, near_out = call(
        functools.partial(send_kernel, n, levels + 1),
        [ext.shape, (fold, cols), ((fold + 20 + 4 * (n - 2) + 7) // 8 * 8, cols)],
        [msg, other, ext],
    )
    edge_in = beyond(edge_out)
    near_in = traded(near_out, 1, 1)
    raw = pinned(marine_layered_warmth, depth_shares, piece_marine_box[0], marine_share_fraction[0])
    block, strips, surface, share_rows, marine, marine_weight = call(
        functools.partial(side_kernel, levels),
        [(levels, rows, cols), (2 * high, cols), (rows, cols), (8, cols), like(raw[2]), like(raw[3])],
        [ext, *raw],
        [VMEM] + [HBM] * 4,
        scratch=buffers(raw[:1])
        + [pltpu.SMEM(depth_shares.shape, F32), pltpu.SemaphoreType.DMA((4,))],
    )
    merged = n == 4 and levs == 2
    adjoint, lev_msg, *far_out = call(
        functools.partial(diffuse_kernel, n, levels),
        [(levels, rows, cols), (2 * rows + (16 if merged else 0), cols)] + [(40, cols)] * (n // 2 - 1),
        [ext, near_in, edge_in, surface, share_rows, msg, other, marine, block, strips],
    )
    lev_in = lev_parts(lev_msg)
    far_in = [traded(x, 2 * i + 2, 1) for i, x in enumerate(far_out)]
    picks, tables, uppers = call(
        functools.partial(near_kernel, n, fold),
        [(3, 4, cells), jax.ShapeDtypeStruct((4, cells, cols), BF16), (8, cells)],
        [msg, other, near_in],
    )
    values, chip, *returns = call(
        functools.partial(slot_kernel, n, len(lev_in), rows),
        [(2 * n, cells), (40, cols)] + [(8, cols)] * n,
        [*lev_in, picks, tables, uppers, marine, marine_weight, *far_in],
        scratch=[pltpu.VMEM((3, 2 * n, cells), F32)] * 2
        + [pltpu.VMEM((2 * n, cols, cells), BF16), pltpu.VMEM((2 * n, cells), F32)],
    )
    if merged:
        theirs = traded(chip, 0, 1)
        slots, partner_cells, partner_tables = call(
            functools.partial(own_kernel, n),
            [(rows, cols), jax.ShapeDtypeStruct((4 * n, cells), jnp.int32)]
            + [jax.ShapeDtypeStruct((4 * n, cells, cols), BF16)],
            [marine, values, lev_in[1], theirs],
        )
        first, second = call(
            merge_kernel, [(32, cols), (32, cols)], [values, *returns[1:], theirs]
        )
        first = by_core(first, (1, 0), (3, 0))
        second = by_core(second, (0, 1), (2, 0))
        gradient, sums = call(
            functools.partial(post_kernel, n),
            [(rows, cols), (rows + 8, cols)],
            [first, second, returns[0], slots, partner_cells, partner_tables],
            scratch=[pltpu.VMEM((2 * n, cells), F32)],
        )
    else:
        (slots,) = call(functools.partial(own_kernel, n), [(rows, cols)], [marine, values])
        gradient = sum(lev_parts(slots))
        sums = returns[0]
        for step in range(1, n):
            sums = sums + traded(returns[step], step, 1)
    results = [(levels, rows, cols), (1, cells), (1, cells)]
    state, air_gradient, wind_gradient = call(
        functools.partial(final_kernel, merged),
        results,
        [gradient, adjoint, share_rows, sums, traded(sums, 0, 1)],
        out_specs=[HBM] * 3,
        scratch=[pltpu.VMEM(x, F32) for x in results] + [pltpu.SemaphoreType.DMA((3,))],
    )
    return (state, air_gradient.reshape(cells), wind_gradient.reshape(cells))


def solution(mesh):
    return jax.shard_map(
        per_device,
        mesh=mesh,
        in_specs=(
            P(("ens", "lev"), "sub", "tile"),
            P(("ens", "tile", "lev", "sub")),
            P(("ens", "tile", "lev", "sub")),
            P("lev"),
            P(("tile", "lev", "sub"), None, None),
            P(("tile", "lev", "sub"), None, None),
            P(("tile", "lev", "sub"), None, None),
            P(("tile", "lev", "sub"), None, None),
            P("sub", "tile"),
            P(("ens", "lev"), "sub", "tile"),
            P(("ens", "tile", "lev", "sub")),
        ),
        out_specs=(
            P(("ens", "lev"), "sub", "tile"),
            P(("ens", "tile", "lev", "sub")),
            P(("ens", "tile", "lev", "sub")),
        ),
        check_vma=False,
    )
```

```python
import functools

import jax
import jax.numpy as jnp
from jax import lax
from jax.experimental import pallas as pl
from jax.experimental.pallas import tpu as pltpu
from jax.sharding import PartitionSpec as P

BULK_ITERS = 3
STEPS = 3
HALO = STEPS
MIXING = 0.2
TRANSFER = 1.0
STABILITY = 0.5
F32 = jnp.float32
BF16 = jnp.bfloat16
VMEM = pl.BlockSpec(memory_space=pltpu.VMEM)
HBM = pl.BlockSpec(memory_space=pltpu.HBM)


def call(kernel, outs, operands, specs=None, out_specs=None, scratch=(), aliases=None):
    outs = [jax.ShapeDtypeStruct(x, F32) if isinstance(x, tuple) else x for x in outs]
    return pl.pallas_call(
        kernel,
        out_shape=outs,
        in_specs=specs or [VMEM] * len(operands),
        out_specs=out_specs or [VMEM] * len(outs),
        scratch_shapes=list(scratch),
        input_output_aliases=aliases or {},
        compiler_params=pltpu.CompilerParams(vmem_limit_bytes=24 * 1024 * 1024),
    )(*operands)


def halves(x):
    high = x.astype(BF16)
    low = (x - high.astype(F32)).astype(BF16)
    return high, low


def fold_place(cols):
    lane = lax.broadcasted_iota(jnp.int32, (8, cols), 1)
    return lax.rem(lane + HALO, cols)


def fold_slots(high, cols, fields):
    each = cols // (2 * HALO * fields)
    groups = high // 8
    return [(g // each, g % each) for g in range(groups)], -(-groups // each)


def folded(ext, high, fields):
    cols = ext.shape[1]
    place = fold_place(cols) // (2 * HALO)
    slots, tiles = fold_slots(high, cols, fields)
    out = [jnp.zeros((8, cols), F32)] * tiles
    for g, (k, at) in enumerate(slots):
        for i in range(fields):
            slot = at * fields + i
            rows = ext[high * i + 8 * g : high * i + 8 * g + 8, :]
            moved = pltpu.roll(rows, 2 * HALO * slot, 1) if slot else rows
            out[k] = jnp.where(place == slot, moved, out[k])
    return jnp.concatenate(out, axis=0)


def strip_base(z):
    return 6 * HALO * z - 4 * HALO


def lanes_from(shape, first, count):
    lane = lax.broadcasted_iota(jnp.int32, shape, 1)
    return lax.rem(lane + (-first) % shape[1], shape[1]) < count


def turn_lanes(x, by):
    by = by % x.shape[1]
    return pltpu.roll(x, by, 1) if by else x


def own_strips(fields):
    width = 2 * HALO
    cols = fields[0].shape[1]
    out = jnp.zeros_like(fields[0])
    for z, x in enumerate(fields):
        base = strip_base(z)
        out = jnp.where(lanes_from(x.shape, base, width), turn_lanes(x, base + width), out)
        out = jnp.where(lanes_from(x.shape, base + 2 * width, width), turn_lanes(x, base + 2 * width), out)
    return out


def strips_beyond(tiles, own, fields, count):
    width = 2 * HALO
    high, cols = own.shape
    out = []
    for g, (k, at) in enumerate(fold_slots(high, cols, count)[0]):
        x = own[8 * g : 8 * g + 8]
        for z, i in enumerate(fields):
            base = strip_base(z) + width
            moved = turn_lanes(tiles[k], base - width * (at * count + i))
            x = jnp.where(lanes_from(x.shape, base, width), moved, x)
        out.append(x)
    return jnp.concatenate(out, axis=0)


def from_strips(strip, z, block):
    shape = block.shape
    first, last = lanes_from(shape, 0, HALO), lanes_from(shape, -HALO, HALO)
    block = jnp.where(first, turn_lanes(strip, -strip_base(z) - 4 * HALO), block)
    return jnp.where(last, turn_lanes(strip, -strip_base(z) - 2 * HALO), block)


def around(x):
    high, cols = x.shape
    return pltpu.roll(x, 1, 0) + pltpu.roll(x, high - 1, 0) + pltpu.roll(x, 1, 1) + pltpu.roll(x, cols - 1, 1)


def diffused(wet, fields):
    keep = wet * (1.0 - MIXING * around(wet))
    mix = MIXING * wet
    out = []
    for v in fields:
        v = wet * v
        for sweep_index in range(STEPS):
            v = keep * v + mix * around(v)
        out.append(v)
    return out


def pack_kernel(n, *refs):
    cot, sea, sky, breeze, energy, sky_index, sky_weight, msg, ext = refs[:9]
    sea_in, sky_in, breeze_in, energy_in, index_in, weight_in, sems = refs[9:]
    rows, cols = sea.shape
    levels = cot.shape[0]
    high = rows + 8
    pairs = [(cot.at[z], ext.at[pl.ds(high * z, rows)]) for z in range(levels)]
    pairs += [(sea, sea_in), (sky_index, index_in), (sky_weight, weight_in)]
    pairs += [(sky, sky_in), (breeze, breeze_in), (energy, energy_in)]
    copies = [pltpu.make_async_copy(a, b, sems.at[i]) for i, (a, b) in enumerate(pairs)]
    for copy in copies:
        copy.start()
    sub = lax.axis_index("sub")
    msg[...] = jnp.zeros_like(msg)
    for z in range(levels + 1):
        ext[high * z + rows : high * (z + 1), :] = jnp.zeros((8, cols), F32)
    for copy in copies:
        copy.wait()
    ext[high * levels : high * levels + rows, :] = sea_in[...].astype(F32)
    msg[0 : 2 * n, :] = index_in[...].astype(F32)
    msg[2 * n : 4 * n, :] = weight_in[...]
    for i, ref in enumerate((sky_in, breeze_in, energy_in)):
        msg[4 * n + i : 4 * n + i + 1, :] = ref[...]
    base = 4 * n + 8
    for i in range(levels + 1):
        at, top, left = high * i, base + HALO * (i // 2), cols * (i % 2)
        outer = jnp.where(sub == 0, ext[at + rows - HALO : at + rows], ext[at : at + HALO])
        msg[top : top + HALO, left : left + cols] = outer
    edges = folded(ext, high, levels + 1)
    for k in range(2):
        msg[4 * n + 16 : 4 * n + 24, cols * k : cols * (k + 1)] = edges[8 * k : 8 * k + 8]


def halo_rows(n, msg, i, cols):
    top, left = 4 * n + 8 + HALO * (i // 2), cols * (i % 2)
    return msg[top : top + HALO, left : left + cols]


def both_bands(msg, other, index, sub):
    own, far = msg[pl.ds(index, 1), :], other[pl.ds(index, 1), :]
    return [jnp.where(sub == 0, own, far), jnp.where(sub == 0, far, own)]


def table_rows(n, msg, other, target, band, sub):
    row = 2 * target + band
    return both_bands(msg, other, row, sub) + both_bands(msg, other, 2 * n + row, sub)


def value_rows(n, msg, other, sub):
    return [x for i in range(3) for x in both_bands(msg, other, 4 * n + i, sub)]


def write_pairs(out, at, rows):
    cols = out.shape[1]
    for i, row in enumerate(rows):
        out[at + i : at + i + 1, :] = row[:, :cols]
        out[at + len(rows) + i : at + len(rows) + i + 1, :] = row[:, cols:]


def write_halves(out, at, x):
    count, cols = x.shape[0], out.shape[1]
    out[at : at + count, :] = x[:, :cols]
    out[at + count : at + 2 * count, :] = x[:, cols:]


def read_halves(ref, at, count):
    return jnp.concatenate([ref[at : at + count, :], ref[at + count : at + 2 * count, :]], axis=1)


def read_pairs(ref, at, count):
    return [
        jnp.concatenate([ref[at + i : at + i + 1, :], ref[at + count + i : at + count + i + 1, :]], axis=1)
        for i in range(count)
    ]


def send_kernel(n, fields, msg, other, ext_in, ext, edge_out, near_out):
    sub, tile = lax.axis_index("sub"), lax.axis_index("tile")
    cols = ext.shape[1]
    high = ext.shape[0] // fields
    rows = high - 8
    for i in range(fields):
        base = high * i
        strip = halo_rows(n, other, i, cols)
        ext[base : base + rows, :] = ext_in[base : base + rows, :]
        ext[base + rows : base + high, :] = jnp.zeros((8, cols), F32)
        ext[base + rows : base + rows + HALO, :] = jnp.where(sub == 0, strip, 0.0)
        ext[base + high - HALO : base + high, :] = jnp.where(sub == 0, 0.0, strip)
    slots, count = fold_slots(high, cols, fields)
    tile_at, at = slots[-1]
    place = fold_place(cols) // (2 * HALO)
    tiles = [other[4 * n + 16 : 4 * n + 24, cols * k : cols * (k + 1)] for k in range(count)]
    for i in range(fields):
        strip = halo_rows(n, msg, i, cols)
        blank = jnp.zeros((8 - 2 * HALO, cols), F32)
        rows_beyond = [jnp.where(sub == 1, strip, 0.0), blank, jnp.where(sub == 1, 0.0, strip)]
        slot = at * fields + i
        moved = pltpu.roll(jnp.concatenate(rows_beyond, axis=0), 2 * HALO * slot, 1)
        tiles[tile_at] = jnp.where(place == slot, moved, tiles[tile_at])
    edges = jnp.concatenate(tiles, axis=0)
    fold = edges.shape[0]
    edge_out[...] = edges
    near_out[0:fold, :] = edges
    near = tile ^ 1
    air = table_rows(n, msg, other, near, 1 - sub, sub) + value_rows(n, msg, other, sub)
    write_pairs(near_out, fold, air)
    at = fold + 20
    for step in range(2, n, 2):
        write_pairs(near_out, at, table_rows(n, msg, other, near ^ step, sub, sub))
        at += 8
    near_out[at : near_out.shape[0], :] = jnp.zeros((near_out.shape[0] - at, cols), F32)


def side_kernel(levels, ext, *refs):
    warm, shares, marine, marine_weight = refs[:4]
    block, strips, surface, block_heat, share_rows, marine_out, marine_weight_out = refs[4:11]
    warm_in, shares_in, sems = refs[11:]
    pairs = [(warm, warm_in), (shares, shares_in), (marine, marine_out), (marine_weight, marine_weight_out)]
    copies = [pltpu.make_async_copy(a, b, sems.at[i]) for i, (a, b) in enumerate(pairs)]
    for copy in copies:
        copy.start()
    rows, cols = surface.shape
    high = rows + 8
    fields = [ext[high * i : high * (i + 1), :] for i in range(levels + 1)]
    for z, x in enumerate(diffused(fields[levels], fields[:levels])):
        block[z] = x[:rows]
    strips[0:high, :] = own_strips(fields[:levels])
    strips[high : 2 * high, :] = own_strips([fields[levels]] * levels)
    for copy in copies:
        copy.wait()
    surface[...] = sum(shares_in[z] * warm_in[z] for z in range(levels))
    block_heat[...] = sum(shares_in[z] * block[z] for z in range(levels))
    for z in range(levels):
        share_rows[z : z + 1, :] = jnp.full((1, cols), shares_in[z], F32)


def diffuse_kernel(n, levels, *refs):
    ext, near_in, edge_in, surface, share_rows, msg, other, marine, block_heat, strips = refs[:10]
    strip_out, lev_out = refs[10:12]
    sub, tile = lax.axis_index("sub"), lax.axis_index("tile")
    rows, cols = surface.shape
    high = rows + 8
    fold = edge_in.shape[0]
    own_values = value_rows(n, msg, other, sub)
    near_values = read_pairs(near_in, fold, 10)[4:]
    for i, out in enumerate(refs[12:]):
        air = table_rows(n, msg, other, tile ^ (2 * i + 2), 1 - sub, sub) + own_values
        air += read_pairs(near_in, fold + 20 + 8 * i, 4) + near_values
        write_pairs(out, 0, air)
    even = tile % 2 == 0
    lane = lax.broadcasted_iota(jnp.int32, (8, cols), 1)
    tiles = []
    for k in range(0, fold, 8):
        near, far = near_in[k : k + 8, :], edge_in[k : k + 8, :]
        right = jnp.where(tile < n - 1, jnp.where(even, near, far), 0.0)
        left = jnp.where(tile > 0, jnp.where(even, far, near), 0.0)
        tiles.append(jnp.where(lax.rem(lane, 2 * HALO) < HALO, right, turn_lanes(left, 2 * HALO)))
    wet = strips_beyond(tiles, strips[high : 2 * high, :], [levels] * levels, levels + 1)
    strip = strips_beyond(tiles, strips[0:high, :], list(range(levels)), levels + 1)
    strip = diffused(wet, [strip])[0][:rows]
    own_wet = ext[high * levels : high * levels + rows, :]
    strip_out[...] = strip
    heat = share_rows[0:1, :] * strip
    for z in range(1, levels):
        heat += share_rows[z : z + 1, :] * turn_lanes(strip, strip_base(0) - strip_base(z))
    heat = from_strips(heat, 0, block_heat[...])
    lev_out[0:rows, :] = surface[...]
    lev_out[rows : 2 * rows, :] = own_wet * heat
    if lev_out.shape[0] > 2 * rows:
        write_halves(lev_out, 2 * rows, marine[...].astype(F32))


def bulk_adjoint(warmth_gap, flux_sens):
    transfer_rate = jnp.full_like(warmth_gap, TRANSFER)
    rates = [transfer_rate]
    slopes = []
    for sweep_index in range(BULK_ITERS):
        bent = jnp.tanh(transfer_rate * warmth_gap)
        slopes.append(TRANSFER * STABILITY * (1.0 - bent * bent))
        transfer_rate = TRANSFER * (1.0 + STABILITY * bent)
        rates.append(transfer_rate)
    contrast_sens = transfer_rate * flux_sens
    rate_sens = warmth_gap * flux_sens
    for sweep_index in reversed(range(BULK_ITERS)):
        inner_sens = rate_sens * slopes[sweep_index]
        contrast_sens = contrast_sens + inner_sens * rates[sweep_index]
        rate_sens = inner_sens * warmth_gap
    return contrast_sens


def onehot(index, count):
    cells = lax.broadcasted_iota(jnp.int32, (count, index.shape[1]), 0)
    return jnp.where(cells == index, 1.0, 0.0).astype(BF16)


def dot(a, b, ca, cb):
    return lax.dot_general(a, b, (((ca,), (cb,)), ((), ())), preferred_element_type=F32)


def turned(x):
    return x.astype(F32).T.astype(BF16)


def look_up(air, at, picks, tables, uppers, turn=False):
    cols = tables.shape[2] if turn else tables.shape[1]
    for band in range(2):
        cell = air[band].astype(jnp.int32)
        hot = onehot(lax.rem(cell, cols), cols)
        tables[at + band] = turned(hot) if turn else hot
        values = [air[4 + band], air[6 + band], air[8 + band]]
        values = jnp.concatenate([x[:, :cols] for x in values] + [x[:, cols:] for x in values], axis=0)
        found = dot(jnp.concatenate(halves(values), axis=0), hot, 1, 0)
        found = found[0:6] + found[6:12]
        upper = cell >= cols
        found = jnp.where(upper, found[3:6], found[0:3])
        place = slice(at + band, at + band + 1)
        picks[0, place, :] = found[0:1]
        picks[1, place, :] = found[1:2]
        picks[2, place, :] = air[2 + band] * found[2:3]
        uppers[place, :] = upper.astype(F32)


def near_kernel(n, fold, msg, other, near_in, ext, block, strip, picks, tables, uppers, adjoint):
    sub, tile = lax.axis_index("sub"), lax.axis_index("tile")
    own = table_rows(n, msg, other, tile, sub, sub) + value_rows(n, msg, other, sub)
    look_up(own, 0, picks, tables, uppers, True)
    look_up(read_pairs(near_in, fold, 10), 2, picks, tables, uppers, True)
    levels, rows, cols = adjoint.shape
    own_wet = ext[(rows + 8) * levels : (rows + 8) * levels + rows, :]
    for z in range(levels):
        adjoint[z] = own_wet * from_strips(strip[...], z, block[z])


def slot_kernel(n, count, rows, *refs):
    lev_parts, refs = refs[:count], refs[count:]
    near_picks, near_tables, near_uppers, marine, weight = refs[:5]
    far_in, refs = refs[5 : 4 + n // 2], refs[4 + n // 2 :]
    values_out, wind_out, uppers, tables, chip_out, held, picks = refs
    sub, tile = lax.axis_index("sub"), lax.axis_index("tile")
    cols = chip_out.shape[1]
    picks[:, 0:4, :] = near_picks[...]
    uppers[0:4, :] = near_uppers[0:4, :]
    for i, ref in enumerate(far_in):
        air = read_pairs(ref, 0, 20)
        for j in range(2):
            look_up(air[10 * j : 10 * j + 10], 4 * i + 4 + 2 * j, picks, tables, uppers)
    table = sum(ref[0 : 2 * rows, :] for ref in lev_parts)
    table = jnp.concatenate(halves(table), axis=1)
    for step in range(n):
        for band in range(2):
            at, place = 2 * step + band, 2 * (tile ^ step) + band
            cell = marine[pl.ds(place, 1), :]
            row, col = cell // cols, lax.rem(cell, cols)
            col_hot = onehot(col, cols)
            spread = dot(table, jnp.concatenate([col_hot, col_hot], axis=0), 1, 0)
            row_mask = lax.broadcasted_iota(jnp.int32, (rows, cell.shape[1]), 0) == row
            for i in range(2):
                piece = jnp.where(row_mask, spread[rows * i : rows * (i + 1)], 0.0)
                held[i, at : at + 1, :] = jnp.sum(piece, axis=0, keepdims=True)
            held[2, at : at + 1, :] = weight[pl.ds(place, 1), :]

    difference = held[0] - picks[0]
    wind = picks[1]
    flux_sens = held[2] * held[1] + picks[2]
    contrast_sens = bulk_adjoint(wind * difference, flux_sens)
    surface_sens = contrast_sens * wind
    wind_sens = contrast_sens * difference
    values_out[...] = surface_sens
    wind_out[...] = wind_sens
    if n == 4:
        sums = functools.partial(air_sums, values_out, wind_out, uppers, near_tables, tables)
        write_halves(chip_out, 8, surface_sens)
        chip_out[24:40, :] = lev_parts[-1][2 * rows : 2 * rows + 16, :]

        lead = leads()

        @pl.when(lead)
        def _():
            chip_out[0:8, :] = sums(2)
            chip_out[8:16, :] = sums(1)

        @pl.when(jnp.logical_not(lead))
        def _():
            chip_out[0:8, :] = sums(3)


def leads():
    tile = lax.axis_index("tile")
    return (lax.axis_index("sub") == 1) != ((tile == 1) | (tile == 2))


def air_sums(values, winds, uppers, near_tables, tables, step):
    rows = [None] * 4
    for band in range(2):
        at = 2 * step + band
        near = at < 4
        hot = near_tables[at] if near else tables[at]
        place = slice(at, at + 1)
        upper = uppers[place, :]
        both = jnp.concatenate([values[place, :], winds[place, :]], axis=0)
        both = jnp.concatenate([both * (1.0 - upper), both * upper], axis=0)
        sums = dot(jnp.concatenate(halves(both), axis=0), hot, 1, 0 if near else 1)
        sums = sums[0:4] + sums[4:8]
        rows[band], rows[2 + band] = sums[0:2], sums[2:4]
    return jnp.concatenate(rows, axis=0)


def kept_kernel(n, values, winds, uppers, near_tables, tables, *returns):
    sums = functools.partial(air_sums, values, winds, uppers, near_tables, tables)
    if n != 4:
        for step in range(n):
            returns[step][...] = sums(step)
        return
    lead = leads()
    own, first, second = returns
    own[...] = sums(0)

    @pl.when(lead)
    def _():
        first[...] = sums(3)
        second[...] = jnp.zeros_like(second)

    @pl.when(jnp.logical_not(lead))
    def _():
        first[...] = sums(2)
        second[...] = sums(1)


def scatter(n, rows, cols, tile, cell_of, value_of, col_hot_of=None):
    total = jnp.zeros((2 * rows, cols), F32)
    for step in range(n):
        for band in range(2):
            at = 2 * step + band
            cell = cell_of(2 * (tile ^ step) + band)
            row, col = cell // cols, lax.rem(cell, cols)
            row_mask = lax.broadcasted_iota(jnp.int32, (rows, cell.shape[1]), 0) == row
            spread = jnp.concatenate(
                [jnp.where(row_mask, x.astype(F32), 0.0).astype(BF16) for x in halves(value_of(at))],
                axis=0,
            )
            if col_hot_of:
                total += dot(spread, col_hot_of(at), 1, 0)
            else:
                total += dot(spread, onehot(col, cols), 1, 1)
    return total[:rows] + total[rows:]


def own_kernel(n, marine, values, *refs):
    tile = lax.axis_index("tile")
    if len(refs) > 1:
        lev_in, theirs, out, cells, tables = refs
        rows, cols = out.shape

        @pl.when(leads())
        def _():
            for band, (ref, at) in enumerate(((lev_in, 2 * rows), (theirs, 24))):
                cells[2 * n * band : 2 * n * (band + 1), :] = read_halves(ref, at, 2 * n).astype(jnp.int32)
                for i in range(2 * n):
                    place = 2 * n * band + 2 * (tile ^ (i // 2)) + i % 2
                    col = lax.rem(cells[pl.ds(place, 1), :], cols)
                    tables[2 * n * band + i] = turned(onehot(col, cols))

    out = refs[2] if len(refs) > 1 else refs[0]
    rows, cols = out.shape
    out[...] = scatter(
        n, rows, cols, tile, lambda i: marine[pl.ds(i, 1), :], lambda i: values[i : i + 1, :]
    )


def partner_part(n, band, second, cells, tables, values, shape):
    rows, cols = shape
    base = 2 * n * band
    values[...] = read_halves(second, 4 * n * band, 2 * n)
    return scatter(
        n,
        rows,
        cols,
        lax.axis_index("tile"),
        lambda i: cells[pl.ds(base + i, 1), :],
        lambda i: values[i : i + 1, :],
        lambda i: tables[base + i],
    )


def post_kernel(n, first, second, own, cells, tables, out, second_out, values):
    lead = leads()
    rows, cols = out.shape[0] - 8, out.shape[1]
    out[0:8, :] = first[0:8, :] + own[...] + jnp.where(lead, 0.0, second[0:8, :])
    second_out[...] = second[...]

    @pl.when(lead)
    def _():
        out[8 : rows + 8, :] = partner_part(n, 1, second, cells, tables, values, (rows, cols))

    @pl.when(jnp.logical_not(lead))
    def _():
        out[8 : rows + 8, :] = jnp.zeros((rows, cols), F32)


def gradient_kernel(n, second, slots, cells, tables, gradient, values):
    gradient[...] = slots[...]

    @pl.when(leads())
    def _():
        gradient[...] += partner_part(n, 0, second, cells, tables, values, gradient.shape)


def merge_kernel(values, kept_first, kept_second, theirs, first, second):
    first[...] = jnp.zeros_like(first)
    first[0:8, :] = kept_first[...] + theirs[0:8, :]
    write_halves(second, 0, values[...])
    second[0:8, :] = jnp.where(leads(), second[0:8, :], kept_second[...] + theirs[8:16, :])
    second[16:32, :] = theirs[8:24, :]


def final_kernel(merged, slots, adjoint, share_rows, sums, other, *refs):
    state_out, air_out, wind_out, state, air, wind, sems = refs
    sub = lax.axis_index("sub")
    gradient = slots[...]
    if merged:
        gradient += jnp.where(leads(), 0.0, other[8 : slots.shape[0] + 8, :])
    for z in range(adjoint.shape[0]):
        state[z] = adjoint[z] + share_rows[z : z + 1, :] * gradient
    copies = [pltpu.make_async_copy(state, state_out, sems.at[0])]
    copies[0].start()
    both = sums[0:8, :] + other[0:8, :]
    own = [jnp.where(sub == 0, both[i : i + 2], both[i + 2 : i + 4]) for i in (0, 4)]
    own = jnp.concatenate(own, axis=1)
    air[...] = -own[0:1]
    wind[...] = own[1:2]
    for i, (a, b) in enumerate(((air, air_out), (wind, wind_out))):
        copies.append(pltpu.make_async_copy(a, b, sems.at[1 + i]))
        copies[-1].start()
    for copy in copies:
        copy.wait()


def traded(x, step, swap=0):
    n, bands = lax.axis_size("tile"), lax.axis_size("sub")
    pairs = [
        (t * bands + s, (t ^ step) * bands + (s ^ swap)) for t in range(n) for s in range(bands)
    ]
    return lax.ppermute(x, ("tile", "sub"), pairs)


def beyond(x):
    n, bands = lax.axis_size("tile"), lax.axis_size("sub")
    pairs = []
    for t in range(n):
        to = t if t in (0, n - 1) else ((t + 1) ^ 1) - 1
        pairs += [(t * bands + s, to * bands + (s ^ 1)) for s in range(bands)]
    return lax.ppermute(x, ("tile", "sub"), pairs)


def by_role(x, lead, rest):
    n, levs, bands = (lax.axis_size(axis) for axis in ("tile", "lev", "sub"))

    def place(t, l, is_lead):
        return (t * levs + l) * bands + (is_lead if t in (0, n - 1) else 1 - is_lead)

    pairs = []
    for t in range(n):
        for l in range(levs):
            for is_lead, (tx, lx) in enumerate((rest, lead)):
                pairs.append((place(t, l, is_lead), place(t ^ tx, l ^ lx, is_lead)))
    return lax.ppermute(x, ("tile", "lev", "sub"), pairs)


def lev_parts(x):
    if lax.axis_size("lev") == 2:
        return [x, lax.ppermute(x, "lev", [(0, 1), (1, 0)])]
    return [lax.psum(x, "lev")]


def per_device(
    marine_layered_warmth,
    bottom_sky_warmth,
    bottom_breeze_magnitude,
    depth_shares,
    piece_sky_box,
    sky_share_fraction,
    piece_marine_box,
    marine_share_fraction,
    marine_indicator,
    marine_result_adjoint,
    energy_transport_adjoint,
):
    n, levs = lax.axis_size("tile"), lax.axis_size("lev")
    levels, rows, cols = marine_layered_warmth.shape
    cells = bottom_sky_warmth.shape[0]
    high = rows + 8
    def pinned(*arrays):
        return [pltpu.with_memory_space_constraint(x, pltpu.HBM) for x in arrays]

    def like(x):
        return jax.ShapeDtypeStruct(x.shape, x.dtype)

    def buffers(arrays):
        return [pltpu.VMEM(x.shape, x.dtype) for x in arrays]

    air = [
        x.reshape(1, cells)
        for x in (bottom_sky_warmth, bottom_breeze_magnitude, energy_transport_adjoint)
    ]
    raw = pinned(
        marine_result_adjoint, marine_indicator, *air, piece_sky_box[0], sky_share_fraction[0]
    )
    msg, ext = call(
        functools.partial(pack_kernel, n),
        [(4 * n + 24, cells), ((levels + 1) * high, cols)],
        raw,
        [HBM] * len(raw),
        scratch=buffers(raw[1:]) + [pltpu.SemaphoreType.DMA((len(raw) - 1 + levels,))],
    )
    other = traded(msg, 0, 1)
    fold = 8 * fold_slots(high, cols, levels + 1)[1]
    ext, edge_out, near_out = call(
        functools.partial(send_kernel, n, levels + 1),
        [ext.shape, (fold, cols), ((fold + 20 + 4 * (n - 2) + 7) // 8 * 8, cols)],
        [msg, other, ext],
    )
    edge_in = beyond(edge_out)
    near_in = traded(near_out, 1, 1)
    raw = pinned(marine_layered_warmth, depth_shares, piece_marine_box[0], marine_share_fraction[0])
    block, strips, surface, block_heat, share_rows, marine, marine_weight = call(
        functools.partial(side_kernel, levels),
        [(levels, rows, cols), (2 * high, cols)]
        + [(rows, cols)] * 2
        + [(8, cols), like(raw[2]), like(raw[3])],
        [ext, *raw],
        [VMEM] + [HBM] * 4,
        scratch=buffers(raw[:1])
        + [pltpu.SMEM(depth_shares.shape, F32), pltpu.SemaphoreType.DMA((4,))],
    )
    merged = n == 4 and levs == 2
    strip, lev_msg, *far_out = call(
        functools.partial(diffuse_kernel, n, levels),
        [(rows, cols), (2 * rows + (16 if merged else 0), cols)] + [(40, cols)] * (n // 2 - 1),
        [ext, near_in, edge_in, surface, share_rows, msg, other, marine, block_heat, strips],
    )
    lev_in = lev_parts(lev_msg)
    far_in = [traded(x, 2 * i + 2, 1) for i, x in enumerate(far_out)]
    picks, tables, uppers, adjoint = call(
        functools.partial(near_kernel, n, fold),
        [(3, 4, cells), jax.ShapeDtypeStruct((4, cells, cols), BF16), (8, cells)]
        + [(levels, rows, cols)],
        [msg, other, near_in, ext, block, strip],
    )
    values, winds, uppers, far_tables, chip = call(
        functools.partial(slot_kernel, n, len(lev_in), rows),
        [(2 * n, cells)] * 3
        + [jax.ShapeDtypeStruct((2 * n, cols, cells), BF16), (40, cols)],
        [*lev_in, picks, tables, uppers, marine, marine_weight, *far_in],
        scratch=[pltpu.VMEM((3, 2 * n, cells), F32)] * 2,
    )
    returns = call(
        functools.partial(kept_kernel, n),
        [(8, cols)] * (3 if merged else n),
        [values, winds, uppers, tables, far_tables],
    )
    if merged:
        theirs = traded(chip, 0, 1)
        slots, partner_cells, partner_tables = call(
            functools.partial(own_kernel, n),
            [(rows, cols), jax.ShapeDtypeStruct((4 * n, cells), jnp.int32)]
            + [jax.ShapeDtypeStruct((4 * n, cells, cols), BF16)],
            [marine, values, lev_in[1], theirs],
        )
        first, second = call(
            merge_kernel, [(32, cols), (32, cols)], [values, *returns[1:], theirs]
        )
        first = by_role(first, (3, 0), (2, 0))
        second = by_role(second, (0, 1), (1, 0))
        scratch = [pltpu.VMEM((2 * n, cells), F32)]
        sums, second = call(
            functools.partial(post_kernel, n),
            [(rows + 8, cols), (32, cols)],
            [first, second, returns[0], partner_cells, partner_tables],
            scratch=scratch,
        )
        (gradient,) = call(
            functools.partial(gradient_kernel, n),
            [(rows, cols)],
            [second, slots, partner_cells, partner_tables],
            scratch=scratch,
        )
    else:
        (slots,) = call(functools.partial(own_kernel, n), [(rows, cols)], [marine, values])
        gradient = sum(lev_parts(slots))
        sums = returns[0]
        for step in range(1, n):
            sums = sums + traded(returns[step], step, 1)
    results = [(levels, rows, cols), (1, cells), (1, cells)]
    state, air_gradient, wind_gradient = call(
        functools.partial(final_kernel, merged),
        results,
        [gradient, adjoint, share_rows, sums, traded(sums, 0, 1)],
        out_specs=[HBM] * 3,
        scratch=[pltpu.VMEM(x, F32) for x in results] + [pltpu.SemaphoreType.DMA((3,))],
    )
    return (state, air_gradient.reshape(cells), wind_gradient.reshape(cells))


def solution(mesh):
    return jax.shard_map(
        per_device,
        mesh=mesh,
        in_specs=(
            P(("ens", "lev"), "sub", "tile"),
            P(("ens", "tile", "lev", "sub")),
            P(("ens", "tile", "lev", "sub")),
            P("lev"),
            P(("tile", "lev", "sub"), None, None),
            P(("tile", "lev", "sub"), None, None),
            P(("tile", "lev", "sub"), None, None),
            P(("tile", "lev", "sub"), None, None),
            P("sub", "tile"),
            P(("ens", "lev"), "sub", "tile"),
            P(("ens", "tile", "lev", "sub")),
        ),
        out_specs=(
            P(("ens", "lev"), "sub", "tile"),
            P(("ens", "tile", "lev", "sub")),
            P(("ens", "tile", "lev", "sub")),
        ),
        check_vma=False,
    )
```

```python
import functools

import jax
import jax.numpy as jnp
from jax import lax
from jax.experimental import pallas as pl
from jax.experimental.pallas import tpu as pltpu
from jax.sharding import PartitionSpec as P

BULK_ITERS = 3
STEPS = 3
HALO = STEPS
MIXING = 0.2
TRANSFER = 1.0
STABILITY = 0.5
F32 = jnp.float32
BF16 = jnp.bfloat16
VMEM = pl.BlockSpec(memory_space=pltpu.VMEM)
HBM = pl.BlockSpec(memory_space=pltpu.HBM)


def call(kernel, outs, operands, specs=None, out_specs=None, scratch=(), aliases=None):
    outs = [jax.ShapeDtypeStruct(x, F32) if isinstance(x, tuple) else x for x in outs]
    return pl.pallas_call(
        kernel,
        out_shape=outs,
        in_specs=specs or [VMEM] * len(operands),
        out_specs=out_specs or [VMEM] * len(outs),
        scratch_shapes=list(scratch),
        input_output_aliases=aliases or {},
        compiler_params=pltpu.CompilerParams(vmem_limit_bytes=24 * 1024 * 1024),
    )(*operands)


def halves(x):
    high = x.astype(BF16)
    low = (x - high.astype(F32)).astype(BF16)
    return high, low


def fold_place(cols):
    lane = lax.broadcasted_iota(jnp.int32, (8, cols), 1)
    return lax.rem(lane + HALO, cols)


def fold_slots(high, cols, fields):
    each = cols // (2 * HALO * fields)
    groups = high // 8
    return [(g // each, g % each) for g in range(groups)], -(-groups // each)


def folded(ext, high, fields):
    cols = ext.shape[1]
    place = fold_place(cols) // (2 * HALO)
    slots, tiles = fold_slots(high, cols, fields)
    out = [jnp.zeros((8, cols), F32)] * tiles
    for g, (k, at) in enumerate(slots):
        for i in range(fields):
            slot = at * fields + i
            rows = ext[high * i + 8 * g : high * i + 8 * g + 8, :]
            moved = pltpu.roll(rows, 2 * HALO * slot, 1) if slot else rows
            out[k] = jnp.where(place == slot, moved, out[k])
    return jnp.concatenate(out, axis=0)


def strip_base(z):
    return 6 * HALO * z - 4 * HALO


def lanes_from(shape, first, count):
    lane = lax.broadcasted_iota(jnp.int32, shape, 1)
    return lax.rem(lane + (-first) % shape[1], shape[1]) < count


def turn_lanes(x, by):
    by = by % x.shape[1]
    return pltpu.roll(x, by, 1) if by else x


def own_strips(fields):
    width = 2 * HALO
    cols = fields[0].shape[1]
    out = jnp.zeros_like(fields[0])
    for z, x in enumerate(fields):
        base = strip_base(z)
        out = jnp.where(lanes_from(x.shape, base, width), turn_lanes(x, base + width), out)
        out = jnp.where(lanes_from(x.shape, base + 2 * width, width), turn_lanes(x, base + 2 * width), out)
    return out


def strips_beyond(tiles, own, fields, count):
    width = 2 * HALO
    high, cols = own.shape
    out = []
    for g, (k, at) in enumerate(fold_slots(high, cols, count)[0]):
        x = own[8 * g : 8 * g + 8]
        for z, i in enumerate(fields):
            base = strip_base(z) + width
            moved = turn_lanes(tiles[k], base - width * (at * count + i))
            x = jnp.where(lanes_from(x.shape, base, width), moved, x)
        out.append(x)
    return jnp.concatenate(out, axis=0)


def from_strips(strip, z, block):
    shape = block.shape
    first, last = lanes_from(shape, 0, HALO), lanes_from(shape, -HALO, HALO)
    block = jnp.where(first, turn_lanes(strip, -strip_base(z) - 4 * HALO), block)
    return jnp.where(last, turn_lanes(strip, -strip_base(z) - 2 * HALO), block)


def around(x):
    high, cols = x.shape
    return pltpu.roll(x, 1, 0) + pltpu.roll(x, high - 1, 0) + pltpu.roll(x, 1, 1) + pltpu.roll(x, cols - 1, 1)


def diffused(wet, fields):
    keep = wet * (1.0 - MIXING * around(wet))
    mix = MIXING * wet
    out = []
    for v in fields:
        v = wet * v
        for sweep_index in range(STEPS):
            v = keep * v + mix * around(v)
        out.append(v)
    return out


def pack_kernel(n, *refs):
    cot, sea, sky, breeze, energy, sky_index, sky_weight, msg, ext = refs[:9]
    sea_in, sky_in, breeze_in, energy_in, index_in, weight_in, sems = refs[9:]
    rows, cols = sea.shape
    levels = cot.shape[0]
    high = rows + 8
    pairs = [(cot.at[z], ext.at[pl.ds(high * z, rows)]) for z in range(levels)]
    pairs += [(sea, sea_in), (sky_index, index_in), (sky_weight, weight_in)]
    pairs += [(sky, sky_in), (breeze, breeze_in), (energy, energy_in)]
    copies = [pltpu.make_async_copy(a, b, sems.at[i]) for i, (a, b) in enumerate(pairs)]
    for copy in copies:
        copy.start()
    sub = lax.axis_index("sub")
    msg[...] = jnp.zeros_like(msg)
    for z in range(levels + 1):
        ext[high * z + rows : high * (z + 1), :] = jnp.zeros((8, cols), F32)
    for copy in copies:
        copy.wait()
    ext[high * levels : high * levels + rows, :] = sea_in[...].astype(F32)
    msg[0 : 2 * n, :] = index_in[...].astype(F32)
    msg[2 * n : 4 * n, :] = weight_in[...]
    for i, ref in enumerate((sky_in, breeze_in, energy_in)):
        msg[4 * n + i : 4 * n + i + 1, :] = ref[...]
    base = 4 * n + 8
    for i in range(levels + 1):
        at, top, left = high * i, base + HALO * (i // 2), cols * (i % 2)
        outer = jnp.where(sub == 0, ext[at + rows - HALO : at + rows], ext[at : at + HALO])
        msg[top : top + HALO, left : left + cols] = outer
    edges = folded(ext, high, levels + 1)
    for k in range(2):
        msg[4 * n + 16 : 4 * n + 24, cols * k : cols * (k + 1)] = edges[8 * k : 8 * k + 8]


def halo_rows(n, msg, i, cols):
    top, left = 4 * n + 8 + HALO * (i // 2), cols * (i % 2)
    return msg[top : top + HALO, left : left + cols]


def both_bands(msg, other, index, sub):
    own, far = msg[pl.ds(index, 1), :], other[pl.ds(index, 1), :]
    return [jnp.where(sub == 0, own, far), jnp.where(sub == 0, far, own)]


def table_rows(n, msg, other, target, band, sub):
    row = 2 * target + band
    return both_bands(msg, other, row, sub) + both_bands(msg, other, 2 * n + row, sub)


def value_rows(n, msg, other, sub):
    return [x for i in range(3) for x in both_bands(msg, other, 4 * n + i, sub)]


def write_pairs(out, at, rows):
    cols = out.shape[1]
    for i, row in enumerate(rows):
        out[at + i : at + i + 1, :] = row[:, :cols]
        out[at + len(rows) + i : at + len(rows) + i + 1, :] = row[:, cols:]


def write_halves(out, at, x):
    count, cols = x.shape[0], out.shape[1]
    out[at : at + count, :] = x[:, :cols]
    out[at + count : at + 2 * count, :] = x[:, cols:]


def read_halves(ref, at, count):
    return jnp.concatenate([ref[at : at + count, :], ref[at + count : at + 2 * count, :]], axis=1)


def read_pairs(ref, at, count):
    return [
        jnp.concatenate([ref[at + i : at + i + 1, :], ref[at + count + i : at + count + i + 1, :]], axis=1)
        for i in range(count)
    ]


def send_kernel(n, fields, msg, other, ext_in, ext, edge_out, near_out):
    sub, tile = lax.axis_index("sub"), lax.axis_index("tile")
    cols = ext.shape[1]
    high = ext.shape[0] // fields
    rows = high - 8
    for i in range(fields):
        base = high * i
        strip = halo_rows(n, other, i, cols)
        ext[base : base + rows, :] = ext_in[base : base + rows, :]
        ext[base + rows : base + high, :] = jnp.zeros((8, cols), F32)
        ext[base + rows : base + rows + HALO, :] = jnp.where(sub == 0, strip, 0.0)
        ext[base + high - HALO : base + high, :] = jnp.where(sub == 0, 0.0, strip)
    slots, count = fold_slots(high, cols, fields)
    tile_at, at = slots[-1]
    place = fold_place(cols) // (2 * HALO)
    tiles = [other[4 * n + 16 : 4 * n + 24, cols * k : cols * (k + 1)] for k in range(count)]
    for i in range(fields):
        strip = halo_rows(n, msg, i, cols)
        blank = jnp.zeros((8 - 2 * HALO, cols), F32)
        rows_beyond = [jnp.where(sub == 1, strip, 0.0), blank, jnp.where(sub == 1, 0.0, strip)]
        slot = at * fields + i
        moved = pltpu.roll(jnp.concatenate(rows_beyond, axis=0), 2 * HALO * slot, 1)
        tiles[tile_at] = jnp.where(place == slot, moved, tiles[tile_at])
    edges = jnp.concatenate(tiles, axis=0)
    fold = edges.shape[0]
    edge_out[...] = edges
    near_out[0:fold, :] = edges
    near = tile ^ 1
    air = table_rows(n, msg, other, near, 1 - sub, sub) + value_rows(n, msg, other, sub)
    write_pairs(near_out, fold, air)
    at = fold + 20
    for step in range(2, n, 2):
        write_pairs(near_out, at, table_rows(n, msg, other, near ^ step, sub, sub))
        at += 8
    near_out[at : near_out.shape[0], :] = jnp.zeros((near_out.shape[0] - at, cols), F32)


def side_kernel(levels, ext, *refs):
    warm, shares, marine, marine_weight = refs[:4]
    block, strips, heat_strips, surface, block_heat, share_rows, marine_out, marine_weight_out = refs[4:12]
    warm_in, shares_in, sems = refs[12:]
    pairs = [(warm, warm_in), (shares, shares_in), (marine, marine_out), (marine_weight, marine_weight_out)]
    copies = [pltpu.make_async_copy(a, b, sems.at[i]) for i, (a, b) in enumerate(pairs)]
    for copy in copies:
        copy.start()
    rows, cols = surface.shape
    high = rows + 8
    fields = [ext[high * i : high * (i + 1), :] for i in range(levels + 1)]
    for z, x in enumerate(diffused(fields[levels], fields[:levels])):
        block[z] = x[:rows]
    strips[0:high, :] = own_strips(fields[:levels])
    strips[high : 2 * high, :] = own_strips([fields[levels]] * levels)
    for copy in copies:
        copy.wait()
    surface[...] = sum(shares_in[z] * warm_in[z] for z in range(levels))
    block_heat[...] = sum(shares_in[z] * block[z] for z in range(levels))
    mixed = sum(shares_in[z] * fields[z] for z in range(levels))
    heat_strips[0:high, :] = own_strips([mixed])
    heat_strips[high : 2 * high, :] = own_strips(fields[levels:])
    for z in range(levels):
        share_rows[z : z + 1, :] = jnp.full((1, cols), shares_in[z], F32)


def diffuse_kernel(n, levels, *refs):
    ext, near_in, edge_in, surface, share_rows, msg, other, marine, block_heat, strips = refs[:10]
    fold_out, lev_out = refs[10:12]
    sub, tile = lax.axis_index("sub"), lax.axis_index("tile")
    rows, cols = surface.shape
    high = rows + 8
    fold = edge_in.shape[0]
    own_values = value_rows(n, msg, other, sub)
    near_values = read_pairs(near_in, fold, 10)[4:]
    for i, out in enumerate(refs[12:]):
        air = table_rows(n, msg, other, tile ^ (2 * i + 2), 1 - sub, sub) + own_values
        air += read_pairs(near_in, fold + 20 + 8 * i, 4) + near_values
        write_pairs(out, 0, air)
    even = tile % 2 == 0
    lane = lax.broadcasted_iota(jnp.int32, (8, cols), 1)
    tiles = []
    for k in range(0, fold, 8):
        near, far = near_in[k : k + 8, :], edge_in[k : k + 8, :]
        right = jnp.where(tile < n - 1, jnp.where(even, near, far), 0.0)
        left = jnp.where(tile > 0, jnp.where(even, far, near), 0.0)
        tiles.append(jnp.where(lax.rem(lane, 2 * HALO) < HALO, right, turn_lanes(left, 2 * HALO)))
    fold_out[...] = jnp.concatenate(tiles, axis=0)
    mixed = []
    for x in tiles:
        shifted = [turn_lanes(x, -2 * HALO * z) for z in range(levels)]
        mixed.append(sum(share_rows[z : z + 1, :] * y for z, y in enumerate(shifted)))
    wet = strips_beyond(tiles, strips[high : 2 * high, :], [levels], levels + 1)
    heat = diffused(wet, [strips_beyond(mixed, strips[0:high, :], [0], levels + 1)])[0]
    heat = from_strips(heat[:rows], 0, block_heat[...])
    own_wet = ext[high * levels : high * levels + rows, :]
    lev_out[0:rows, :] = surface[...]
    lev_out[rows : 2 * rows, :] = own_wet * heat
    if lev_out.shape[0] > 2 * rows:
        write_halves(lev_out, 2 * rows, marine[...].astype(F32))


def bulk_adjoint(warmth_gap, flux_sens):
    transfer_rate = jnp.full_like(warmth_gap, TRANSFER)
    rates = [transfer_rate]
    slopes = []
    for sweep_index in range(BULK_ITERS):
        bent = jnp.tanh(transfer_rate * warmth_gap)
        slopes.append(TRANSFER * STABILITY * (1.0 - bent * bent))
        transfer_rate = TRANSFER * (1.0 + STABILITY * bent)
        rates.append(transfer_rate)
    contrast_sens = transfer_rate * flux_sens
    rate_sens = warmth_gap * flux_sens
    for sweep_index in reversed(range(BULK_ITERS)):
        inner_sens = rate_sens * slopes[sweep_index]
        contrast_sens = contrast_sens + inner_sens * rates[sweep_index]
        rate_sens = inner_sens * warmth_gap
    return contrast_sens


def onehot(index, count):
    cells = lax.broadcasted_iota(jnp.int32, (count, index.shape[1]), 0).astype(BF16)
    return jnp.where(cells == index.astype(BF16), jnp.ones((), BF16), jnp.zeros((), BF16))


def dot(a, b, ca, cb):
    return lax.dot_general(a, b, (((ca,), (cb,)), ((), ())), preferred_element_type=F32)


def turned(x):
    return x.astype(F32).T.astype(BF16)


def look_up(air, at, picks, tables, uppers, turn=False):
    cols = tables.shape[2] if turn else tables.shape[1]
    for band in range(2):
        cell = air[band].astype(jnp.int32)
        hot = onehot(lax.rem(cell, cols), cols)
        tables[at + band] = turned(hot) if turn else hot
        values = [air[4 + band], air[6 + band], air[8 + band]]
        values = jnp.concatenate([x[:, :cols] for x in values] + [x[:, cols:] for x in values], axis=0)
        found = dot(jnp.concatenate(halves(values), axis=0), hot, 1, 0)
        found = found[0:6] + found[6:12]
        upper = cell >= cols
        found = jnp.where(upper, found[3:6], found[0:3])
        place = slice(at + band, at + band + 1)
        picks[0, place, :] = found[0:1]
        picks[1, place, :] = found[1:2]
        picks[2, place, :] = air[2 + band] * found[2:3]
        uppers[place, :] = upper.astype(F32)


def near_kernel(n, fold, msg, other, near_in, ext, block, strips, folds, picks, tables, uppers, adjoint):
    sub, tile = lax.axis_index("sub"), lax.axis_index("tile")
    own = table_rows(n, msg, other, tile, sub, sub) + value_rows(n, msg, other, sub)
    look_up(own, 0, picks, tables, uppers, True)
    look_up(read_pairs(near_in, fold, 10), 2, picks, tables, uppers, True)
    levels, rows, cols = adjoint.shape
    high = rows + 8
    tiles = [folds[k : k + 8, :] for k in range(0, fold, 8)]
    wet = strips_beyond(tiles, strips[high : 2 * high, :], [levels] * levels, levels + 1)
    strip = strips_beyond(tiles, strips[0:high, :], list(range(levels)), levels + 1)
    strip = diffused(wet, [strip])[0][:rows]
    own_wet = ext[high * levels : high * levels + rows, :]
    for z in range(levels):
        adjoint[z] = own_wet * from_strips(strip, z, block[z])


def slot_kernel(n, count, rows, *refs):
    lev_parts, refs = refs[:count], refs[count:]
    near_picks, near_tables, near_uppers, marine, weight = refs[:5]
    far_in, refs = refs[5 : 4 + n // 2], refs[4 + n // 2 :]
    values_out, wind_out, uppers, tables, chip_out, held, picks = refs
    sub, tile = lax.axis_index("sub"), lax.axis_index("tile")
    cols = chip_out.shape[1]
    picks[:, 0:4, :] = near_picks[...]
    uppers[0:4, :] = near_uppers[0:4, :]
    for i, ref in enumerate(far_in):
        air = read_pairs(ref, 0, 20)
        for j in range(2):
            look_up(air[10 * j : 10 * j + 10], 4 * i + 4 + 2 * j, picks, tables, uppers)
    table = sum(ref[0 : 2 * rows, :] for ref in lev_parts)
    table = jnp.concatenate(halves(table), axis=1)
    for step in range(n):
        for band in range(2):
            at, place = 2 * step + band, 2 * (tile ^ step) + band
            cell = marine[pl.ds(place, 1), :]
            row, col = cell // cols, lax.rem(cell, cols)
            col_hot = onehot(col, cols)
            spread = dot(table, jnp.concatenate([col_hot, col_hot], axis=0), 1, 0)
            row_mask = lax.broadcasted_iota(jnp.int32, (rows, cell.shape[1]), 0) == row
            for i in range(2):
                piece = jnp.where(row_mask, spread[rows * i : rows * (i + 1)], 0.0)
                held[i, at : at + 1, :] = jnp.sum(piece, axis=0, keepdims=True)
            held[2, at : at + 1, :] = weight[pl.ds(place, 1), :]

    difference = held[0] - picks[0]
    wind = picks[1]
    flux_sens = held[2] * held[1] + picks[2]
    contrast_sens = bulk_adjoint(wind * difference, flux_sens)
    surface_sens = contrast_sens * wind
    wind_sens = contrast_sens * difference
    values_out[...] = surface_sens
    wind_out[...] = wind_sens
    if n == 4:
        sums = functools.partial(air_sums, values_out, wind_out, uppers, near_tables, tables)
        write_halves(chip_out, 8, surface_sens)
        chip_out[24:40, :] = lev_parts[-1][2 * rows : 2 * rows + 16, :]

        lead = leads()

        @pl.when(lead)
        def _():
            chip_out[0:8, :] = sums(2)
            chip_out[8:16, :] = sums(1)

        @pl.when(jnp.logical_not(lead))
        def _():
            chip_out[0:8, :] = sums(3)


def leads():
    tile = lax.axis_index("tile")
    return (lax.axis_index("sub") == 1) != ((tile == 1) | (tile == 2))


def air_sums(values, winds, uppers, near_tables, tables, step):
    rows = [None] * 4
    for band in range(2):
        at = 2 * step + band
        near = at < 4
        hot = near_tables[at] if near else tables[at]
        place = slice(at, at + 1)
        upper = uppers[place, :]
        both = jnp.concatenate([values[place, :], winds[place, :]], axis=0)
        both = jnp.concatenate([both * (1.0 - upper), both * upper], axis=0)
        sums = dot(jnp.concatenate(halves(both), axis=0), hot, 1, 0 if near else 1)
        sums = sums[0:4] + sums[4:8]
        rows[band], rows[2 + band] = sums[0:2], sums[2:4]
    return jnp.concatenate(rows, axis=0)


def kept_kernel(n, values, winds, uppers, near_tables, tables, *returns):
    sums = functools.partial(air_sums, values, winds, uppers, near_tables, tables)
    if n != 4:
        for step in range(n):
            returns[step][...] = sums(step)
        return
    lead = leads()
    own, first, second = returns
    own[...] = sums(0)

    @pl.when(lead)
    def _():
        first[...] = sums(3)
        second[...] = jnp.zeros_like(second)

    @pl.when(jnp.logical_not(lead))
    def _():
        first[...] = sums(2)
        second[...] = sums(1)


def scatter(n, rows, cols, tile, cell_of, value_of, col_hot_of=None):
    total = jnp.zeros((2 * rows, cols), F32)
    for step in range(n):
        for band in range(2):
            at = 2 * step + band
            cell = cell_of(2 * (tile ^ step) + band)
            row, col = cell // cols, lax.rem(cell, cols)
            row_mask = lax.broadcasted_iota(jnp.int32, (rows, cell.shape[1]), 0) == row
            spread = jnp.concatenate(
                [jnp.where(row_mask, x.astype(F32), 0.0).astype(BF16) for x in halves(value_of(at))],
                axis=0,
            )
            if col_hot_of:
                total += dot(spread, col_hot_of(at), 1, 0)
            else:
                total += dot(spread, onehot(col, cols), 1, 1)
    return total[:rows] + total[rows:]


def own_kernel(n, marine, values, *refs):
    tile = lax.axis_index("tile")
    if len(refs) > 1:
        lev_in, theirs, out, cells, tables = refs
        rows, cols = out.shape

        @pl.when(leads())
        def _():
            for band, (ref, at) in enumerate(((lev_in, 2 * rows), (theirs, 24))):
                cells[2 * n * band : 2 * n * (band + 1), :] = read_halves(ref, at, 2 * n).astype(jnp.int32)
                for i in range(2 * n):
                    place = 2 * n * band + 2 * (tile ^ (i // 2)) + i % 2
                    col = lax.rem(cells[pl.ds(place, 1), :], cols)
                    tables[2 * n * band + i] = turned(onehot(col, cols))

    out = refs[2] if len(refs) > 1 else refs[0]
    rows, cols = out.shape
    out[...] = scatter(
        n, rows, cols, tile, lambda i: marine[pl.ds(i, 1), :], lambda i: values[i : i + 1, :]
    )


def partner_part(n, band, second, cells, tables, values, shape):
    rows, cols = shape
    base = 2 * n * band
    values[...] = read_halves(second, 4 * n * band, 2 * n)
    return scatter(
        n,
        rows,
        cols,
        lax.axis_index("tile"),
        lambda i: cells[pl.ds(base + i, 1), :],
        lambda i: values[i : i + 1, :],
        lambda i: tables[base + i],
    )


def post_kernel(n, first, second, own, cells, tables, out, second_out, values):
    lead = leads()
    rows, cols = out.shape[0] - 8, out.shape[1]
    out[0:8, :] = first[0:8, :] + own[...] + jnp.where(lead, 0.0, second[0:8, :])
    second_out[...] = second[...]

    @pl.when(lead)
    def _():
        out[8 : rows + 8, :] = partner_part(n, 1, second, cells, tables, values, (rows, cols))

    @pl.when(jnp.logical_not(lead))
    def _():
        out[8 : rows + 8, :] = jnp.zeros((rows, cols), F32)


def gradient_kernel(n, second, slots, cells, tables, gradient, values):
    gradient[...] = slots[...]

    @pl.when(leads())
    def _():
        gradient[...] += partner_part(n, 0, second, cells, tables, values, gradient.shape)


def merge_kernel(values, kept_first, kept_second, theirs, first, second):
    first[...] = jnp.zeros_like(first)
    first[0:8, :] = kept_first[...] + theirs[0:8, :]
    write_halves(second, 0, values[...])
    second[0:8, :] = jnp.where(leads(), second[0:8, :], kept_second[...] + theirs[8:16, :])
    second[16:32, :] = theirs[8:24, :]


def final_kernel(merged, slots, adjoint, share_rows, sums, other, *refs):
    state_out, air_out, wind_out, state, air, wind, sems = refs
    sub = lax.axis_index("sub")
    gradient = slots[...]
    if merged:
        gradient += jnp.where(leads(), 0.0, other[8 : slots.shape[0] + 8, :])
    for z in range(adjoint.shape[0]):
        state[z] = adjoint[z] + share_rows[z : z + 1, :] * gradient
    copies = [pltpu.make_async_copy(state, state_out, sems.at[0])]
    copies[0].start()
    both = sums[0:8, :] + other[0:8, :]
    own = [jnp.where(sub == 0, both[i : i + 2], both[i + 2 : i + 4]) for i in (0, 4)]
    own = jnp.concatenate(own, axis=1)
    air[...] = -own[0:1]
    wind[...] = own[1:2]
    for i, (a, b) in enumerate(((air, air_out), (wind, wind_out))):
        copies.append(pltpu.make_async_copy(a, b, sems.at[1 + i]))
        copies[-1].start()
    for copy in copies:
        copy.wait()


def traded(x, step, swap=0):
    n, bands = lax.axis_size("tile"), lax.axis_size("sub")
    pairs = [
        (t * bands + s, (t ^ step) * bands + (s ^ swap)) for t in range(n) for s in range(bands)
    ]
    return lax.ppermute(x, ("tile", "sub"), pairs)


def beyond(x):
    n, bands = lax.axis_size("tile"), lax.axis_size("sub")
    pairs = []
    for t in range(n):
        to = t if t in (0, n - 1) else ((t + 1) ^ 1) - 1
        pairs += [(t * bands + s, to * bands + (s ^ 1)) for s in range(bands)]
    return lax.ppermute(x, ("tile", "sub"), pairs)


def by_role(x, lead, rest):
    n, levs, bands = (lax.axis_size(axis) for axis in ("tile", "lev", "sub"))

    def place(t, l, is_lead):
        return (t * levs + l) * bands + (is_lead if t in (0, n - 1) else 1 - is_lead)

    pairs = []
    for t in range(n):
        for l in range(levs):
            for is_lead, (tx, lx) in enumerate((rest, lead)):
                pairs.append((place(t, l, is_lead), place(t ^ tx, l ^ lx, is_lead)))
    return lax.ppermute(x, ("tile", "lev", "sub"), pairs)


def lev_parts(x):
    if lax.axis_size("lev") == 2:
        return [x, lax.ppermute(x, "lev", [(0, 1), (1, 0)])]
    return [lax.psum(x, "lev")]


def per_device(
    marine_layered_warmth,
    bottom_sky_warmth,
    bottom_breeze_magnitude,
    depth_shares,
    piece_sky_box,
    sky_share_fraction,
    piece_marine_box,
    marine_share_fraction,
    marine_indicator,
    marine_result_adjoint,
    energy_transport_adjoint,
):
    n, levs = lax.axis_size("tile"), lax.axis_size("lev")
    levels, rows, cols = marine_layered_warmth.shape
    cells = bottom_sky_warmth.shape[0]
    high = rows + 8
    def pinned(*arrays):
        return [pltpu.with_memory_space_constraint(x, pltpu.HBM) for x in arrays]

    def like(x):
        return jax.ShapeDtypeStruct(x.shape, x.dtype)

    def buffers(arrays):
        return [pltpu.VMEM(x.shape, x.dtype) for x in arrays]

    air = [
        x.reshape(1, cells)
        for x in (bottom_sky_warmth, bottom_breeze_magnitude, energy_transport_adjoint)
    ]
    raw = pinned(
        marine_result_adjoint, marine_indicator, *air, piece_sky_box[0], sky_share_fraction[0]
    )
    msg, ext = call(
        functools.partial(pack_kernel, n),
        [(4 * n + 24, cells), ((levels + 1) * high, cols)],
        raw,
        [HBM] * len(raw),
        scratch=buffers(raw[1:]) + [pltpu.SemaphoreType.DMA((len(raw) - 1 + levels,))],
    )
    other = traded(msg, 0, 1)
    fold = 8 * fold_slots(high, cols, levels + 1)[1]
    ext, edge_out, near_out = call(
        functools.partial(send_kernel, n, levels + 1),
        [ext.shape, (fold, cols), ((fold + 20 + 4 * (n - 2) + 7) // 8 * 8, cols)],
        [msg, other, ext],
    )
    edge_in = beyond(edge_out)
    near_in = traded(near_out, 1, 1)
    raw = pinned(marine_layered_warmth, depth_shares, piece_marine_box[0], marine_share_fraction[0])
    block, strips, heat_strips, surface, block_heat, share_rows, marine, marine_weight = call(
        functools.partial(side_kernel, levels),
        [(levels, rows, cols), (2 * high, cols), (2 * high, cols)]
        + [(rows, cols)] * 2
        + [(8, cols), like(raw[2]), like(raw[3])],
        [ext, *raw],
        [VMEM] + [HBM] * 4,
        scratch=buffers(raw[:1])
        + [pltpu.SMEM(depth_shares.shape, F32), pltpu.SemaphoreType.DMA((4,))],
    )
    merged = n == 4 and levs == 2
    folds, lev_msg, *far_out = call(
        functools.partial(diffuse_kernel, n, levels),
        [(fold, cols), (2 * rows + (16 if merged else 0), cols)] + [(40, cols)] * (n // 2 - 1),
        [ext, near_in, edge_in, surface, share_rows, msg, other, marine, block_heat, heat_strips],
    )
    lev_in = lev_parts(lev_msg)
    far_in = [traded(x, 2 * i + 2, 1) for i, x in enumerate(far_out)]
    picks, tables, uppers, adjoint = call(
        functools.partial(near_kernel, n, fold),
        [(3, 4, cells), jax.ShapeDtypeStruct((4, cells, cols), BF16), (8, cells)]
        + [(levels, rows, cols)],
        [msg, other, near_in, ext, block, strips, folds],
    )
    values, winds, uppers, far_tables, chip = call(
        functools.partial(slot_kernel, n, len(lev_in), rows),
        [(2 * n, cells)] * 3
        + [jax.ShapeDtypeStruct((2 * n, cols, cells), BF16), (40, cols)],
        [*lev_in, picks, tables, uppers, marine, marine_weight, *far_in],
        scratch=[pltpu.VMEM((3, 2 * n, cells), F32)] * 2,
    )
    returns = call(
        functools.partial(kept_kernel, n),
        [(8, cols)] * (3 if merged else n),
        [values, winds, uppers, tables, far_tables],
    )
    if merged:
        theirs = traded(chip, 0, 1)
        slots, partner_cells, partner_tables = call(
            functools.partial(own_kernel, n),
            [(rows, cols), jax.ShapeDtypeStruct((4 * n, cells), jnp.int32)]
            + [jax.ShapeDtypeStruct((4 * n, cells, cols), BF16)],
            [marine, values, lev_in[1], theirs],
        )
        first, second = call(
            merge_kernel, [(32, cols), (32, cols)], [values, *returns[1:], theirs]
        )
        first = by_role(first, (3, 0), (2, 0))
        second = by_role(second, (0, 1), (1, 0))
        scratch = [pltpu.VMEM((2 * n, cells), F32)]
        sums, second = call(
            functools.partial(post_kernel, n),
            [(rows + 8, cols), (32, cols)],
            [first, second, returns[0], partner_cells, partner_tables],
            scratch=scratch,
        )
        (gradient,) = call(
            functools.partial(gradient_kernel, n),
            [(rows, cols)],
            [second, slots, partner_cells, partner_tables],
            scratch=scratch,
        )
    else:
        (slots,) = call(functools.partial(own_kernel, n), [(rows, cols)], [marine, values])
        gradient = sum(lev_parts(slots))
        sums = returns[0]
        for step in range(1, n):
            sums = sums + traded(returns[step], step, 1)
    results = [(levels, rows, cols), (1, cells), (1, cells)]
    state, air_gradient, wind_gradient = call(
        functools.partial(final_kernel, merged),
        results,
        [gradient, adjoint, share_rows, sums, traded(sums, 0, 1)],
        out_specs=[HBM] * 3,
        scratch=[pltpu.VMEM(x, F32) for x in results] + [pltpu.SemaphoreType.DMA((3,))],
    )
    return (state, air_gradient.reshape(cells), wind_gradient.reshape(cells))


def solution(mesh):
    return jax.shard_map(
        per_device,
        mesh=mesh,
        in_specs=(
            P(("ens", "lev"), "sub", "tile"),
            P(("ens", "tile", "lev", "sub")),
            P(("ens", "tile", "lev", "sub")),
            P("lev"),
            P(("tile", "lev", "sub"), None, None),
            P(("tile", "lev", "sub"), None, None),
            P(("tile", "lev", "sub"), None, None),
            P(("tile", "lev", "sub"), None, None),
            P("sub", "tile"),
            P(("ens", "lev"), "sub", "tile"),
            P(("ens", "tile", "lev", "sub")),
        ),
        out_specs=(
            P(("ens", "lev"), "sub", "tile"),
            P(("ens", "tile", "lev", "sub")),
            P(("ens", "tile", "lev", "sub")),
        ),
        check_vma=False,
    )
```

```python
import functools

import jax
import jax.numpy as jnp
from jax import lax
from jax.experimental import pallas as pl
from jax.experimental.pallas import tpu as pltpu
from jax.sharding import PartitionSpec as P

BULK_ITERS = 3
STEPS = 3
HALO = STEPS
MIXING = 0.2
TRANSFER = 1.0
STABILITY = 0.5
F32 = jnp.float32
BF16 = jnp.bfloat16
VMEM = pl.BlockSpec(memory_space=pltpu.VMEM)
HBM = pl.BlockSpec(memory_space=pltpu.HBM)


def call(kernel, outs, operands, specs=None, out_specs=None, scratch=(), aliases=None):
    outs = [jax.ShapeDtypeStruct(x, F32) if isinstance(x, tuple) else x for x in outs]
    return pl.pallas_call(
        kernel,
        out_shape=outs,
        in_specs=specs or [VMEM] * len(operands),
        out_specs=out_specs or [VMEM] * len(outs),
        scratch_shapes=list(scratch),
        input_output_aliases=aliases or {},
        compiler_params=pltpu.CompilerParams(vmem_limit_bytes=24 * 1024 * 1024),
    )(*operands)


def halves(x):
    high = x.astype(BF16)
    low = (x - high.astype(F32)).astype(BF16)
    return high, low


def fold_place(cols):
    lane = lax.broadcasted_iota(jnp.int32, (8, cols), 1)
    return lax.rem(lane + HALO, cols)


def fold_slots(high, cols, fields):
    each = cols // (2 * HALO * fields)
    groups = high // 8
    return [(g // each, g % each) for g in range(groups)], -(-groups // each)


def folded(ext, high, fields):
    cols = ext.shape[1]
    place = fold_place(cols) // (2 * HALO)
    slots, tiles = fold_slots(high, cols, fields)
    out = [jnp.zeros((8, cols), F32)] * tiles
    for g, (k, at) in enumerate(slots[:-1]):
        for i in range(fields):
            slot = at * fields + i
            rows = ext[high * i + 8 * g : high * i + 8 * g + 8, :]
            moved = pltpu.roll(rows, 2 * HALO * slot, 1) if slot else rows
            out[k] = jnp.where(place == slot, moved, out[k])
    return jnp.concatenate(out, axis=0)


def strip_base(z):
    return 6 * HALO * z - 4 * HALO


def lanes_from(shape, first, count):
    lane = lax.broadcasted_iota(jnp.int32, shape, 1)
    return lax.rem(lane + (-first) % shape[1], shape[1]) < count


def turn_lanes(x, by):
    by = by % x.shape[1]
    return pltpu.roll(x, by, 1) if by else x


def own_strips(fields):
    width = 2 * HALO
    cols = fields[0].shape[1]
    out = jnp.zeros_like(fields[0])
    for z, x in enumerate(fields):
        base = strip_base(z)
        out = jnp.where(lanes_from(x.shape, base, width), turn_lanes(x, base + width), out)
        out = jnp.where(lanes_from(x.shape, base + 2 * width, width), turn_lanes(x, base + 2 * width), out)
    return out


def strips_beyond(tiles, own, fields, count):
    width = 2 * HALO
    high, cols = own.shape
    out = []
    for g, (k, at) in enumerate(fold_slots(high, cols, count)[0]):
        x = own[8 * g : 8 * g + 8]
        for z, i in enumerate(fields):
            base = strip_base(z if len(fields) > 1 else 0) + width
            moved = turn_lanes(tiles[k], base - width * (at * count + i))
            x = jnp.where(lanes_from(x.shape, base, width), moved, x)
        out.append(x)
    return jnp.concatenate(out, axis=0)


def from_strips(strip, z, block):
    shape = block.shape
    first, last = lanes_from(shape, 0, HALO), lanes_from(shape, -HALO, HALO)
    block = jnp.where(first, turn_lanes(strip, -strip_base(z) - 4 * HALO), block)
    return jnp.where(last, turn_lanes(strip, -strip_base(z) - 2 * HALO), block)


def around(x):
    high, cols = x.shape
    return pltpu.roll(x, 1, 0) + pltpu.roll(x, high - 1, 0) + pltpu.roll(x, 1, 1) + pltpu.roll(x, cols - 1, 1)


def diffused(wet, fields):
    keep = wet * (1.0 - MIXING * around(wet))
    mix = MIXING * wet
    out = []
    for v in fields:
        v = wet * v
        for sweep_index in range(STEPS):
            v = keep * v + mix * around(v)
        out.append(v)
    return out


def pack_kernel(n, *refs):
    cot, sea, sky, breeze, energy, sky_index, sky_weight, msg, ext = refs[:9]
    sea_in, sky_in, breeze_in, energy_in, index_in, weight_in, sems = refs[9:]
    rows, cols = sea.shape
    levels = cot.shape[0]
    high = rows + 8
    pairs = [(cot.at[z], ext.at[pl.ds(high * z, rows)]) for z in range(levels)]
    pairs += [(sea, sea_in), (sky_index, index_in), (sky_weight, weight_in)]
    pairs += [(sky, sky_in), (breeze, breeze_in), (energy, energy_in)]
    copies = [pltpu.make_async_copy(a, b, sems.at[i]) for i, (a, b) in enumerate(pairs)]
    for copy in copies:
        copy.start()
    sub = lax.axis_index("sub")
    msg[4 * n : 4 * n + 16, :] = jnp.zeros((16, msg.shape[1]), F32)
    for z in range(levels + 1):
        ext[high * z + rows : high * (z + 1), :] = jnp.zeros((8, cols), F32)
    for copy in copies:
        copy.wait()
    ext[high * levels : high * levels + rows, :] = sea_in[...].astype(F32)
    msg[0 : 2 * n, :] = index_in[...].astype(F32)
    msg[2 * n : 4 * n, :] = weight_in[...]
    for i, ref in enumerate((sky_in, breeze_in, energy_in)):
        msg[4 * n + i : 4 * n + i + 1, :] = ref[...]
    base = 4 * n + 8
    for i in range(levels + 1):
        at, top, left = high * i, base + HALO * (i // 2), cols * (i % 2)
        outer = jnp.where(sub == 0, ext[at + rows - HALO : at + rows], ext[at : at + HALO])
        msg[top : top + HALO, left : left + cols] = outer
    edges = folded(ext, high, levels + 1)
    for k in range(2):
        msg[4 * n + 16 : 4 * n + 24, cols * k : cols * (k + 1)] = edges[8 * k : 8 * k + 8]


def halo_rows(n, msg, i, cols):
    top, left = 4 * n + 8 + HALO * (i // 2), cols * (i % 2)
    return msg[top : top + HALO, left : left + cols]


def both_bands(msg, other, index, sub):
    own, far = msg[pl.ds(index, 1), :], other[pl.ds(index, 1), :]
    return [jnp.where(sub == 0, own, far), jnp.where(sub == 0, far, own)]


def table_rows(n, msg, other, target, band, sub):
    row = 2 * target + band
    return both_bands(msg, other, row, sub) + both_bands(msg, other, 2 * n + row, sub)


def value_rows(n, msg, other, sub):
    return [x for i in range(3) for x in both_bands(msg, other, 4 * n + i, sub)]


def write_pairs(out, at, rows):
    cols = out.shape[1]
    for i, row in enumerate(rows):
        out[at + i : at + i + 1, :] = row[:, :cols]
        out[at + len(rows) + i : at + len(rows) + i + 1, :] = row[:, cols:]


def write_halves(out, at, x):
    count, cols = x.shape[0], out.shape[1]
    out[at : at + count, :] = x[:, :cols]
    out[at + count : at + 2 * count, :] = x[:, cols:]


def read_halves(ref, at, count):
    return jnp.concatenate([ref[at : at + count, :], ref[at + count : at + 2 * count, :]], axis=1)


def read_pairs(ref, at, count):
    return [
        jnp.concatenate([ref[at + i : at + i + 1, :], ref[at + count + i : at + count + i + 1, :]], axis=1)
        for i in range(count)
    ]


def send_kernel(n, fields, msg, other, ext_in, ext, edge_out, near_out):
    sub, tile = lax.axis_index("sub"), lax.axis_index("tile")
    cols = ext.shape[1]
    high = ext.shape[0] // fields
    rows = high - 8
    for i in range(fields):
        base = high * i
        strip = halo_rows(n, other, i, cols)
        ext[base : base + rows, :] = ext_in[base : base + rows, :]
        ext[base + rows : base + high, :] = jnp.zeros((8, cols), F32)
        ext[base + rows : base + rows + HALO, :] = jnp.where(sub == 0, strip, 0.0)
        ext[base + high - HALO : base + high, :] = jnp.where(sub == 0, 0.0, strip)
    slots, count = fold_slots(high, cols, fields)
    tile_at, at = slots[-1]
    place = fold_place(cols) // (2 * HALO)
    tiles = [other[4 * n + 16 : 4 * n + 24, cols * k : cols * (k + 1)] for k in range(count)]
    for i in range(fields):
        strip = halo_rows(n, msg, i, cols)
        blank = jnp.zeros((8 - 2 * HALO, cols), F32)
        rows_beyond = [jnp.where(sub == 1, strip, 0.0), blank, jnp.where(sub == 1, 0.0, strip)]
        slot = at * fields + i
        moved = pltpu.roll(jnp.concatenate(rows_beyond, axis=0), 2 * HALO * slot, 1)
        tiles[tile_at] = jnp.where(place == slot, moved, tiles[tile_at])
    edges = jnp.concatenate(tiles, axis=0)
    fold = edges.shape[0]
    edge_out[...] = edges
    near_out[0:fold, :] = edges
    near = tile ^ 1
    air = table_rows(n, msg, other, near, 1 - sub, sub) + value_rows(n, msg, other, sub)
    write_pairs(near_out, fold, air)
    at = fold + 20
    for step in range(2, n, 2):
        write_pairs(near_out, at, table_rows(n, msg, other, near ^ step, sub, sub))
        at += 8
    near_out[at : near_out.shape[0], :] = jnp.zeros((near_out.shape[0] - at, cols), F32)


def side_kernel(levels, ext, *refs):
    warm, shares, marine, marine_weight = refs[:4]
    block, strips, heat_strips, surface, block_heat, share_rows, marine_out, marine_weight_out = refs[4:12]
    warm_in, shares_in, sems = refs[12:]
    pairs = [(warm, warm_in), (shares, shares_in), (marine, marine_out), (marine_weight, marine_weight_out)]
    copies = [pltpu.make_async_copy(a, b, sems.at[i]) for i, (a, b) in enumerate(pairs)]
    for copy in copies:
        copy.start()
    rows, cols = surface.shape
    high = rows + 8
    fields = [ext[high * i : high * (i + 1), :] for i in range(levels + 1)]
    for z, x in enumerate(diffused(fields[levels], fields[:levels])):
        block[z] = x[:rows]
    strips[0:high, :] = own_strips(fields[:levels])
    strips[high : 2 * high, :] = own_strips([fields[levels]] * levels)
    for copy in copies:
        copy.wait()
    surface[...] = sum(shares_in[z] * warm_in[z] for z in range(levels))
    block_heat[...] = sum(shares_in[z] * block[z] for z in range(levels))
    mixed = sum(shares_in[z] * fields[z] for z in range(levels))
    heat_strips[0:high, :] = own_strips([mixed])
    heat_strips[high : 2 * high, :] = own_strips(fields[levels:])
    for z in range(levels):
        share_rows[z : z + 1, :] = jnp.full((1, cols), shares_in[z], F32)


def diffuse_kernel(n, levels, *refs):
    ext, near_in, edge_in, surface, share_rows, msg, other, marine, block_heat, strips = refs[:10]
    fold_out, lev_out = refs[10:12]
    sub, tile = lax.axis_index("sub"), lax.axis_index("tile")
    rows, cols = surface.shape
    high = rows + 8
    fold = edge_in.shape[0]
    own_values = value_rows(n, msg, other, sub)
    near_values = read_pairs(near_in, fold, 10)[4:]
    for i, out in enumerate(refs[12:]):
        air = table_rows(n, msg, other, tile ^ (2 * i + 2), 1 - sub, sub) + own_values
        air += read_pairs(near_in, fold + 20 + 8 * i, 4) + near_values
        write_pairs(out, 0, air)
    even = tile % 2 == 0
    lane = lax.broadcasted_iota(jnp.int32, (8, cols), 1)
    tiles = []
    for k in range(0, fold, 8):
        near, far = near_in[k : k + 8, :], edge_in[k : k + 8, :]
        right = jnp.where(tile < n - 1, jnp.where(even, near, far), 0.0)
        left = jnp.where(tile > 0, jnp.where(even, far, near), 0.0)
        tiles.append(jnp.where(lax.rem(lane, 2 * HALO) < HALO, right, turn_lanes(left, 2 * HALO)))
    fold_out[...] = jnp.concatenate(tiles, axis=0)
    wet = strips_beyond(tiles, strips[high : 2 * high, :], [levels], levels + 1)
    heat = strips[0:high, :]
    for z in range(levels):
        scaled = [share_rows[z : z + 1, :] * x for x in tiles]
        beyond_z = strips_beyond(scaled, jnp.zeros_like(heat), [z], levels + 1)
        heat += beyond_z
    heat = diffused(wet, [heat])[0]
    heat = from_strips(heat[:rows], 0, block_heat[...])
    own_wet = ext[high * levels : high * levels + rows, :]
    lev_out[0:rows, :] = surface[...]
    lev_out[rows : 2 * rows, :] = own_wet * heat
    if lev_out.shape[0] > 2 * rows:
        write_halves(lev_out, 2 * rows, marine[...].astype(F32))


def bulk_adjoint(warmth_gap, flux_sens):
    transfer_rate = jnp.full_like(warmth_gap, TRANSFER)
    rates = [transfer_rate]
    slopes = []
    for sweep_index in range(BULK_ITERS):
        bent = jnp.tanh(transfer_rate * warmth_gap)
        slopes.append(TRANSFER * STABILITY * (1.0 - bent * bent))
        transfer_rate = TRANSFER * (1.0 + STABILITY * bent)
        rates.append(transfer_rate)
    contrast_sens = transfer_rate * flux_sens
    rate_sens = warmth_gap * flux_sens
    for sweep_index in reversed(range(BULK_ITERS)):
        inner_sens = rate_sens * slopes[sweep_index]
        contrast_sens = contrast_sens + inner_sens * rates[sweep_index]
        rate_sens = inner_sens * warmth_gap
    return contrast_sens


def onehot(index, count):
    cells = lax.broadcasted_iota(jnp.int32, (count, index.shape[1]), 0).astype(BF16)
    return jnp.where(cells == index.astype(BF16), jnp.ones((), BF16), jnp.zeros((), BF16))


def dot(a, b, ca, cb):
    return lax.dot_general(a, b, (((ca,), (cb,)), ((), ())), preferred_element_type=F32)


def turned(x):
    return x.astype(F32).T.astype(BF16)


def look_up(air, at, picks, tables, uppers, turn=False):
    cols = tables.shape[2] if turn else tables.shape[1]
    for band in range(2):
        cell = air[band].astype(jnp.int32)
        hot = onehot(lax.rem(cell, cols), cols)
        tables[at + band] = turned(hot) if turn else hot
        values = [air[4 + band], air[6 + band], air[8 + band]]
        values = jnp.concatenate([x[:, :cols] for x in values] + [x[:, cols:] for x in values], axis=0)
        found = dot(jnp.concatenate(halves(values), axis=0), hot, 1, 0)
        found = found[0:6] + found[6:12]
        upper = cell >= cols
        found = jnp.where(upper, found[3:6], found[0:3])
        place = slice(at + band, at + band + 1)
        picks[0, place, :] = found[0:1]
        picks[1, place, :] = found[1:2]
        picks[2, place, :] = air[2 + band] * found[2:3]
        uppers[place, :] = upper.astype(F32)


def near_kernel(n, fold, msg, other, near_in, ext, block, strips, folds, picks, tables, uppers, adjoint):
    sub, tile = lax.axis_index("sub"), lax.axis_index("tile")
    own = table_rows(n, msg, other, tile, sub, sub) + value_rows(n, msg, other, sub)
    look_up(own, 0, picks, tables, uppers, True)
    look_up(read_pairs(near_in, fold, 10), 2, picks, tables, uppers, True)
    levels, rows, cols = adjoint.shape
    high = rows + 8
    tiles = [folds[k : k + 8, :] for k in range(0, fold, 8)]
    wet = strips_beyond(tiles, strips[high : 2 * high, :], [levels] * levels, levels + 1)
    strip = strips_beyond(tiles, strips[0:high, :], list(range(levels)), levels + 1)
    strip = diffused(wet, [strip])[0][:rows]
    own_wet = ext[high * levels : high * levels + rows, :]
    for z in range(levels):
        adjoint[z] = own_wet * from_strips(strip, z, block[z])


def slot_kernel(n, count, rows, *refs):
    lev_parts, refs = refs[:count], refs[count:]
    near_picks, near_tables, near_uppers, marine, weight = refs[:5]
    far_in, refs = refs[5 : 4 + n // 2], refs[4 + n // 2 :]
    values_out, wind_out, uppers, tables, chip_out, held, picks = refs
    sub, tile = lax.axis_index("sub"), lax.axis_index("tile")
    cols = chip_out.shape[1]
    picks[:, 0:4, :] = near_picks[...]
    uppers[0:4, :] = near_uppers[0:4, :]
    for i, ref in enumerate(far_in):
        air = read_pairs(ref, 0, 20)
        for j in range(2):
            look_up(air[10 * j : 10 * j + 10], 4 * i + 4 + 2 * j, picks, tables, uppers)
    table = sum(ref[0 : 2 * rows, :] for ref in lev_parts)
    table = jnp.concatenate(halves(table), axis=1)
    for step in range(n):
        for band in range(2):
            at, place = 2 * step + band, 2 * (tile ^ step) + band
            cell = marine[pl.ds(place, 1), :]
            row, col = cell // cols, lax.rem(cell, cols)
            col_hot = onehot(col, cols)
            spread = dot(table, jnp.concatenate([col_hot, col_hot], axis=0), 1, 0)
            row_mask = lax.broadcasted_iota(jnp.int32, (rows, cell.shape[1]), 0) == row
            for i in range(2):
                piece = jnp.where(row_mask, spread[rows * i : rows * (i + 1)], 0.0)
                held[i, at : at + 1, :] = jnp.sum(piece, axis=0, keepdims=True)
            held[2, at : at + 1, :] = weight[pl.ds(place, 1), :]

    difference = held[0] - picks[0]
    wind = picks[1]
    flux_sens = held[2] * held[1] + picks[2]
    contrast_sens = bulk_adjoint(wind * difference, flux_sens)
    surface_sens = contrast_sens * wind
    wind_sens = contrast_sens * difference
    values_out[...] = surface_sens
    wind_out[...] = wind_sens
    if n == 4:
        sums = functools.partial(air_sums, values_out, wind_out, uppers, near_tables, tables)
        write_halves(chip_out, 8, surface_sens)
        chip_out[24:40, :] = lev_parts[-1][2 * rows : 2 * rows + 16, :]

        lead = leads()

        @pl.when(lead)
        def _():
            chip_out[0:8, :] = sums(1)
            chip_out[8:16, :] = sums(2)

        @pl.when(jnp.logical_not(lead))
        def _():
            chip_out[0:8, :] = sums(3)


def leads():
    tile = lax.axis_index("tile")
    return (lax.axis_index("sub") == 1) != ((tile == 1) | (tile == 2))


def air_sums(values, winds, uppers, near_tables, tables, step):
    rows = [None] * 4
    for band in range(2):
        at = 2 * step + band
        near = at < 4
        hot = near_tables[at] if near else tables[at]
        place = slice(at, at + 1)
        upper = uppers[place, :]
        both = jnp.concatenate([values[place, :], winds[place, :]], axis=0)
        both = jnp.concatenate([both * (1.0 - upper), both * upper], axis=0)
        sums = dot(jnp.concatenate(halves(both), axis=0), hot, 1, 0 if near else 1)
        sums = sums[0:4] + sums[4:8]
        rows[band], rows[2 + band] = sums[0:2], sums[2:4]
    return jnp.concatenate(rows, axis=0)


def kept_kernel(n, values, winds, uppers, near_tables, tables, *returns):
    sums = functools.partial(air_sums, values, winds, uppers, near_tables, tables)
    if n != 4:
        for step in range(n):
            returns[step][...] = sums(step)
        return
    lead = leads()
    own, first, second = returns
    own[...] = sums(0)

    @pl.when(lead)
    def _():
        first[...] = sums(3)
        second[...] = jnp.zeros_like(second)

    @pl.when(jnp.logical_not(lead))
    def _():
        first[...] = sums(1)
        second[...] = sums(2)


def scatter(n, rows, cols, tile, cell_of, value_of, col_hot_of=None):
    total = jnp.zeros((2 * rows, cols), F32)
    for step in range(n):
        for band in range(2):
            at = 2 * step + band
            cell = cell_of(2 * (tile ^ step) + band)
            row, col = cell // cols, lax.rem(cell, cols)
            row_hot = onehot(row, rows)
            high, low = halves(value_of(at))
            spread = jnp.concatenate([row_hot * high, row_hot * low], axis=0)
            if col_hot_of:
                total += dot(spread, col_hot_of(at), 1, 0)
            else:
                total += dot(spread, onehot(col, cols), 1, 1)
    return total[:rows] + total[rows:]


def own_kernel(n, marine, values, *refs):
    tile = lax.axis_index("tile")
    if len(refs) > 1:
        lev_in, theirs, out, cells, tables = refs
        rows, cols = out.shape

        @pl.when(leads())
        def _():
            for band, (ref, at) in enumerate(((lev_in, 2 * rows), (theirs, 24))):
                cells[2 * n * band : 2 * n * (band + 1), :] = read_halves(ref, at, 2 * n).astype(jnp.int32)
                for i in range(2 * n):
                    place = 2 * n * band + 2 * (tile ^ (i // 2)) + i % 2
                    col = lax.rem(cells[pl.ds(place, 1), :], cols)
                    tables[2 * n * band + i] = turned(onehot(col, cols))

    out = refs[2] if len(refs) > 1 else refs[0]
    rows, cols = out.shape
    out[...] = scatter(
        n, rows, cols, tile, lambda i: marine[pl.ds(i, 1), :], lambda i: values[i : i + 1, :]
    )


def partner_part(n, band, second, cells, tables, values, shape):
    rows, cols = shape
    base = 2 * n * band
    values[...] = read_halves(second, 4 * n * band, 2 * n)
    return scatter(
        n,
        rows,
        cols,
        lax.axis_index("tile"),
        lambda i: cells[pl.ds(base + i, 1), :],
        lambda i: values[i : i + 1, :],
        lambda i: tables[base + i],
    )


def post_kernel(n, first, second, own, cells, tables, out, second_out, values):
    lead = leads()
    rows, cols = out.shape[0] - 8, out.shape[1]
    out[0:8, :] = first[0:8, :] + own[...] + jnp.where(lead, 0.0, second[0:8, :])
    second_out[...] = second[...]

    @pl.when(lead)
    def _():
        out[8 : rows + 8, :] = partner_part(n, 1, second, cells, tables, values, (rows, cols))

    @pl.when(jnp.logical_not(lead))
    def _():
        out[8 : rows + 8, :] = jnp.zeros((rows, cols), F32)


def gradient_kernel(n, second, slots, cells, tables, gradient, values):
    gradient[...] = slots[...]

    @pl.when(leads())
    def _():
        gradient[...] += partner_part(n, 0, second, cells, tables, values, gradient.shape)


def merge_kernel(values, kept_first, kept_second, theirs, first, second):
    first[...] = jnp.zeros_like(first)
    first[0:8, :] = kept_first[...] + theirs[0:8, :]
    write_halves(second, 0, values[...])
    second[0:8, :] = jnp.where(leads(), second[0:8, :], kept_second[...] + theirs[8:16, :])
    second[16:32, :] = theirs[8:24, :]


def final_kernel(merged, slots, adjoint, share_rows, sums, other, *refs):
    state_out, air_out, wind_out, state, air, wind, sems = refs
    sub = lax.axis_index("sub")
    gradient = slots[...]
    if merged:
        gradient += jnp.where(leads(), 0.0, other[8 : slots.shape[0] + 8, :])
    for z in range(adjoint.shape[0]):
        state[z] = adjoint[z] + share_rows[z : z + 1, :] * gradient
    copies = [pltpu.make_async_copy(state, state_out, sems.at[0])]
    copies[0].start()
    both = sums[0:8, :] + other[0:8, :]
    own = [jnp.where(sub == 0, both[i : i + 2], both[i + 2 : i + 4]) for i in (0, 4)]
    own = jnp.concatenate(own, axis=1)
    air[...] = -own[0:1]
    wind[...] = own[1:2]
    for i, (a, b) in enumerate(((air, air_out), (wind, wind_out))):
        copies.append(pltpu.make_async_copy(a, b, sems.at[1 + i]))
        copies[-1].start()
    for copy in copies:
        copy.wait()


def traded(x, step, swap=0):
    n, bands = lax.axis_size("tile"), lax.axis_size("sub")
    pairs = [
        (t * bands + s, (t ^ step) * bands + (s ^ swap)) for t in range(n) for s in range(bands)
    ]
    return lax.ppermute(x, ("tile", "sub"), pairs)


def beyond(x):
    n, bands = lax.axis_size("tile"), lax.axis_size("sub")
    pairs = []
    for t in range(n):
        to = t if t in (0, n - 1) else ((t + 1) ^ 1) - 1
        pairs += [(t * bands + s, to * bands + (s ^ 1)) for s in range(bands)]
    return lax.ppermute(x, ("tile", "sub"), pairs)


def by_role(x, lead, rest):
    n, levs, bands = (lax.axis_size(axis) for axis in ("tile", "lev", "sub"))

    def place(t, l, is_lead):
        return (t * levs + l) * bands + (is_lead if t in (0, n - 1) else 1 - is_lead)

    pairs = []
    for t in range(n):
        for l in range(levs):
            for is_lead, (tx, lx) in enumerate((rest, lead)):
                pairs.append((place(t, l, is_lead), place(t ^ tx, l ^ lx, is_lead)))
    return lax.ppermute(x, ("tile", "lev", "sub"), pairs)


def lev_parts(x):
    if lax.axis_size("lev") == 2:
        return [x, lax.ppermute(x, "lev", [(0, 1), (1, 0)])]
    return [lax.psum(x, "lev")]


def per_device(
    marine_layered_warmth,
    bottom_sky_warmth,
    bottom_breeze_magnitude,
    depth_shares,
    piece_sky_box,
    sky_share_fraction,
    piece_marine_box,
    marine_share_fraction,
    marine_indicator,
    marine_result_adjoint,
    energy_transport_adjoint,
):
    n, levs = lax.axis_size("tile"), lax.axis_size("lev")
    levels, rows, cols = marine_layered_warmth.shape
    cells = bottom_sky_warmth.shape[0]
    high = rows + 8
    def pinned(*arrays):
        return [pltpu.with_memory_space_constraint(x, pltpu.HBM) for x in arrays]

    def like(x):
        return jax.ShapeDtypeStruct(x.shape, x.dtype)

    def buffers(arrays):
        return [pltpu.VMEM(x.shape, x.dtype) for x in arrays]

    air = [
        x.reshape(1, cells)
        for x in (bottom_sky_warmth, bottom_breeze_magnitude, energy_transport_adjoint)
    ]
    raw = pinned(
        marine_result_adjoint, marine_indicator, *air, piece_sky_box[0], sky_share_fraction[0]
    )
    msg, ext = call(
        functools.partial(pack_kernel, n),
        [(4 * n + 24, cells), ((levels + 1) * high, cols)],
        raw,
        [HBM] * len(raw),
        scratch=buffers(raw[1:]) + [pltpu.SemaphoreType.DMA((len(raw) - 1 + levels,))],
    )
    other = traded(msg, 0, 1)
    fold = 8 * fold_slots(high, cols, levels + 1)[1]
    ext, edge_out, near_out = call(
        functools.partial(send_kernel, n, levels + 1),
        [ext.shape, (fold, cols), ((fold + 20 + 4 * (n - 2) + 7) // 8 * 8, cols)],
        [msg, other, ext],
    )
    edge_in = beyond(edge_out)
    near_in = traded(near_out, 1, 1)
    raw = pinned(marine_layered_warmth, depth_shares, piece_marine_box[0], marine_share_fraction[0])
    block, strips, heat_strips, surface, block_heat, share_rows, marine, marine_weight = call(
        functools.partial(side_kernel, levels),
        [(levels, rows, cols), (2 * high, cols), (2 * high, cols)]
        + [(rows, cols)] * 2
        + [(8, cols), like(raw[2]), like(raw[3])],
        [ext, *raw],
        [VMEM] + [HBM] * 4,
        scratch=buffers(raw[:1])
        + [pltpu.SMEM(depth_shares.shape, F32), pltpu.SemaphoreType.DMA((4,))],
    )
    merged = n == 4 and levs == 2
    folds, lev_msg, *far_out = call(
        functools.partial(diffuse_kernel, n, levels),
        [(fold, cols), (2 * rows + (16 if merged else 0), cols)] + [(40, cols)] * (n // 2 - 1),
        [ext, near_in, edge_in, surface, share_rows, msg, other, marine, block_heat, heat_strips],
    )
    lev_in = lev_parts(lev_msg)
    far_in = [traded(x, 2 * i + 2, 1) for i, x in enumerate(far_out)]
    picks, tables, uppers, adjoint = call(
        functools.partial(near_kernel, n, fold),
        [(3, 4, cells), jax.ShapeDtypeStruct((4, cells, cols), BF16), (8, cells)]
        + [(levels, rows, cols)],
        [msg, other, near_in, ext, block, strips, folds],
    )
    values, winds, uppers, far_tables, chip = call(
        functools.partial(slot_kernel, n, len(lev_in), rows),
        [(2 * n, cells)] * 3
        + [jax.ShapeDtypeStruct((2 * n, cols, cells), BF16), (40, cols)],
        [*lev_in, picks, tables, uppers, marine, marine_weight, *far_in],
        scratch=[pltpu.VMEM((3, 2 * n, cells), F32)] * 2,
    )
    returns = call(
        functools.partial(kept_kernel, n),
        [(8, cols)] * (3 if merged else n),
        [values, winds, uppers, tables, far_tables],
    )
    if merged:
        theirs = traded(chip, 0, 1)
        slots, partner_cells, partner_tables = call(
            functools.partial(own_kernel, n),
            [(rows, cols), jax.ShapeDtypeStruct((4 * n, cells), jnp.int32)]
            + [jax.ShapeDtypeStruct((4 * n, cells, cols), BF16)],
            [marine, values, lev_in[1], theirs],
        )
        first, second = call(
            merge_kernel, [(32, cols), (32, cols)], [values, *returns[1:], theirs]
        )
        first = by_role(first, (3, 0), (1, 0))
        second = by_role(second, (0, 1), (2, 0))
        scratch = [pltpu.VMEM((2 * n, cells), F32)]
        sums, second = call(
            functools.partial(post_kernel, n),
            [(rows + 8, cols), (32, cols)],
            [first, second, returns[0], partner_cells, partner_tables],
            scratch=scratch,
        )
        (gradient,) = call(
            functools.partial(gradient_kernel, n),
            [(rows, cols)],
            [second, slots, partner_cells, partner_tables],
            scratch=scratch,
        )
    else:
        (slots,) = call(functools.partial(own_kernel, n), [(rows, cols)], [marine, values])
        gradient = sum(lev_parts(slots))
        sums = returns[0]
        for step in range(1, n):
            sums = sums + traded(returns[step], step, 1)
    results = [(levels, rows, cols), (1, cells), (1, cells)]
    state, air_gradient, wind_gradient = call(
        functools.partial(final_kernel, merged),
        results,
        [gradient, adjoint, share_rows, sums, traded(sums, 0, 1)],
        out_specs=[HBM] * 3,
        scratch=[pltpu.VMEM(x, F32) for x in results] + [pltpu.SemaphoreType.DMA((3,))],
    )
    return (state, air_gradient.reshape(cells), wind_gradient.reshape(cells))


def solution(mesh):
    return jax.shard_map(
        per_device,
        mesh=mesh,
        in_specs=(
            P(("ens", "lev"), "sub", "tile"),
            P(("ens", "tile", "lev", "sub")),
            P(("ens", "tile", "lev", "sub")),
            P("lev"),
            P(("tile", "lev", "sub"), None, None),
            P(("tile", "lev", "sub"), None, None),
            P(("tile", "lev", "sub"), None, None),
            P(("tile", "lev", "sub"), None, None),
            P("sub", "tile"),
            P(("ens", "lev"), "sub", "tile"),
            P(("ens", "tile", "lev", "sub")),
        ),
        out_specs=(
            P(("ens", "lev"), "sub", "tile"),
            P(("ens", "tile", "lev", "sub")),
            P(("ens", "tile", "lev", "sub")),
        ),
        check_vma=False,
    )
```

```python
import functools

import jax
import jax.numpy as jnp
from jax import lax
from jax.experimental import pallas as pl
from jax.experimental.pallas import tpu as pltpu
from jax.sharding import PartitionSpec as P

BULK_ITERS = 3
STEPS = 3
HALO = STEPS
MIXING = 0.2
TRANSFER = 1.0
STABILITY = 0.5
F32 = jnp.float32
BF16 = jnp.bfloat16
VMEM = pl.BlockSpec(memory_space=pltpu.VMEM)
HBM = pl.BlockSpec(memory_space=pltpu.HBM)


def call(kernel, outs, operands, specs=None, out_specs=None, scratch=(), aliases=None):
    outs = [jax.ShapeDtypeStruct(x, F32) if isinstance(x, tuple) else x for x in outs]
    return pl.pallas_call(
        kernel,
        out_shape=outs,
        in_specs=specs or [VMEM] * len(operands),
        out_specs=out_specs or [VMEM] * len(outs),
        scratch_shapes=list(scratch),
        input_output_aliases=aliases or {},
        compiler_params=pltpu.CompilerParams(vmem_limit_bytes=24 * 1024 * 1024),
    )(*operands)


def halves(x):
    high = x.astype(BF16)
    low = (x - high.astype(F32)).astype(BF16)
    return high, low


def fold_place(cols):
    lane = lax.broadcasted_iota(jnp.int32, (8, cols), 1)
    return lax.rem(lane + HALO, cols)


def fold_slots(high, cols, fields):
    each = cols // (2 * HALO * fields)
    groups = high // 8
    return [(g // each, g % each) for g in range(groups)], -(-groups // each)


def folded(ext, high, fields):
    cols = ext.shape[1]
    place = fold_place(cols) // (2 * HALO)
    slots, tiles = fold_slots(high, cols, fields)
    out = [jnp.zeros((8, cols), F32)] * tiles
    for g, (k, at) in enumerate(slots[:-1]):
        for i in range(fields):
            slot = at * fields + i
            rows = ext[high * i + 8 * g : high * i + 8 * g + 8, :]
            moved = pltpu.roll(rows, 2 * HALO * slot, 1) if slot else rows
            out[k] = jnp.where(place == slot, moved, out[k])
    return jnp.concatenate(out, axis=0)


def strip_base(z):
    return 6 * HALO * z - 4 * HALO


def lanes_from(shape, first, count):
    lane = lax.broadcasted_iota(jnp.int32, shape, 1)
    return lax.rem(lane + (-first) % shape[1], shape[1]) < count


def turn_lanes(x, by):
    by = by % x.shape[1]
    return pltpu.roll(x, by, 1) if by else x


def own_strips(fields):
    width = 2 * HALO
    cols = fields[0].shape[1]
    out = jnp.zeros_like(fields[0])
    for z, x in enumerate(fields):
        base = strip_base(z)
        out = jnp.where(lanes_from(x.shape, base, width), turn_lanes(x, base + width), out)
        out = jnp.where(lanes_from(x.shape, base + 2 * width, width), turn_lanes(x, base + 2 * width), out)
    return out


def strips_beyond(tiles, own, fields, count):
    width = 2 * HALO
    high, cols = own.shape
    out = []
    for g, (k, at) in enumerate(fold_slots(high, cols, count)[0]):
        x = own[8 * g : 8 * g + 8]
        for z, i in enumerate(fields):
            base = strip_base(z if len(fields) > 1 else 0) + width
            moved = turn_lanes(tiles[k], base - width * (at * count + i))
            x = jnp.where(lanes_from(x.shape, base, width), moved, x)
        out.append(x)
    return jnp.concatenate(out, axis=0)


def strips_apart(right, left, own, i, count):
    width = 2 * HALO
    base = strip_base(0) + width
    high, cols = own.shape
    out = []
    for g, (k, at) in enumerate(fold_slots(high, cols, count)[0]):
        x = own[8 * g : 8 * g + 8]
        by = base - width * (at * count + i)
        x = jnp.where(lanes_from(x.shape, base, HALO), turn_lanes(right[k], by), x)
        out.append(jnp.where(lanes_from(x.shape, base + HALO, HALO), turn_lanes(left[k], by + width), x))
    return jnp.concatenate(out, axis=0)


def from_strips(strip, z, block):
    shape = block.shape
    first, last = lanes_from(shape, 0, HALO), lanes_from(shape, -HALO, HALO)
    block = jnp.where(first, turn_lanes(strip, -strip_base(z) - 4 * HALO), block)
    return jnp.where(last, turn_lanes(strip, -strip_base(z) - 2 * HALO), block)


def around(x):
    high, cols = x.shape
    return pltpu.roll(x, 1, 0) + pltpu.roll(x, high - 1, 0) + pltpu.roll(x, 1, 1) + pltpu.roll(x, cols - 1, 1)


def diffused(wet, fields):
    keep = wet * (1.0 - MIXING * around(wet))
    mix = MIXING * wet
    out = []
    for v in fields:
        v = wet * v
        for sweep_index in range(STEPS):
            v = keep * v + mix * around(v)
        out.append(v)
    return out


def pack_kernel(n, *refs):
    cot, sea, sky, breeze, energy, sky_index, sky_weight, msg, ext = refs[:9]
    sea_in, sky_in, breeze_in, energy_in, index_in, weight_in, sems = refs[9:]
    rows, cols = sea.shape
    levels = cot.shape[0]
    high = rows + 8
    pairs = [(cot.at[z], ext.at[pl.ds(high * z, rows)]) for z in range(levels)]
    pairs += [(sea, sea_in), (sky_index, index_in), (sky_weight, weight_in)]
    pairs += [(sky, sky_in), (breeze, breeze_in), (energy, energy_in)]
    copies = [pltpu.make_async_copy(a, b, sems.at[i]) for i, (a, b) in enumerate(pairs)]
    for copy in copies:
        copy.start()
    sub = lax.axis_index("sub")
    msg[4 * n : 4 * n + 16, :] = jnp.zeros((16, msg.shape[1]), F32)
    for z in range(levels + 1):
        ext[high * z + rows : high * (z + 1), :] = jnp.zeros((8, cols), F32)
    for copy in copies:
        copy.wait()
    ext[high * levels : high * levels + rows, :] = sea_in[...].astype(F32)
    msg[0 : 2 * n, :] = index_in[...].astype(F32)
    msg[2 * n : 4 * n, :] = weight_in[...]
    for i, ref in enumerate((sky_in, breeze_in, energy_in)):
        msg[4 * n + i : 4 * n + i + 1, :] = ref[...]
    base = 4 * n + 8
    for i in range(levels + 1):
        at, top, left = high * i, base + HALO * (i // 2), cols * (i % 2)
        outer = jnp.where(sub == 0, ext[at + rows - HALO : at + rows], ext[at : at + HALO])
        msg[top : top + HALO, left : left + cols] = outer
    edges = folded(ext, high, levels + 1)
    for k in range(2):
        msg[4 * n + 16 : 4 * n + 24, cols * k : cols * (k + 1)] = edges[8 * k : 8 * k + 8]


def halo_rows(n, msg, i, cols):
    top, left = 4 * n + 8 + HALO * (i // 2), cols * (i % 2)
    return msg[top : top + HALO, left : left + cols]


def both_bands(msg, other, index, sub):
    own, far = msg[pl.ds(index, 1), :], other[pl.ds(index, 1), :]
    return [jnp.where(sub == 0, own, far), jnp.where(sub == 0, far, own)]


def table_rows(n, msg, other, target, band, sub):
    row = 2 * target + band
    return both_bands(msg, other, row, sub) + both_bands(msg, other, 2 * n + row, sub)


def value_rows(n, msg, other, sub):
    return [x for i in range(3) for x in both_bands(msg, other, 4 * n + i, sub)]


def write_pairs(out, at, rows):
    cols = out.shape[1]
    for i, row in enumerate(rows):
        out[at + i : at + i + 1, :] = row[:, :cols]
        out[at + len(rows) + i : at + len(rows) + i + 1, :] = row[:, cols:]


def write_halves(out, at, x):
    count, cols = x.shape[0], out.shape[1]
    out[at : at + count, :] = x[:, :cols]
    out[at + count : at + 2 * count, :] = x[:, cols:]


def read_halves(ref, at, count):
    return jnp.concatenate([ref[at : at + count, :], ref[at + count : at + 2 * count, :]], axis=1)


def read_pairs(ref, at, count):
    return [
        jnp.concatenate([ref[at + i : at + i + 1, :], ref[at + count + i : at + count + i + 1, :]], axis=1)
        for i in range(count)
    ]


def send_kernel(n, fields, msg, other, ext_in, ext, edge_out, near_out):
    sub, tile = lax.axis_index("sub"), lax.axis_index("tile")
    cols = ext.shape[1]
    high = ext.shape[0] // fields
    rows = high - 8
    for i in range(fields):
        base = high * i
        strip = halo_rows(n, other, i, cols)
        ext[base : base + rows, :] = ext_in[base : base + rows, :]
        ext[base + rows : base + high, :] = jnp.zeros((8, cols), F32)
        ext[base + rows : base + rows + HALO, :] = jnp.where(sub == 0, strip, 0.0)
        ext[base + high - HALO : base + high, :] = jnp.where(sub == 0, 0.0, strip)
    slots, count = fold_slots(high, cols, fields)
    tile_at, at = slots[-1]
    place = fold_place(cols) // (2 * HALO)
    tiles = [other[4 * n + 16 : 4 * n + 24, cols * k : cols * (k + 1)] for k in range(count)]
    for i in range(fields):
        strip = halo_rows(n, msg, i, cols)
        blank = jnp.zeros((8 - 2 * HALO, cols), F32)
        rows_beyond = [jnp.where(sub == 1, strip, 0.0), blank, jnp.where(sub == 1, 0.0, strip)]
        slot = at * fields + i
        moved = pltpu.roll(jnp.concatenate(rows_beyond, axis=0), 2 * HALO * slot, 1)
        tiles[tile_at] = jnp.where(place == slot, moved, tiles[tile_at])
    edges = jnp.concatenate(tiles, axis=0)
    fold = edges.shape[0]
    edge_out[...] = edges
    near_out[0:fold, :] = edges
    near = tile ^ 1
    air = table_rows(n, msg, other, near, 1 - sub, sub) + value_rows(n, msg, other, sub)
    write_pairs(near_out, fold, air)
    at = fold + 20
    for step in range(2, n, 2):
        write_pairs(near_out, at, table_rows(n, msg, other, near ^ step, sub, sub))
        at += 8
    near_out[at : near_out.shape[0], :] = jnp.zeros((near_out.shape[0] - at, cols), F32)


def side_kernel(levels, ext, *refs):
    warm, shares, marine, marine_weight = refs[:4]
    block, strips, heat_strips, surface, block_heat, share_rows, marine_out, marine_weight_out = refs[4:12]
    warm_in, shares_in, sems = refs[12:]
    pairs = [(warm, warm_in), (shares, shares_in), (marine, marine_out), (marine_weight, marine_weight_out)]
    copies = [pltpu.make_async_copy(a, b, sems.at[i]) for i, (a, b) in enumerate(pairs)]
    for copy in copies:
        copy.start()
    rows, cols = surface.shape
    high = rows + 8
    fields = [ext[high * i : high * (i + 1), :] for i in range(levels + 1)]
    for z, x in enumerate(diffused(fields[levels], fields[:levels])):
        block[z] = x[:rows]
    strips[0:high, :] = own_strips(fields[:levels])
    strips[high : 2 * high, :] = own_strips([fields[levels]] * levels)
    for copy in copies:
        copy.wait()
    surface[...] = sum(shares_in[z] * warm_in[z] for z in range(levels))
    block_heat[...] = sum(shares_in[z] * block[z] for z in range(levels))
    mixed = sum(shares_in[z] * fields[z] for z in range(levels))
    heat_strips[0:high, :] = own_strips([mixed])
    heat_strips[high : 2 * high, :] = own_strips(fields[levels:])
    for z in range(levels):
        share_rows[z : z + 1, :] = jnp.full((1, cols), shares_in[z], F32)


def diffuse_kernel(n, levels, *refs):
    ext, near_in, edge_in, surface, share_rows, msg, other, marine, block_heat, strips = refs[:10]
    fold_out, lev_out = refs[10:12]
    sub, tile = lax.axis_index("sub"), lax.axis_index("tile")
    rows, cols = surface.shape
    high = rows + 8
    fold = edge_in.shape[0]
    own_values = value_rows(n, msg, other, sub)
    near_values = read_pairs(near_in, fold, 10)[4:]
    for i, out in enumerate(refs[12:]):
        air = table_rows(n, msg, other, tile ^ (2 * i + 2), 1 - sub, sub) + own_values
        air += read_pairs(near_in, fold + 20 + 8 * i, 4) + near_values
        write_pairs(out, 0, air)
    even = tile % 2 == 0
    lane = lax.broadcasted_iota(jnp.int32, (8, cols), 1)
    tiles, rights, lefts = [], [], []
    for k in range(0, fold, 8):
        near, far = near_in[k : k + 8, :], edge_in[k : k + 8, :]
        right = jnp.where(tile < n - 1, jnp.where(even, near, far), 0.0)
        left = jnp.where(tile > 0, jnp.where(even, far, near), 0.0)
        tiles.append(jnp.where(lax.rem(lane, 2 * HALO) < HALO, right, turn_lanes(left, 2 * HALO)))
        rights.append(right)
        lefts.append(left)
    fold_out[...] = jnp.concatenate(tiles, axis=0)
    wet = strips_apart(rights, lefts, strips[high : 2 * high, :], levels, levels + 1)
    heat = strips[0:high, :]
    for z in range(levels):
        scaled = [[share_rows[z : z + 1, :] * x for x in side] for side in (rights, lefts)]
        heat += strips_apart(*scaled, jnp.zeros_like(heat), z, levels + 1)
    heat = diffused(wet, [heat])[0]
    heat = from_strips(heat[:rows], 0, block_heat[...])
    own_wet = ext[high * levels : high * levels + rows, :]
    lev_out[0:rows, :] = surface[...]
    lev_out[rows : 2 * rows, :] = own_wet * heat
    if lev_out.shape[0] > 2 * rows:
        write_halves(lev_out, 2 * rows, marine[...].astype(F32))


def bulk_adjoint(warmth_gap, flux_sens):
    transfer_rate = jnp.full_like(warmth_gap, TRANSFER)
    rates = [transfer_rate]
    slopes = []
    for sweep_index in range(BULK_ITERS):
        bent = jnp.tanh(transfer_rate * warmth_gap)
        slopes.append(TRANSFER * STABILITY * (1.0 - bent * bent))
        transfer_rate = TRANSFER * (1.0 + STABILITY * bent)
        rates.append(transfer_rate)
    contrast_sens = transfer_rate * flux_sens
    rate_sens = warmth_gap * flux_sens
    for sweep_index in reversed(range(BULK_ITERS)):
        inner_sens = rate_sens * slopes[sweep_index]
        contrast_sens = contrast_sens + inner_sens * rates[sweep_index]
        rate_sens = inner_sens * warmth_gap
    return contrast_sens


def onehot(index, count):
    cells = lax.broadcasted_iota(jnp.int32, (count, index.shape[1]), 0).astype(BF16)
    return jnp.where(cells == index.astype(BF16), jnp.ones((), BF16), jnp.zeros((), BF16))


def dot(a, b, ca, cb):
    return lax.dot_general(a, b, (((ca,), (cb,)), ((), ())), preferred_element_type=F32)


def turned(x):
    return x.astype(F32).T.astype(BF16)


def look_up(air, at, picks, tables, uppers, turn=False):
    cols = tables.shape[2] if turn else tables.shape[1]
    for band in range(2):
        cell = air[band].astype(jnp.int32)
        hot = onehot(lax.rem(cell, cols), cols)
        tables[at + band] = turned(hot) if turn else hot
        values = [air[4 + band], air[6 + band], air[8 + band]]
        values = jnp.concatenate([x[:, :cols] for x in values] + [x[:, cols:] for x in values], axis=0)
        found = dot(jnp.concatenate(halves(values), axis=0), hot, 1, 0)
        found = found[0:6] + found[6:12]
        upper = cell >= cols
        found = jnp.where(upper, found[3:6], found[0:3])
        place = slice(at + band, at + band + 1)
        picks[0, place, :] = found[0:1]
        picks[1, place, :] = found[1:2]
        picks[2, place, :] = air[2 + band] * found[2:3]
        uppers[place, :] = upper.astype(F32)


def near_kernel(n, fold, msg, other, near_in, ext, block, strips, folds, picks, tables, uppers, adjoint):
    sub, tile = lax.axis_index("sub"), lax.axis_index("tile")
    own = table_rows(n, msg, other, tile, sub, sub) + value_rows(n, msg, other, sub)
    look_up(own, 0, picks, tables, uppers, True)
    look_up(read_pairs(near_in, fold, 10), 2, picks, tables, uppers, True)
    levels, rows, cols = adjoint.shape
    high = rows + 8
    tiles = [folds[k : k + 8, :] for k in range(0, fold, 8)]
    wet = strips_beyond(tiles, strips[high : 2 * high, :], [levels] * levels, levels + 1)
    strip = strips_beyond(tiles, strips[0:high, :], list(range(levels)), levels + 1)
    strip = diffused(wet, [strip])[0][:rows]
    own_wet = ext[high * levels : high * levels + rows, :]
    for z in range(levels):
        adjoint[z] = own_wet * from_strips(strip, z, block[z])


def slot_kernel(n, count, rows, *refs):
    lev_parts, refs = refs[:count], refs[count:]
    near_picks, near_tables, near_uppers, marine, weight = refs[:5]
    far_in, refs = refs[5 : 4 + n // 2], refs[4 + n // 2 :]
    values_out, wind_out, uppers, tables, chip_out, held, picks = refs
    sub, tile = lax.axis_index("sub"), lax.axis_index("tile")
    cols = chip_out.shape[1]
    picks[:, 0:4, :] = near_picks[...]
    uppers[0:4, :] = near_uppers[0:4, :]
    for i, ref in enumerate(far_in):
        air = read_pairs(ref, 0, 20)
        for j in range(2):
            look_up(air[10 * j : 10 * j + 10], 4 * i + 4 + 2 * j, picks, tables, uppers)
    table = sum(ref[0 : 2 * rows, :] for ref in lev_parts)
    table = jnp.concatenate(halves(table), axis=1)
    for step in range(n):
        for band in range(2):
            at, place = 2 * step + band, 2 * (tile ^ step) + band
            cell = marine[pl.ds(place, 1), :]
            row, col = cell // cols, lax.rem(cell, cols)
            col_hot = onehot(col, cols)
            spread = dot(table, jnp.concatenate([col_hot, col_hot], axis=0), 1, 0)
            row_mask = lax.broadcasted_iota(jnp.int32, (rows, cell.shape[1]), 0) == row
            for i in range(2):
                piece = jnp.where(row_mask, spread[rows * i : rows * (i + 1)], 0.0)
                held[i, at : at + 1, :] = jnp.sum(piece, axis=0, keepdims=True)
            held[2, at : at + 1, :] = weight[pl.ds(place, 1), :]

    difference = held[0] - picks[0]
    wind = picks[1]
    flux_sens = held[2] * held[1] + picks[2]
    contrast_sens = bulk_adjoint(wind * difference, flux_sens)
    surface_sens = contrast_sens * wind
    wind_sens = contrast_sens * difference
    values_out[...] = surface_sens
    wind_out[...] = wind_sens
    if n == 4:
        sums = functools.partial(air_sums, values_out, wind_out, uppers, near_tables, tables)
        write_halves(chip_out, 8, surface_sens)
        chip_out[24:40, :] = lev_parts[-1][2 * rows : 2 * rows + 16, :]

        lead = leads()

        @pl.when(lead)
        def _():
            chip_out[0:8, :] = sums(1)
            chip_out[8:16, :] = sums(2)

        @pl.when(jnp.logical_not(lead))
        def _():
            chip_out[0:8, :] = sums(3)


def leads():
    tile = lax.axis_index("tile")
    return (lax.axis_index("sub") == 1) != ((tile == 1) | (tile == 2))


def air_sums(values, winds, uppers, near_tables, tables, step):
    rows = [None] * 4
    for band in range(2):
        at = 2 * step + band
        near = at < 4
        hot = near_tables[at] if near else tables[at]
        place = slice(at, at + 1)
        upper = uppers[place, :]
        both = jnp.concatenate([values[place, :], winds[place, :]], axis=0)
        both = jnp.concatenate([both * (1.0 - upper), both * upper], axis=0)
        sums = dot(jnp.concatenate(halves(both), axis=0), hot, 1, 0 if near else 1)
        sums = sums[0:4] + sums[4:8]
        rows[band], rows[2 + band] = sums[0:2], sums[2:4]
    return jnp.concatenate(rows, axis=0)


def kept_kernel(n, values, winds, uppers, near_tables, tables, *returns):
    sums = functools.partial(air_sums, values, winds, uppers, near_tables, tables)
    if n != 4:
        for step in range(n):
            returns[step][...] = sums(step)
        return
    lead = leads()
    own, first, second = returns
    own[...] = sums(0)

    @pl.when(lead)
    def _():
        first[...] = sums(3)
        second[...] = jnp.zeros_like(second)

    @pl.when(jnp.logical_not(lead))
    def _():
        first[...] = sums(1)
        second[...] = sums(2)


def scatter(n, rows, cols, tile, cell_of, value_of, col_hot_of=None):
    total = jnp.zeros((2 * rows, cols), F32)
    for step in range(n):
        for band in range(2):
            at = 2 * step + band
            cell = cell_of(2 * (tile ^ step) + band)
            row, col = cell // cols, lax.rem(cell, cols)
            row_hot = onehot(row, rows)
            high, low = halves(value_of(at))
            spread = jnp.concatenate([row_hot * high, row_hot * low], axis=0)
            if col_hot_of:
                total += dot(spread, col_hot_of(at), 1, 0)
            else:
                total += dot(spread, onehot(col, cols), 1, 1)
    return total[:rows] + total[rows:]


def own_kernel(n, marine, values, *refs):
    tile = lax.axis_index("tile")
    if len(refs) > 1:
        lev_in, theirs, out, cells, tables = refs
        rows, cols = out.shape

        @pl.when(leads())
        def _():
            for band, (ref, at) in enumerate(((lev_in, 2 * rows), (theirs, 24))):
                cells[2 * n * band : 2 * n * (band + 1), :] = read_halves(ref, at, 2 * n).astype(jnp.int32)
                for i in range(2 * n):
                    place = 2 * n * band + 2 * (tile ^ (i // 2)) + i % 2
                    col = lax.rem(cells[pl.ds(place, 1), :], cols)
                    tables[2 * n * band + i] = turned(onehot(col, cols))

    out = refs[2] if len(refs) > 1 else refs[0]
    rows, cols = out.shape
    out[...] = scatter(
        n, rows, cols, tile, lambda i: marine[pl.ds(i, 1), :], lambda i: values[i : i + 1, :]
    )


def partner_part(n, band, second, cells, tables, values, shape):
    rows, cols = shape
    base = 2 * n * band
    values[...] = read_halves(second, 4 * n * band, 2 * n)
    return scatter(
        n,
        rows,
        cols,
        lax.axis_index("tile"),
        lambda i: cells[pl.ds(base + i, 1), :],
        lambda i: values[i : i + 1, :],
        lambda i: tables[base + i],
    )


def post_kernel(n, first, second, own, cells, tables, out, second_out, values):
    lead = leads()
    rows, cols = out.shape[0] - 8, out.shape[1]
    out[0:8, :] = first[0:8, :] + own[...] + jnp.where(lead, 0.0, second[0:8, :])
    second_out[...] = second[...]

    @pl.when(lead)
    def _():
        out[8 : rows + 8, :] = partner_part(n, 1, second, cells, tables, values, (rows, cols))

    @pl.when(jnp.logical_not(lead))
    def _():
        out[8 : rows + 8, :] = jnp.zeros((rows, cols), F32)


def gradient_kernel(n, second, slots, cells, tables, gradient, values):
    gradient[...] = slots[...]

    @pl.when(leads())
    def _():
        gradient[...] += partner_part(n, 0, second, cells, tables, values, gradient.shape)


def merge_kernel(values, kept_first, kept_second, theirs, first, second):
    first[...] = jnp.zeros_like(first)
    first[0:8, :] = kept_first[...] + theirs[0:8, :]
    write_halves(second, 0, values[...])
    second[0:8, :] = jnp.where(leads(), second[0:8, :], kept_second[...] + theirs[8:16, :])
    second[16:32, :] = theirs[8:24, :]


def final_kernel(merged, slots, adjoint, share_rows, sums, other, *refs):
    state_out, air_out, wind_out, state, air, wind, sems = refs
    sub = lax.axis_index("sub")
    gradient = slots[...]
    if merged:
        gradient += jnp.where(leads(), 0.0, other[8 : slots.shape[0] + 8, :])
    for z in range(adjoint.shape[0]):
        state[z] = adjoint[z] + share_rows[z : z + 1, :] * gradient
    copies = [pltpu.make_async_copy(state, state_out, sems.at[0])]
    copies[0].start()
    both = sums[0:8, :] + other[0:8, :]
    own = [jnp.where(sub == 0, both[i : i + 2], both[i + 2 : i + 4]) for i in (0, 4)]
    own = jnp.concatenate(own, axis=1)
    air[...] = -own[0:1]
    wind[...] = own[1:2]
    for i, (a, b) in enumerate(((air, air_out), (wind, wind_out))):
        copies.append(pltpu.make_async_copy(a, b, sems.at[1 + i]))
        copies[-1].start()
    for copy in copies:
        copy.wait()


def traded(x, step, swap=0):
    n, bands = lax.axis_size("tile"), lax.axis_size("sub")
    pairs = [
        (t * bands + s, (t ^ step) * bands + (s ^ swap)) for t in range(n) for s in range(bands)
    ]
    return lax.ppermute(x, ("tile", "sub"), pairs)


def beyond(x):
    n, bands = lax.axis_size("tile"), lax.axis_size("sub")
    pairs = []
    for t in range(n):
        to = t if t in (0, n - 1) else ((t + 1) ^ 1) - 1
        pairs += [(t * bands + s, to * bands + (s ^ 1)) for s in range(bands)]
    return lax.ppermute(x, ("tile", "sub"), pairs)


def by_role(x, lead, rest):
    n, levs, bands = (lax.axis_size(axis) for axis in ("tile", "lev", "sub"))

    def place(t, l, is_lead):
        return (t * levs + l) * bands + (is_lead if t in (0, n - 1) else 1 - is_lead)

    pairs = []
    for t in range(n):
        for l in range(levs):
            for is_lead, (tx, lx) in enumerate((rest, lead)):
                pairs.append((place(t, l, is_lead), place(t ^ tx, l ^ lx, is_lead)))
    return lax.ppermute(x, ("tile", "lev", "sub"), pairs)


def lev_parts(x):
    if lax.axis_size("lev") == 2:
        return [x, lax.ppermute(x, "lev", [(0, 1), (1, 0)])]
    return [lax.psum(x, "lev")]


def per_device(
    marine_layered_warmth,
    bottom_sky_warmth,
    bottom_breeze_magnitude,
    depth_shares,
    piece_sky_box,
    sky_share_fraction,
    piece_marine_box,
    marine_share_fraction,
    marine_indicator,
    marine_result_adjoint,
    energy_transport_adjoint,
):
    n, levs = lax.axis_size("tile"), lax.axis_size("lev")
    levels, rows, cols = marine_layered_warmth.shape
    cells = bottom_sky_warmth.shape[0]
    high = rows + 8
    def pinned(*arrays):
        return [pltpu.with_memory_space_constraint(x, pltpu.HBM) for x in arrays]

    def like(x):
        return jax.ShapeDtypeStruct(x.shape, x.dtype)

    def buffers(arrays):
        return [pltpu.VMEM(x.shape, x.dtype) for x in arrays]

    air = [
        x.reshape(1, cells)
        for x in (bottom_sky_warmth, bottom_breeze_magnitude, energy_transport_adjoint)
    ]
    raw = pinned(
        marine_result_adjoint, marine_indicator, *air, piece_sky_box[0], sky_share_fraction[0]
    )
    msg, ext = call(
        functools.partial(pack_kernel, n),
        [(4 * n + 24, cells), ((levels + 1) * high, cols)],
        raw,
        [HBM] * len(raw),
        scratch=buffers(raw[1:]) + [pltpu.SemaphoreType.DMA((len(raw) - 1 + levels,))],
    )
    other = traded(msg, 0, 1)
    fold = 8 * fold_slots(high, cols, levels + 1)[1]
    ext, edge_out, near_out = call(
        functools.partial(send_kernel, n, levels + 1),
        [ext.shape, (fold, cols), ((fold + 20 + 4 * (n - 2) + 7) // 8 * 8, cols)],
        [msg, other, ext],
    )
    edge_in = beyond(edge_out)
    near_in = traded(near_out, 1, 1)
    raw = pinned(marine_layered_warmth, depth_shares, piece_marine_box[0], marine_share_fraction[0])
    block, strips, heat_strips, surface, block_heat, share_rows, marine, marine_weight = call(
        functools.partial(side_kernel, levels),
        [(levels, rows, cols), (2 * high, cols), (2 * high, cols)]
        + [(rows, cols)] * 2
        + [(8, cols), like(raw[2]), like(raw[3])],
        [ext, *raw],
        [VMEM] + [HBM] * 4,
        scratch=buffers(raw[:1])
        + [pltpu.SMEM(depth_shares.shape, F32), pltpu.SemaphoreType.DMA((4,))],
    )
    merged = n == 4 and levs == 2
    folds, lev_msg, *far_out = call(
        functools.partial(diffuse_kernel, n, levels),
        [(fold, cols), (2 * rows + (16 if merged else 0), cols)] + [(40, cols)] * (n // 2 - 1),
        [ext, near_in, edge_in, surface, share_rows, msg, other, marine, block_heat, heat_strips],
    )
    lev_in = lev_parts(lev_msg)
    far_in = [traded(x, 2 * i + 2, 1) for i, x in enumerate(far_out)]
    picks, tables, uppers, adjoint = call(
        functools.partial(near_kernel, n, fold),
        [(3, 4, cells), jax.ShapeDtypeStruct((4, cells, cols), BF16), (8, cells)]
        + [(levels, rows, cols)],
        [msg, other, near_in, ext, block, strips, folds],
    )
    values, winds, uppers, far_tables, chip = call(
        functools.partial(slot_kernel, n, len(lev_in), rows),
        [(2 * n, cells)] * 3
        + [jax.ShapeDtypeStruct((2 * n, cols, cells), BF16), (40, cols)],
        [*lev_in, picks, tables, uppers, marine, marine_weight, *far_in],
        scratch=[pltpu.VMEM((3, 2 * n, cells), F32)] * 2,
    )
    returns = call(
        functools.partial(kept_kernel, n),
        [(8, cols)] * (3 if merged else n),
        [values, winds, uppers, tables, far_tables],
    )
    if merged:
        theirs = traded(chip, 0, 1)
        slots, partner_cells, partner_tables = call(
            functools.partial(own_kernel, n),
            [(rows, cols), jax.ShapeDtypeStruct((4 * n, cells), jnp.int32)]
            + [jax.ShapeDtypeStruct((4 * n, cells, cols), BF16)],
            [marine, values, lev_in[1], theirs],
        )
        first, second = call(
            merge_kernel, [(32, cols), (32, cols)], [values, *returns[1:], theirs]
        )
        first = by_role(first, (3, 0), (1, 0))
        second = by_role(second, (0, 1), (2, 0))
        scratch = [pltpu.VMEM((2 * n, cells), F32)]
        sums, second = call(
            functools.partial(post_kernel, n),
            [(rows + 8, cols), (32, cols)],
            [first, second, returns[0], partner_cells, partner_tables],
            scratch=scratch,
        )
        (gradient,) = call(
            functools.partial(gradient_kernel, n),
            [(rows, cols)],
            [second, slots, partner_cells, partner_tables],
            scratch=scratch,
        )
    else:
        (slots,) = call(functools.partial(own_kernel, n), [(rows, cols)], [marine, values])
        gradient = sum(lev_parts(slots))
        sums = returns[0]
        for step in range(1, n):
            sums = sums + traded(returns[step], step, 1)
    results = [(levels, rows, cols), (1, cells), (1, cells)]
    state, air_gradient, wind_gradient = call(
        functools.partial(final_kernel, merged),
        results,
        [gradient, adjoint, share_rows, sums, traded(sums, 0, 1)],
        out_specs=[HBM] * 3,
        scratch=[pltpu.VMEM(x, F32) for x in results] + [pltpu.SemaphoreType.DMA((3,))],
    )
    return (state, air_gradient.reshape(cells), wind_gradient.reshape(cells))


def solution(mesh):
    return jax.shard_map(
        per_device,
        mesh=mesh,
        in_specs=(
            P(("ens", "lev"), "sub", "tile"),
            P(("ens", "tile", "lev", "sub")),
            P(("ens", "tile", "lev", "sub")),
            P("lev"),
            P(("tile", "lev", "sub"), None, None),
            P(("tile", "lev", "sub"), None, None),
            P(("tile", "lev", "sub"), None, None),
            P(("tile", "lev", "sub"), None, None),
            P("sub", "tile"),
            P(("ens", "lev"), "sub", "tile"),
            P(("ens", "tile", "lev", "sub")),
        ),
        out_specs=(
            P(("ens", "lev"), "sub", "tile"),
            P(("ens", "tile", "lev", "sub")),
            P(("ens", "tile", "lev", "sub")),
        ),
        check_vma=False,
    )
```

```python
import functools

import jax
import jax.numpy as jnp
from jax import lax
from jax.experimental import pallas as pl
from jax.experimental.pallas import tpu as pltpu
from jax.sharding import PartitionSpec as P

BULK_ITERS = 3
STEPS = 3
HALO = STEPS
MIXING = 0.2
TRANSFER = 1.0
STABILITY = 0.5
F32 = jnp.float32
BF16 = jnp.bfloat16
VMEM = pl.BlockSpec(memory_space=pltpu.VMEM)
HBM = pl.BlockSpec(memory_space=pltpu.HBM)


def call(kernel, outs, operands, specs=None, out_specs=None, scratch=(), aliases=None):
    outs = [jax.ShapeDtypeStruct(x, F32) if isinstance(x, tuple) else x for x in outs]
    return pl.pallas_call(
        kernel,
        out_shape=outs,
        in_specs=specs or [VMEM] * len(operands),
        out_specs=out_specs or [VMEM] * len(outs),
        scratch_shapes=list(scratch),
        input_output_aliases=aliases or {},
        compiler_params=pltpu.CompilerParams(vmem_limit_bytes=24 * 1024 * 1024),
    )(*operands)


def halves(x):
    high = x.astype(BF16)
    low = (x - high.astype(F32)).astype(BF16)
    return high, low


def fold_place(cols):
    lane = lax.broadcasted_iota(jnp.int32, (8, cols), 1)
    return lax.rem(lane + HALO, cols)


def fold_slots(high, cols, fields):
    each = cols // (2 * HALO * fields)
    groups = high // 8
    return [(g // each, g % each) for g in range(groups)], -(-groups // each)


def folded(ext, high, fields):
    cols = ext.shape[1]
    place = fold_place(cols) // (2 * HALO)
    slots, tiles = fold_slots(high, cols, fields)
    out = [jnp.zeros((8, cols), F32)] * tiles
    for g, (k, at) in enumerate(slots[:-1]):
        for i in range(fields):
            slot = at * fields + i
            rows = ext[high * i + 8 * g : high * i + 8 * g + 8, :]
            moved = pltpu.roll(rows, 2 * HALO * slot, 1) if slot else rows
            out[k] = jnp.where(place == slot, moved, out[k])
    return jnp.concatenate(out, axis=0)


def strip_base(z):
    return 6 * HALO * z - 4 * HALO


def lanes_from(shape, first, count):
    lane = lax.broadcasted_iota(jnp.int32, shape, 1)
    return lax.rem(lane + (-first) % shape[1], shape[1]) < count


def turn_lanes(x, by):
    by = by % x.shape[1]
    return pltpu.roll(x, by, 1) if by else x


def own_strips(fields):
    width = 2 * HALO
    cols = fields[0].shape[1]
    out = jnp.zeros_like(fields[0])
    for z, x in enumerate(fields):
        base = strip_base(z)
        out = jnp.where(lanes_from(x.shape, base, width), turn_lanes(x, base + width), out)
        out = jnp.where(lanes_from(x.shape, base + 2 * width, width), turn_lanes(x, base + 2 * width), out)
    return out


def strips_beyond(tiles, own, fields, count):
    width = 2 * HALO
    high, cols = own.shape
    out = []
    for g, (k, at) in enumerate(fold_slots(high, cols, count)[0]):
        x = own[8 * g : 8 * g + 8]
        for z, i in enumerate(fields):
            base = strip_base(z if len(fields) > 1 else 0) + width
            moved = turn_lanes(tiles[k], base - width * (at * count + i))
            x = jnp.where(lanes_from(x.shape, base, width), moved, x)
        out.append(x)
    return jnp.concatenate(out, axis=0)


def strips_apart(right, left, own, i, count):
    width = 2 * HALO
    base = strip_base(0) + width
    high, cols = own.shape
    out = []
    for g, (k, at) in enumerate(fold_slots(high, cols, count)[0]):
        x = own[8 * g : 8 * g + 8]
        by = base - width * (at * count + i)
        x = jnp.where(lanes_from(x.shape, base, HALO), turn_lanes(right[k], by), x)
        out.append(jnp.where(lanes_from(x.shape, base + HALO, HALO), turn_lanes(left[k], by + width), x))
    return jnp.concatenate(out, axis=0)


def from_strips(strip, z, block):
    shape = block.shape
    first, last = lanes_from(shape, 0, HALO), lanes_from(shape, -HALO, HALO)
    block = jnp.where(first, turn_lanes(strip, -strip_base(z) - 4 * HALO), block)
    return jnp.where(last, turn_lanes(strip, -strip_base(z) - 2 * HALO), block)


def around(x):
    high, cols = x.shape
    return pltpu.roll(x, 1, 0) + pltpu.roll(x, high - 1, 0) + pltpu.roll(x, 1, 1) + pltpu.roll(x, cols - 1, 1)


def diffused(wet, fields):
    keep = wet * (1.0 - MIXING * around(wet))
    mix = MIXING * wet
    out = []
    for v in fields:
        v = wet * v
        for sweep_index in range(STEPS):
            v = keep * v + mix * around(v)
        out.append(v)
    return out


def pack_kernel(n, *refs):
    cot, sea, sky, breeze, energy, sky_index, sky_weight, msg, ext = refs[:9]
    sea_in, sky_in, breeze_in, energy_in, index_in, weight_in, sems = refs[9:]
    rows, cols = sea.shape
    levels = cot.shape[0]
    high = rows + 8
    pairs = [(cot.at[z], ext.at[pl.ds(high * z, rows)]) for z in range(levels)]
    pairs += [(sea, sea_in), (sky_index, index_in), (sky_weight, weight_in)]
    pairs += [(sky, sky_in), (breeze, breeze_in), (energy, energy_in)]
    copies = [pltpu.make_async_copy(a, b, sems.at[i]) for i, (a, b) in enumerate(pairs)]
    for copy in copies:
        copy.start()
    sub = lax.axis_index("sub")
    msg[4 * n : 4 * n + 16, :] = jnp.zeros((16, msg.shape[1]), F32)
    for z in range(levels + 1):
        ext[high * z + rows : high * (z + 1), :] = jnp.zeros((8, cols), F32)
    for copy in copies[: levels + 1]:
        copy.wait()
    ext[high * levels : high * levels + rows, :] = sea_in[...].astype(F32)
    base = 4 * n + 8
    for i in range(levels + 1):
        at, top, left = high * i, base + HALO * (i // 2), cols * (i % 2)
        outer = jnp.where(sub == 0, ext[at + rows - HALO : at + rows], ext[at : at + HALO])
        msg[top : top + HALO, left : left + cols] = outer
    edges = folded(ext, high, levels + 1)
    for k in range(2):
        msg[4 * n + 16 : 4 * n + 24, cols * k : cols * (k + 1)] = edges[8 * k : 8 * k + 8]
    for copy in copies[levels + 1 :]:
        copy.wait()
    msg[0 : 2 * n, :] = index_in[...].astype(F32)
    msg[2 * n : 4 * n, :] = weight_in[...]
    for i, ref in enumerate((sky_in, breeze_in, energy_in)):
        msg[4 * n + i : 4 * n + i + 1, :] = ref[...]


def halo_rows(n, msg, i, cols):
    top, left = 4 * n + 8 + HALO * (i // 2), cols * (i % 2)
    return msg[top : top + HALO, left : left + cols]


def both_bands(msg, other, index, sub):
    own, far = msg[pl.ds(index, 1), :], other[pl.ds(index, 1), :]
    return [jnp.where(sub == 0, own, far), jnp.where(sub == 0, far, own)]


def table_rows(n, msg, other, target, band, sub):
    row = 2 * target + band
    return both_bands(msg, other, row, sub) + both_bands(msg, other, 2 * n + row, sub)


def value_rows(n, msg, other, sub):
    return [x for i in range(3) for x in both_bands(msg, other, 4 * n + i, sub)]


def write_pairs(out, at, rows):
    cols = out.shape[1]
    for i, row in enumerate(rows):
        out[at + i : at + i + 1, :] = row[:, :cols]
        out[at + len(rows) + i : at + len(rows) + i + 1, :] = row[:, cols:]


def write_halves(out, at, x):
    count, cols = x.shape[0], out.shape[1]
    out[at : at + count, :] = x[:, :cols]
    out[at + count : at + 2 * count, :] = x[:, cols:]


def read_halves(ref, at, count):
    return jnp.concatenate([ref[at : at + count, :], ref[at + count : at + 2 * count, :]], axis=1)


def read_pairs(ref, at, count):
    return [
        jnp.concatenate([ref[at + i : at + i + 1, :], ref[at + count + i : at + count + i + 1, :]], axis=1)
        for i in range(count)
    ]


def send_kernel(n, fields, msg, other, ext_in, ext, edge_out, near_out):
    sub, tile = lax.axis_index("sub"), lax.axis_index("tile")
    cols = ext.shape[1]
    high = ext.shape[0] // fields
    rows = high - 8
    for i in range(fields):
        base = high * i
        strip = halo_rows(n, other, i, cols)
        ext[base : base + rows, :] = ext_in[base : base + rows, :]
        ext[base + rows : base + high, :] = jnp.zeros((8, cols), F32)
        ext[base + rows : base + rows + HALO, :] = jnp.where(sub == 0, strip, 0.0)
        ext[base + high - HALO : base + high, :] = jnp.where(sub == 0, 0.0, strip)
    slots, count = fold_slots(high, cols, fields)
    tile_at, at = slots[-1]
    place = fold_place(cols) // (2 * HALO)
    tiles = [other[4 * n + 16 : 4 * n + 24, cols * k : cols * (k + 1)] for k in range(count)]
    for i in range(fields):
        strip = halo_rows(n, msg, i, cols)
        blank = jnp.zeros((8 - 2 * HALO, cols), F32)
        rows_beyond = [jnp.where(sub == 1, strip, 0.0), blank, jnp.where(sub == 1, 0.0, strip)]
        slot = at * fields + i
        moved = pltpu.roll(jnp.concatenate(rows_beyond, axis=0), 2 * HALO * slot, 1)
        tiles[tile_at] = jnp.where(place == slot, moved, tiles[tile_at])
    edges = jnp.concatenate(tiles, axis=0)
    fold = edges.shape[0]
    edge_out[...] = edges
    near_out[0:fold, :] = edges
    near = tile ^ 1
    air = table_rows(n, msg, other, near, 1 - sub, sub) + value_rows(n, msg, other, sub)
    write_pairs(near_out, fold, air)
    at = fold + 20
    for step in range(2, n, 2):
        write_pairs(near_out, at, table_rows(n, msg, other, near ^ step, sub, sub))
        at += 8
    near_out[at : near_out.shape[0], :] = jnp.zeros((near_out.shape[0] - at, cols), F32)


def side_kernel(levels, ext, *refs):
    warm, shares, marine, marine_weight = refs[:4]
    block, strips, heat_strips, surface, block_heat, share_rows, marine_out, marine_weight_out = refs[4:12]
    warm_in, shares_in, sems = refs[12:]
    pairs = [(warm, warm_in), (shares, shares_in), (marine, marine_out), (marine_weight, marine_weight_out)]
    copies = [pltpu.make_async_copy(a, b, sems.at[i]) for i, (a, b) in enumerate(pairs)]
    for copy in copies:
        copy.start()
    rows, cols = surface.shape
    high = rows + 8
    fields = [ext[high * i : high * (i + 1), :] for i in range(levels + 1)]
    for z, x in enumerate(diffused(fields[levels], fields[:levels])):
        block[z] = x[:rows]
    strips[0:high, :] = own_strips(fields[:levels])
    strips[high : 2 * high, :] = own_strips([fields[levels]] * levels)
    for copy in copies:
        copy.wait()
    surface[...] = sum(shares_in[z] * warm_in[z] for z in range(levels))
    block_heat[...] = sum(shares_in[z] * block[z] for z in range(levels))
    mixed = sum(shares_in[z] * fields[z] for z in range(levels))
    heat_strips[0:high, :] = own_strips([mixed])
    heat_strips[high : 2 * high, :] = own_strips(fields[levels:])
    for z in range(levels):
        share_rows[z : z + 1, :] = jnp.full((1, cols), shares_in[z], F32)


def diffuse_kernel(n, levels, *refs):
    ext, near_in, edge_in, surface, share_rows, msg, other, marine, block_heat, strips = refs[:10]
    fold_out, lev_out = refs[10:12]
    sub, tile = lax.axis_index("sub"), lax.axis_index("tile")
    rows, cols = surface.shape
    high = rows + 8
    fold = edge_in.shape[0]
    own_values = value_rows(n, msg, other, sub)
    near_values = read_pairs(near_in, fold, 10)[4:]
    for i, out in enumerate(refs[12:]):
        air = table_rows(n, msg, other, tile ^ (2 * i + 2), 1 - sub, sub) + own_values
        air += read_pairs(near_in, fold + 20 + 8 * i, 4) + near_values
        write_pairs(out, 0, air)
    even = tile % 2 == 0
    lane = lax.broadcasted_iota(jnp.int32, (8, cols), 1)
    tiles, rights, lefts = [], [], []
    for k in range(0, fold, 8):
        near, far = near_in[k : k + 8, :], edge_in[k : k + 8, :]
        right = jnp.where(tile < n - 1, jnp.where(even, near, far), 0.0)
        left = jnp.where(tile > 0, jnp.where(even, far, near), 0.0)
        tiles.append(jnp.where(lax.rem(lane, 2 * HALO) < HALO, right, turn_lanes(left, 2 * HALO)))
        rights.append(right)
        lefts.append(left)
    fold_out[...] = jnp.concatenate(tiles, axis=0)
    wet = strips_apart(rights, lefts, strips[high : 2 * high, :], levels, levels + 1)
    heat = strips[0:high, :]
    for z in range(levels):
        scaled = [[share_rows[z : z + 1, :] * x for x in side] for side in (rights, lefts)]
        heat += strips_apart(*scaled, jnp.zeros_like(heat), z, levels + 1)
    heat = diffused(wet, [heat])[0]
    heat = from_strips(heat[:rows], 0, block_heat[...])
    own_wet = ext[high * levels : high * levels + rows, :]
    lev_out[0:rows, :] = surface[...]
    lev_out[rows : 2 * rows, :] = own_wet * heat
    if lev_out.shape[0] > 2 * rows:
        write_halves(lev_out, 2 * rows, marine[...].astype(F32))


def bulk_adjoint(warmth_gap, flux_sens):
    transfer_rate = jnp.full_like(warmth_gap, TRANSFER)
    rates = [transfer_rate]
    slopes = []
    for sweep_index in range(BULK_ITERS):
        bent = jnp.tanh(transfer_rate * warmth_gap)
        slopes.append(TRANSFER * STABILITY * (1.0 - bent * bent))
        transfer_rate = TRANSFER * (1.0 + STABILITY * bent)
        rates.append(transfer_rate)
    contrast_sens = transfer_rate * flux_sens
    rate_sens = warmth_gap * flux_sens
    for sweep_index in reversed(range(BULK_ITERS)):
        inner_sens = rate_sens * slopes[sweep_index]
        contrast_sens = contrast_sens + inner_sens * rates[sweep_index]
        rate_sens = inner_sens * warmth_gap
    return contrast_sens


def onehot(index, count):
    cells = lax.broadcasted_iota(jnp.int32, (count, index.shape[1]), 0).astype(BF16)
    return jnp.where(cells == index.astype(BF16), jnp.ones((), BF16), jnp.zeros((), BF16))


def dot(a, b, ca, cb):
    return lax.dot_general(a, b, (((ca,), (cb,)), ((), ())), preferred_element_type=F32)


def turned(x):
    return x.astype(F32).T.astype(BF16)


def look_up(air, at, picks, tables, uppers, turn=False):
    cols = tables.shape[2] if turn else tables.shape[1]
    for band in range(2):
        cell = air[band].astype(jnp.int32)
        hot = onehot(lax.rem(cell, cols), cols)
        tables[at + band] = turned(hot) if turn else hot
        values = [air[4 + band], air[6 + band], air[8 + band]]
        values = jnp.concatenate([x[:, :cols] for x in values] + [x[:, cols:] for x in values], axis=0)
        found = dot(jnp.concatenate(halves(values), axis=0), hot, 1, 0)
        found = found[0:6] + found[6:12]
        upper = cell >= cols
        found = jnp.where(upper, found[3:6], found[0:3])
        place = slice(at + band, at + band + 1)
        picks[0, place, :] = found[0:1]
        picks[1, place, :] = found[1:2]
        picks[2, place, :] = air[2 + band] * found[2:3]
        uppers[place, :] = upper.astype(F32)


def near_kernel(n, fold, msg, other, near_in, ext, block, strips, folds, picks, tables, uppers, adjoint):
    sub, tile = lax.axis_index("sub"), lax.axis_index("tile")
    own = table_rows(n, msg, other, tile, sub, sub) + value_rows(n, msg, other, sub)
    look_up(own, 0, picks, tables, uppers, True)
    look_up(read_pairs(near_in, fold, 10), 2, picks, tables, uppers, True)
    levels, rows, cols = adjoint.shape
    high = rows + 8
    tiles = [folds[k : k + 8, :] for k in range(0, fold, 8)]
    wet = strips_beyond(tiles, strips[high : 2 * high, :], [levels] * levels, levels + 1)
    strip = strips_beyond(tiles, strips[0:high, :], list(range(levels)), levels + 1)
    strip = diffused(wet, [strip])[0][:rows]
    own_wet = ext[high * levels : high * levels + rows, :]
    for z in range(levels):
        adjoint[z] = own_wet * from_strips(strip, z, block[z])


def slot_kernel(n, count, rows, *refs):
    lev_parts, refs = refs[:count], refs[count:]
    near_picks, near_tables, near_uppers, marine, weight = refs[:5]
    far_in, refs = refs[5 : 4 + n // 2], refs[4 + n // 2 :]
    values_out, wind_out, uppers, tables, chip_out, held, picks = refs
    sub, tile = lax.axis_index("sub"), lax.axis_index("tile")
    cols = chip_out.shape[1]
    picks[:, 0:4, :] = near_picks[...]
    uppers[0:4, :] = near_uppers[0:4, :]
    for i, ref in enumerate(far_in):
        air = read_pairs(ref, 0, 20)
        for j in range(2):
            look_up(air[10 * j : 10 * j + 10], 4 * i + 4 + 2 * j, picks, tables, uppers)
    table = sum(ref[0 : 2 * rows, :] for ref in lev_parts)
    table = jnp.concatenate(halves(table), axis=1)
    for step in range(n):
        for band in range(2):
            at, place = 2 * step + band, 2 * (tile ^ step) + band
            cell = marine[pl.ds(place, 1), :]
            row, col = cell // cols, lax.rem(cell, cols)
            col_hot = onehot(col, cols)
            spread = dot(table, jnp.concatenate([col_hot, col_hot], axis=0), 1, 0)
            row_mask = lax.broadcasted_iota(jnp.int32, (rows, cell.shape[1]), 0) == row
            for i in range(2):
                piece = jnp.where(row_mask, spread[rows * i : rows * (i + 1)], 0.0)
                held[i, at : at + 1, :] = jnp.sum(piece, axis=0, keepdims=True)
            held[2, at : at + 1, :] = weight[pl.ds(place, 1), :]

    difference = held[0] - picks[0]
    wind = picks[1]
    flux_sens = held[2] * held[1] + picks[2]
    contrast_sens = bulk_adjoint(wind * difference, flux_sens)
    surface_sens = contrast_sens * wind
    wind_sens = contrast_sens * difference
    values_out[...] = surface_sens
    wind_out[...] = wind_sens
    if n == 4:
        sums = functools.partial(air_sums, values_out, wind_out, uppers, near_tables, tables)
        write_halves(chip_out, 8, surface_sens)
        chip_out[24:40, :] = lev_parts[-1][2 * rows : 2 * rows + 16, :]

        lead = leads()

        @pl.when(lead)
        def _():
            chip_out[0:8, :] = sums(1)
            chip_out[8:16, :] = sums(2)

        @pl.when(jnp.logical_not(lead))
        def _():
            chip_out[0:8, :] = sums(3)


def leads():
    tile = lax.axis_index("tile")
    return (lax.axis_index("sub") == 1) != ((tile == 1) | (tile == 2))


def air_sums(values, winds, uppers, near_tables, tables, step):
    rows = [None] * 4
    for band in range(2):
        at = 2 * step + band
        near = at < 4
        hot = near_tables[at] if near else tables[at]
        place = slice(at, at + 1)
        upper = uppers[place, :]
        both = jnp.concatenate([values[place, :], winds[place, :]], axis=0)
        both = jnp.concatenate([both * (1.0 - upper), both * upper], axis=0)
        sums = dot(jnp.concatenate(halves(both), axis=0), hot, 1, 0 if near else 1)
        sums = sums[0:4] + sums[4:8]
        rows[band], rows[2 + band] = sums[0:2], sums[2:4]
    return jnp.concatenate(rows, axis=0)


def kept_kernel(n, values, winds, uppers, near_tables, tables, *returns):
    sums = functools.partial(air_sums, values, winds, uppers, near_tables, tables)
    if n != 4:
        for step in range(n):
            returns[step][...] = sums(step)
        return
    lead = leads()
    own, first, second = returns
    own[...] = sums(0)

    @pl.when(lead)
    def _():
        first[...] = sums(3)
        second[...] = jnp.zeros_like(second)

    @pl.when(jnp.logical_not(lead))
    def _():
        first[...] = sums(1)
        second[...] = sums(2)


def scatter(n, rows, cols, tile, cell_of, value_of, col_hot_of=None):
    total = jnp.zeros((2 * rows, cols), F32)
    for step in range(n):
        for band in range(2):
            at = 2 * step + band
            cell = cell_of(2 * (tile ^ step) + band)
            row, col = cell // cols, lax.rem(cell, cols)
            row_hot = onehot(row, rows)
            high, low = halves(value_of(at))
            spread = jnp.concatenate([row_hot * high, row_hot * low], axis=0)
            if col_hot_of:
                total += dot(spread, col_hot_of(at), 1, 0)
            else:
                total += dot(spread, onehot(col, cols), 1, 1)
    return total[:rows] + total[rows:]


def own_kernel(n, marine, values, *refs):
    tile = lax.axis_index("tile")
    if len(refs) > 1:
        lev_in, theirs, out, cells, tables = refs
        rows, cols = out.shape

        @pl.when(leads())
        def _():
            for band, (ref, at) in enumerate(((lev_in, 2 * rows), (theirs, 24))):
                cells[2 * n * band : 2 * n * (band + 1), :] = read_halves(ref, at, 2 * n).astype(jnp.int32)
                for i in range(2 * n):
                    place = 2 * n * band + 2 * (tile ^ (i // 2)) + i % 2
                    col = lax.rem(cells[pl.ds(place, 1), :], cols)
                    tables[2 * n * band + i] = turned(onehot(col, cols))

    out = refs[2] if len(refs) > 1 else refs[0]
    rows, cols = out.shape
    out[...] = scatter(
        n, rows, cols, tile, lambda i: marine[pl.ds(i, 1), :], lambda i: values[i : i + 1, :]
    )


def partner_part(n, band, second, cells, tables, values, shape):
    rows, cols = shape
    base = 2 * n * band
    values[...] = read_halves(second, 4 * n * band, 2 * n)
    return scatter(
        n,
        rows,
        cols,
        lax.axis_index("tile"),
        lambda i: cells[pl.ds(base + i, 1), :],
        lambda i: values[i : i + 1, :],
        lambda i: tables[base + i],
    )


def post_kernel(n, first, second, own, cells, tables, out, second_out, values):
    lead = leads()
    rows, cols = out.shape[0] - 8, out.shape[1]
    out[0:8, :] = first[0:8, :] + own[...] + jnp.where(lead, 0.0, second[0:8, :])
    second_out[...] = second[...]

    @pl.when(lead)
    def _():
        out[8 : rows + 8, :] = partner_part(n, 1, second, cells, tables, values, (rows, cols))

    @pl.when(jnp.logical_not(lead))
    def _():
        out[8 : rows + 8, :] = jnp.zeros((rows, cols), F32)


def gradient_kernel(n, second, slots, cells, tables, gradient, values):
    gradient[...] = slots[...]

    @pl.when(leads())
    def _():
        gradient[...] += partner_part(n, 0, second, cells, tables, values, gradient.shape)


def merge_kernel(values, kept_first, kept_second, theirs, first, second):
    first[...] = jnp.zeros_like(first)
    first[0:8, :] = kept_first[...] + theirs[0:8, :]
    write_halves(second, 0, values[...])
    second[0:8, :] = jnp.where(leads(), second[0:8, :], kept_second[...] + theirs[8:16, :])
    second[16:32, :] = theirs[8:24, :]


def final_kernel(merged, slots, adjoint, share_rows, sums, other, *refs):
    state_out, air_out, wind_out, state, air, wind, sems = refs
    sub = lax.axis_index("sub")
    gradient = slots[...]
    if merged:
        gradient += jnp.where(leads(), 0.0, other[8 : slots.shape[0] + 8, :])
    for z in range(adjoint.shape[0]):
        state[z] = adjoint[z] + share_rows[z : z + 1, :] * gradient
    copies = [pltpu.make_async_copy(state, state_out, sems.at[0])]
    copies[0].start()
    both = sums[0:8, :] + other[0:8, :]
    own = [jnp.where(sub == 0, both[i : i + 2], both[i + 2 : i + 4]) for i in (0, 4)]
    own = jnp.concatenate(own, axis=1)
    air[...] = -own[0:1]
    wind[...] = own[1:2]
    for i, (a, b) in enumerate(((air, air_out), (wind, wind_out))):
        copies.append(pltpu.make_async_copy(a, b, sems.at[1 + i]))
        copies[-1].start()
    for copy in copies:
        copy.wait()


def traded(x, step, swap=0):
    n, bands = lax.axis_size("tile"), lax.axis_size("sub")
    pairs = [
        (t * bands + s, (t ^ step) * bands + (s ^ swap)) for t in range(n) for s in range(bands)
    ]
    return lax.ppermute(x, ("tile", "sub"), pairs)


def beyond(x):
    n, bands = lax.axis_size("tile"), lax.axis_size("sub")
    pairs = []
    for t in range(n):
        to = t if t in (0, n - 1) else ((t + 1) ^ 1) - 1
        pairs += [(t * bands + s, to * bands + (s ^ 1)) for s in range(bands)]
    return lax.ppermute(x, ("tile", "sub"), pairs)


def by_role(x, lead, rest):
    n, levs, bands = (lax.axis_size(axis) for axis in ("tile", "lev", "sub"))

    def place(t, l, is_lead):
        return (t * levs + l) * bands + (is_lead if t in (0, n - 1) else 1 - is_lead)

    pairs = []
    for t in range(n):
        for l in range(levs):
            for is_lead, (tx, lx) in enumerate((rest, lead)):
                pairs.append((place(t, l, is_lead), place(t ^ tx, l ^ lx, is_lead)))
    return lax.ppermute(x, ("tile", "lev", "sub"), pairs)


def lev_parts(x):
    if lax.axis_size("lev") == 2:
        return [x, lax.ppermute(x, "lev", [(0, 1), (1, 0)])]
    return [lax.psum(x, "lev")]


def per_device(
    marine_layered_warmth,
    bottom_sky_warmth,
    bottom_breeze_magnitude,
    depth_shares,
    piece_sky_box,
    sky_share_fraction,
    piece_marine_box,
    marine_share_fraction,
    marine_indicator,
    marine_result_adjoint,
    energy_transport_adjoint,
):
    n, levs = lax.axis_size("tile"), lax.axis_size("lev")
    levels, rows, cols = marine_layered_warmth.shape
    cells = bottom_sky_warmth.shape[0]
    high = rows + 8
    def pinned(*arrays):
        return [pltpu.with_memory_space_constraint(x, pltpu.HBM) for x in arrays]

    def like(x):
        return jax.ShapeDtypeStruct(x.shape, x.dtype)

    def buffers(arrays):
        return [pltpu.VMEM(x.shape, x.dtype) for x in arrays]

    air = [
        x.reshape(1, cells)
        for x in (bottom_sky_warmth, bottom_breeze_magnitude, energy_transport_adjoint)
    ]
    raw = pinned(
        marine_result_adjoint, marine_indicator, *air, piece_sky_box[0], sky_share_fraction[0]
    )
    msg, ext = call(
        functools.partial(pack_kernel, n),
        [(4 * n + 24, cells), ((levels + 1) * high, cols)],
        raw,
        [HBM] * len(raw),
        scratch=buffers(raw[1:]) + [pltpu.SemaphoreType.DMA((len(raw) - 1 + levels,))],
    )
    other = traded(msg, 0, 1)
    fold = 8 * fold_slots(high, cols, levels + 1)[1]
    ext, edge_out, near_out = call(
        functools.partial(send_kernel, n, levels + 1),
        [ext.shape, (fold, cols), ((fold + 20 + 4 * (n - 2) + 7) // 8 * 8, cols)],
        [msg, other, ext],
    )
    edge_in = beyond(edge_out)
    near_in = traded(near_out, 1, 1)
    raw = pinned(marine_layered_warmth, depth_shares, piece_marine_box[0], marine_share_fraction[0])
    block, strips, heat_strips, surface, block_heat, share_rows, marine, marine_weight = call(
        functools.partial(side_kernel, levels),
        [(levels, rows, cols), (2 * high, cols), (2 * high, cols)]
        + [(rows, cols)] * 2
        + [(8, cols), like(raw[2]), like(raw[3])],
        [ext, *raw],
        [VMEM] + [HBM] * 4,
        scratch=buffers(raw[:1])
        + [pltpu.SMEM(depth_shares.shape, F32), pltpu.SemaphoreType.DMA((4,))],
    )
    merged = n == 4 and levs == 2
    folds, lev_msg, *far_out = call(
        functools.partial(diffuse_kernel, n, levels),
        [(fold, cols), (2 * rows + (16 if merged else 0), cols)] + [(40, cols)] * (n // 2 - 1),
        [ext, near_in, edge_in, surface, share_rows, msg, other, marine, block_heat, heat_strips],
    )
    lev_in = lev_parts(lev_msg)
    far_in = [traded(x, 2 * i + 2, 1) for i, x in enumerate(far_out)]
    picks, tables, uppers, adjoint = call(
        functools.partial(near_kernel, n, fold),
        [(3, 4, cells), jax.ShapeDtypeStruct((4, cells, cols), BF16), (8, cells)]
        + [(levels, rows, cols)],
        [msg, other, near_in, ext, block, strips, folds],
    )
    values, winds, uppers, far_tables, chip = call(
        functools.partial(slot_kernel, n, len(lev_in), rows),
        [(2 * n, cells)] * 3
        + [jax.ShapeDtypeStruct((2 * n, cols, cells), BF16), (40, cols)],
        [*lev_in, picks, tables, uppers, marine, marine_weight, *far_in],
        scratch=[pltpu.VMEM((3, 2 * n, cells), F32)] * 2,
    )
    returns = call(
        functools.partial(kept_kernel, n),
        [(8, cols)] * (3 if merged else n),
        [values, winds, uppers, tables, far_tables],
    )
    if merged:
        theirs = traded(chip, 0, 1)
        slots, partner_cells, partner_tables = call(
            functools.partial(own_kernel, n),
            [(rows, cols), jax.ShapeDtypeStruct((4 * n, cells), jnp.int32)]
            + [jax.ShapeDtypeStruct((4 * n, cells, cols), BF16)],
            [marine, values, lev_in[1], theirs],
        )
        first, second = call(
            merge_kernel, [(32, cols), (32, cols)], [values, *returns[1:], theirs]
        )
        first = by_role(first, (3, 0), (1, 0))
        second = by_role(second, (0, 1), (2, 0))
        scratch = [pltpu.VMEM((2 * n, cells), F32)]
        sums, second = call(
            functools.partial(post_kernel, n),
            [(rows + 8, cols), (32, cols)],
            [first, second, returns[0], partner_cells, partner_tables],
            scratch=scratch,
        )
        (gradient,) = call(
            functools.partial(gradient_kernel, n),
            [(rows, cols)],
            [second, slots, partner_cells, partner_tables],
            scratch=scratch,
        )
    else:
        (slots,) = call(functools.partial(own_kernel, n), [(rows, cols)], [marine, values])
        gradient = sum(lev_parts(slots))
        sums = returns[0]
        for step in range(1, n):
            sums = sums + traded(returns[step], step, 1)
    results = [(levels, rows, cols), (1, cells), (1, cells)]
    state, air_gradient, wind_gradient = call(
        functools.partial(final_kernel, merged),
        results,
        [gradient, adjoint, share_rows, sums, traded(sums, 0, 1)],
        out_specs=[HBM] * 3,
        scratch=[pltpu.VMEM(x, F32) for x in results] + [pltpu.SemaphoreType.DMA((3,))],
    )
    return (state, air_gradient.reshape(cells), wind_gradient.reshape(cells))


def solution(mesh):
    return jax.shard_map(
        per_device,
        mesh=mesh,
        in_specs=(
            P(("ens", "lev"), "sub", "tile"),
            P(("ens", "tile", "lev", "sub")),
            P(("ens", "tile", "lev", "sub")),
            P("lev"),
            P(("tile", "lev", "sub"), None, None),
            P(("tile", "lev", "sub"), None, None),
            P(("tile", "lev", "sub"), None, None),
            P(("tile", "lev", "sub"), None, None),
            P("sub", "tile"),
            P(("ens", "lev"), "sub", "tile"),
            P(("ens", "tile", "lev", "sub")),
        ),
        out_specs=(
            P(("ens", "lev"), "sub", "tile"),
            P(("ens", "tile", "lev", "sub")),
            P(("ens", "tile", "lev", "sub")),
        ),
        check_vma=False,
    )
```
